128 devices in a mesh: row: 8 (over z, core), col: 16 (over y, x).
Axes of the slice: x: 4, y: 4, z: 4, core: 2. Of those that a mesh axis runs over, the one named last changes fastest.
Arguments:
- densities: bfloat16 [128, 3, 256, 128], P(('row', 'col')), may hold values from -6 to 6
- positions: float32 [128, 3, 256], replicated, may hold values from -1 to 1
- areas: float32 [128, 256], replicated, may hold values from 0.15 to 0.6
- bases: bfloat16 [128, 32, 3, 256], P(('row', 'col')), may hold values from -0.21875 to 0.21875
- near_pairs: int32 [1920, 2], replicated, may hold values from 0 to 127, as said below
- far_pairs: int32 [768, 2], replicated, may hold values from 0 to 127
- couplings: bfloat16 [768, 1024], replicated, may hold values from -1 to 1
Outputs:
- potentials: bfloat16 [128, 3, 256, 128], P(('row', 'col'))
The draws below stay inside these ranges and needn't reach their ends.
Inputs may be any that keep to these rules, and one draw needn't show every extreme that they name: `near_pairs`: cluster g is held by the device of mesh row (g) // 16 and mesh column (g) % 16. For each mesh row i and column j, at most 40 rows (t, s) have t held in mesh row i and s held in mesh column j, and some (i, j) has exactly 40.
All inputs are finite; a program needn't handle non-finite values.
Results may differ from the reference program's by a relative error of at most 0.005.
Values may be sent and summed in bfloat16 or wider, within the bound.
No kernel may reach another device: no remote copies, remote signals or barrier semaphores. Data moves between devices by JAX's collectives and lax.ppermute only.
A program may use at most 128 MiB of HBM per device.

```python
import math
import jax
import jax.numpy as jnp
from jax import lax

CS = 256
LOADS = 128
RANK = 32
CPD = 1
NCL = 128
NEAR_MOST = 40
NNEAR = 1920
NFAR = 768
N_ROW = 8
N_COL = 16


def draw_near_pairs(key, part):
    key = jax.random.fold_in(key, 11)
    devices_total = N_ROW * N_COL
    slot_total = NEAR_MOST * devices_total
    kept_count = NNEAR
    subkeys = jax.random.split(key, 6)
    slot_owner = jnp.arange(slot_total, dtype=jnp.int32) // NEAR_MOST
    fullest = jax.random.randint(subkeys[0], (), 0, devices_total)
    shuffled = jax.random.permutation(subkeys[1], slot_total).astype(jnp.int32)
    ranking = jnp.where(slot_owner == fullest, jnp.arange(slot_total, dtype=jnp.int32) - slot_total, shuffled)
    chosen_slots = jnp.argsort(ranking, stable=True)[:kept_count].astype(jnp.int32)
    holder = chosen_slots // NEAR_MOST
    mesh_row = holder // N_COL
    mesh_column = holder % N_COL
    heads = mesh_row * (N_COL * CPD) + jax.random.randint(subkeys[2], (kept_count,), 0, N_COL * CPD)
    tails = (jax.random.randint(subkeys[3], (kept_count,), 0, N_ROW) * N_COL + mesh_column) * CPD + jax.random.randint(subkeys[4], (kept_count,), 0, CPD)
    pair_rows = jnp.stack([heads, tails], axis=1).astype(jnp.int32)
    return pair_rows[jax.random.permutation(subkeys[5], kept_count)]


def with_ends(array, rng, low, largest):
    shape = array.shape
    spot = [jax.random.randint(jax.random.fold_in(rng, axis), (), 0, shape[axis]) for axis in range(len(shape))]
    array = array.at[tuple(spot)].set(low)
    longest = shape.index(max(shape))
    spot[longest] = (spot[longest] + 1) % shape[longest]
    return array.at[tuple(spot)].set(largest)


def block_levels(key, extent, cuts, low, high):
    loudness, own = 1.0, jax.random.fold_in(key, 6)
    for dim, blocks in cuts:
        steps = jnp.exp(jax.random.uniform(jax.random.fold_in(own, dim), (blocks,), jnp.float32, low / len(cuts), high / len(cuts)))
        loudness = loudness * jnp.repeat(steps, extent[dim] // blocks).reshape([-1 if axis == dim else 1 for axis in range(len(extent))])
    return loudness


def centred(rng, dims, scale, limit, cuts=(), held_as=jnp.bfloat16):
    array = jax.random.normal(rng, dims, jnp.float32) * scale
    if len(cuts) > 0:
        array = block_levels(rng, dims, cuts, -0.22, 0.18) * array
    return jnp.clip(array, min=-limit, max=limit).astype(held_as)


def setup_inputs(seed: int = 0) -> dict:
    arg_keys = jax.random.split(jax.random.key(seed), 8)
    return {
        "densities": centred(arg_keys[0], (NCL, 3, CS, LOADS), 1.0, 6.0, ((0, 128),)),
        "positions": jnp.clip(jax.random.uniform(arg_keys[1], (NCL, 3, CS), jnp.float32, -1.0, 1.0), -1.0, 1.0),
        "areas": jnp.clip(jnp.exp(jax.random.uniform(arg_keys[2], (NCL, CS), jnp.float32, math.log(0.15), math.log(0.6))), 0.15, 0.6),
        "bases": centred(arg_keys[3], (NCL, RANK, 3, CS), (3 * CS) ** -0.5, 0.21875, ((0, 128),)),
        "near_pairs": draw_near_pairs(jax.random.fold_in(arg_keys[7], 71), 0),
        "far_pairs": with_ends(jax.random.randint(arg_keys[5], (NFAR, 2), 0, NCL), jax.random.fold_in(arg_keys[5], 1), 0, NCL - 1).astype(jnp.int32),
        "couplings": centred(arg_keys[6], (NFAR, RANK * RANK), RANK ** -0.5, 1.0),
    }


eps_square = 0.0004
lame_ratio = 1.8
kelvin_coef = 1.0 / (16.0 * 3.141592653589793 * 0.7)

def kelvin_tile(pos_target, wt_target, pos_source, wt_source):
    offset = pos_target[:, :, None] - pos_source[:, None, :]
    inverse = lax.rsqrt(lax.optimization_barrier(jnp.sum(offset * offset, axis=0)) + eps_square)
    cubed = inverse * inverse * inverse
    weight = kelvin_coef * wt_target[:, None] * wt_source[None, :]
    identity = jnp.eye(3, dtype=jnp.float32)
    blocks = (offset[:, None] * offset[None, :] * cubed + lame_ratio * identity[:, :, None, None] * inverse) * weight
    panels = pos_target.shape[1]
    return jnp.transpose(blocks, (0, 2, 1, 3)).reshape(3 * panels, 3 * panels).astype(jnp.bfloat16)

def reference(densities, positions, areas, bases, near_pairs, far_pairs, couplings):
    clusters = densities.shape[0]
    width = 3 * CS
    flat = densities.reshape(clusters, width, LOADS)

    def near_step(totals, pair_row):
        first = pair_row[0]
        second = pair_row[1]
        tile = kelvin_tile(positions[first], areas[first], positions[second], areas[second])
        forward = jnp.dot(tile, flat[second], preferred_element_type=jnp.float32)
        backward = lax.dot_general(tile, flat[first], (((0,), (0,)), ((), ())), preferred_element_type=jnp.float32)
        other = jnp.where(first != second, 1.0, 0.0).astype(jnp.float32)
        totals = totals.at[first].add(forward)
        totals = totals.at[second].add(backward * other)
        return (totals, None)
    near_field, _ = lax.scan(near_step, jnp.zeros((clusters, width, LOADS), jnp.float32), near_pairs)
    basis_flat = bases.reshape(clusters, RANK, width).astype(jnp.float32)
    moments = jnp.einsum('crw,cwl->crl', basis_flat, flat.astype(jnp.float32), precision=lax.Precision.HIGHEST).astype(jnp.bfloat16)
    moment_wide = moments.astype(jnp.float32)
    far_heads = far_pairs[:, 0]
    far_tails = far_pairs[:, 1]
    blocks = couplings.reshape(-1, RANK, RANK).astype(jnp.float32)
    forward = jnp.einsum('frq,fql->frl', blocks, moment_wide[far_tails], precision=lax.Precision.HIGHEST)
    other = jnp.where(far_heads != far_tails, 1.0, 0.0).astype(jnp.float32)
    backward = jnp.einsum('fqr,fql->frl', blocks, moment_wide[far_heads], precision=lax.Precision.HIGHEST) * other[:, None, None]
    coefficients = jnp.zeros((clusters, RANK, LOADS), jnp.float32).at[far_heads].add(forward).at[far_tails].add(backward)
    expanded = jnp.einsum('crw,crl->cwl', basis_flat, coefficients, precision=lax.Precision.HIGHEST)
    return (near_field + expanded).reshape(densities.shape).astype(jnp.bfloat16)
```

```python
import functools

import jax
import jax.numpy as jnp
from jax import lax
from jax.experimental import pallas as pl
from jax.experimental.pallas import tpu as pltpu
from jax.sharding import PartitionSpec as P


CS = 256
LOADS = 128
RANK = 32
HALF = CS // 2
DENS = 3 * HALF
UNIT = 2 * DENS + RANK
FULL = 3 * CS + RANK
AXES = ("row", "col")
SIDE = 4

eps_square = 0.0004
lame_ratio = 1.8
kelvin_coef = 1.0 / (16.0 * 3.141592653589793 * 0.7)
VMEM_LIMIT = 48 * 1024 * 1024
bf16 = jnp.bfloat16
f32 = jnp.float32


def routes(move):
    pairs = []
    for z in range(SIDE):
        for core in range(2):
            for y in range(SIDE):
                for x in range(SIDE):
                    to_z, to_core, to_y, to_x = move(z, core, y, x)
                    source = (z * 2 + core) * 16 + y * SIDE + x
                    target = ((to_z % SIDE) * 2 + to_core) * 16 + (to_y % SIDE) * SIDE + to_x % SIDE
                    pairs.append((source, target))
    return pairs


def swap_core(value):
    return lax.ppermute(value, AXES, routes(lambda z, c, y, x: (z, 1 - c, y, x)))


def along_first(value, step):
    move = lambda z, c, y, x: (z, c, y, x + step) if c == 0 else (z, c, y + step, x)
    return lax.ppermute(value, AXES, routes(move))


def along_second(value, step):
    move = lambda z, c, y, x: (z, c, y + step, x) if c == 0 else (z, c, y, x + step)
    return lax.ppermute(value, AXES, routes(move))


def along_z(value, step):
    return lax.ppermute(value, AXES, routes(lambda z, c, y, x: (z + step, c, y, x)))


def whole(count):
    return [pl.BlockSpec(memory_space=pltpu.VMEM)] * count


def dot32(a, b):
    return jnp.dot(a, b, preferred_element_type=f32)


def prepare_kernel(core_ref, dens_ref, bases_ref, own_ref, other_ref, moments_ref):
    core = core_ref[0]
    total = jnp.zeros((RANK, LOADS), f32)
    mine = pl.multiple_of(core * HALF, HALF)
    theirs = pl.multiple_of((1 - core) * HALF, HALF)
    for j in range(3):
        total += dot32(bases_ref[0, :, j, :], dens_ref[0, j])
        own_ref[j * HALF : (j + 1) * HALF] = dens_ref[0, j, pl.ds(mine, HALF), :]
        other_ref[j * HALF : (j + 1) * HALF] = dens_ref[0, j, pl.ds(theirs, HALF), :]
    moments_ref[...] = total.astype(bf16)


def prepare(core, densities, bases):
    half = jax.ShapeDtypeStruct((DENS, LOADS), bf16)
    return pl.pallas_call(
        prepare_kernel,
        out_shape=(half, half, jax.ShapeDtypeStruct((RANK, LOADS), bf16)),
        in_specs=[pl.BlockSpec(memory_space=pltpu.SMEM)] + whole(2),
        out_specs=tuple(whole(3)),
        name="moments_and_halves",
    )(jnp.reshape(core, (1,)), densities, bases)


def near_kernel(first_unit, buffers, is_first, is_last, counts, sources, targets, blocks, *refs):
    units = 2 * buffers
    slots = 2 * units
    held = refs[:buffers]
    refs = refs[buffers:]
    if not is_first:
        carried, refs = refs[0], refs[1:]
    if is_last:
        keep, send, refs = refs[0], refs[1], refs[2:]
    else:
        result, refs = refs[0], refs[1:]
    acc, flat, spread, tile, code, weight, sems = refs

    copies = []
    for k in range(buffers):
        place = flat.at[k * 2 * UNIT : (k + 1) * 2 * UNIT]
        copies.append(pltpu.make_async_copy(held[k], place, sems.at[k]))
        copies[-1].start()

    def list_target(t, filled):
        for s in range(slots):
            count = counts[t, 2 * first_unit + s]
            code[filled] = t * 64 + s
            weight[filled] = count
            filled = filled + jnp.where(count > 0, 1, 0)
        code[filled] = t * 64
        weight[filled] = 0
        return filled + (filled & 1)

    entries = lax.fori_loop(0, 8, list_target, 0)
    for t in range(8):
        columns = jnp.transpose(targets[t])
        for i in range(4):
            spread[t, i] = jnp.broadcast_to(columns[:, i : i + 1], (CS, HALF))
    if is_first:
        acc[:, : 3 * CS] = jnp.zeros((8, 3 * CS, LOADS), f32)
    else:
        acc[...] = carried[...]
    for copy in copies:
        copy.wait()

    moments = jnp.concatenate(
        [flat[u * UNIT + 2 * DENS : (u + 1) * UNIT, :] for u in range(units)], axis=0
    )
    far = dot32(blocks[...], moments)
    for t in range(8):
        part = far[t * RANK : (t + 1) * RANK]
        if is_first:
            acc[t, 3 * CS :] = part
        else:
            acc[t, 3 * CS :] += part

    def make_tile(t, slot, amount):
        rows = []
        for h in range(2):
            row = sources[2 * first_unit + slot[h]]
            rows.append((row[0:1], row[1:2], row[2:3], row[3:4] * amount[h]))
        step = 16
        for at in range(0, CS, step):
            here = [spread[t, i, at : at + step] for i in range(4)]
            for h in range(2):
                lanes = slice(h * HALF, (h + 1) * HALF)
                dx, dy, dz = (here[i] - rows[h][i] for i in range(3))
                inverse = lax.rsqrt(dx * dx + dy * dy + dz * dz + eps_square)
                scaled = (here[3] * rows[h][3]) * inverse
                cubed = scaled * (inverse * inverse)
                level = lame_ratio * scaled
                ex, ey, ez = dx * cubed, dy * cubed, dz * cubed
                values = (dx * ex + level, dy * ey + level, dz * ez + level, dx * ey, dx * ez, dy * ez)
                for b in range(6):
                    tile[b, at : at + step, lanes] = values[b].astype(bf16)

    def add_products(t, slot):
        f = []
        for j in range(3):
            parts = []
            for h in range(2):
                base = slot[h] // 2 * UNIT + slot[h] % 2 * DENS + j * HALF
                parts.append(flat[pl.ds(pl.multiple_of(base, 16), HALF), :])
            f.append(jnp.concatenate(parts, axis=0))
        xy = dot32(tile[3], jnp.concatenate([f[1], f[0]], axis=1))
        xz = dot32(tile[4], jnp.concatenate([f[2], f[0]], axis=1))
        yz = dot32(tile[5], jnp.concatenate([f[2], f[1]], axis=1))
        acc[t, :CS] += xy[:, :LOADS] + xz[:, :LOADS] + dot32(tile[0], f[0])
        acc[t, CS : 2 * CS] += xy[:, LOADS:] + yz[:, :LOADS] + dot32(tile[1], f[1])
        acc[t, 2 * CS : 3 * CS] += xz[:, LOADS:] + yz[:, LOADS:] + dot32(tile[2], f[2])

    def task(k, carry):
        t = code[2 * k] // 64
        slot = [code[2 * k + h] % 64 for h in range(2)]
        amount = [weight[2 * k + h].astype(f32) * kelvin_coef for h in range(2)]
        make_tile(t, slot, amount)
        add_products(t, slot)
        return carry

    lax.fori_loop(0, entries // 2, task, 0)
    if is_last:
        keep[...] = acc[:4]
        send[...] = acc[4:].astype(bf16)
    else:
        result[...] = acc[...]


def near(first_unit, buffers, carried, is_last, counts, sources, targets, blocks):
    count = len(buffers)
    slots = 4 * count
    is_first = carried is None
    if is_last:
        shapes = (
            jax.ShapeDtypeStruct((4, FULL, LOADS), f32),
            jax.ShapeDtypeStruct((4, FULL, LOADS), bf16),
        )
        out_specs = tuple(whole(2))
    else:
        shapes = jax.ShapeDtypeStruct((8, FULL, LOADS), f32)
        out_specs = whole(1)[0]
    operands = [counts, sources, targets, blocks] + list(buffers)
    specs = [pl.BlockSpec(memory_space=pltpu.SMEM)] + whole(3)
    specs += [pl.BlockSpec(memory_space=pl.ANY)] * count
    if not is_first:
        operands.append(carried)
        specs += whole(1)
    return pl.pallas_call(
        functools.partial(near_kernel, first_unit, count, is_first, is_last),
        out_shape=shapes,
        in_specs=specs,
        out_specs=out_specs,
        scratch_shapes=[
            pltpu.VMEM((8, FULL, LOADS), f32),
            pltpu.VMEM((count * 2 * UNIT, LOADS), bf16),
            pltpu.VMEM((8, 4, CS, HALF), f32),
            pltpu.VMEM((6, CS, CS), bf16),
            pltpu.SMEM((8 * slots + 16,), jnp.int32),
            pltpu.SMEM((8 * slots + 16,), jnp.int32),
            pltpu.SemaphoreType.DMA((count,)),
        ],
        compiler_params=pltpu.CompilerParams(vmem_limit_bytes=VMEM_LIMIT),
        cost_estimate=pl.CostEstimate(
            flops=count * 1_000_000_000, bytes_accessed=8_000_000, transcendentals=count * 500_000
        ),
        name=f"near_from_{first_unit}",
    )(*operands)


def finish_kernel(keep, swapped, one, two, three, bases, out):
    def total(rows):
        return (
            keep[rows] + swapped[rows].astype(f32) + one[rows].astype(f32)
            + two[rows].astype(f32) + three[rows].astype(f32)
        )

    coefficients = total(slice(3 * CS, FULL))
    high = coefficients.astype(bf16)
    low = (coefficients - high.astype(f32)).astype(bf16)
    both = jnp.concatenate([high, low], axis=0)
    for j in range(3):
        basis = bases[0, :, j, :]
        twice = jnp.concatenate([basis, basis], axis=0)
        expanded = lax.dot_general(
            twice, both, (((0,), (0,)), ((), ())), preferred_element_type=f32
        )
        out[0, j] = (total(slice(j * CS, (j + 1) * CS)) + expanded).astype(bf16)


def finish(keep, swapped, others, bases):
    return pl.pallas_call(
        finish_kernel,
        out_shape=jax.ShapeDtypeStruct((1, 3, CS, LOADS), bf16),
        in_specs=whole(6),
        out_specs=whole(1)[0],
        name="sum_and_expand",
    )(keep, swapped, *others, bases)


def local(densities, positions, areas, bases, near_pairs, far_pairs, couplings):
    row = lax.axis_index("row")
    col = lax.axis_index("col")
    z, core = row // 2, row % 2
    y, x = col // SIDE, col % SIDE
    first_at = jnp.where(core == 0, x, y)
    second_at = jnp.where(core == 0, y, x)

    def unit_of(cluster):
        on_y, on_x = cluster // SIDE % SIDE, cluster % SIDE
        first = (jnp.where(core == 0, on_x, on_y) - first_at) % SIDE
        second = (jnp.where(core == 0, on_y, on_x) - second_at) % SIDE
        put = lambda r: jnp.where(r == 0, 0, jnp.where(r == 1, 2, jnp.where(r == 2, 3, 1)))
        return put(second) * SIDE + put(first)

    def other_core(cluster):
        return (cluster // 16 % 2 + core) % 2

    def slot_of(cluster):
        return jnp.where(cluster // 32 == z, unit_of(cluster) * 2 + other_core(cluster), -1)

    def target_of(cluster):
        place = other_core(cluster) * 4 + (cluster // 32 - z) % SIDE
        return jnp.where(cluster % 16 == col, place, -1)

    own, other, moments = prepare(core, densities, bases)
    partner = swap_core(other)
    unit = jnp.concatenate([own, partner, moments], axis=0)
    from_below = along_first(unit, 1)
    from_above = along_first(unit, -1)
    from_across = along_first(unit, 2)

    heads, tails = near_pairs[:, 0], near_pairs[:, 1]
    mark = lambda index, size: index[None, :] == jnp.arange(size, dtype=jnp.int32)[:, None]
    to_targets = jnp.concatenate(
        [target_of(heads), jnp.where(heads != tails, target_of(tails), -1)]
    )
    from_slots = jnp.concatenate([slot_of(tails), slot_of(heads)])
    counts = lax.dot_general(
        mark(to_targets, 8).astype(bf16),
        mark(from_slots, 32).astype(bf16),
        (((1,), (1,)), ((), ())),
        preferred_element_type=f32,
    ).astype(jnp.int32)

    far_heads, far_tails = far_pairs[:, 0], far_pairs[:, 1]

    def cell(target, source):
        ours = (target_of(target) >= 0) & (slot_of(source) >= 0) & (other_core(source) == 0)
        return jnp.where(ours, target_of(target) * 16 + unit_of(source), -1)

    forward = dot32(mark(cell(far_heads, far_tails), 128).astype(bf16), couplings)
    back_cell = jnp.where(far_heads != far_tails, cell(far_tails, far_heads), -1)
    backward = dot32(mark(back_cell, 128).astype(bf16), couplings)
    forward = forward.reshape(8, 16, RANK, RANK)
    backward = backward.reshape(8, 16, RANK, RANK)
    blocks = jnp.transpose(forward, (0, 2, 1, 3)) + jnp.transpose(backward, (0, 3, 1, 2))
    blocks = blocks.reshape(8 * RANK, 16 * RANK).astype(bf16)

    table = jnp.concatenate([positions, areas[:, None, :]], axis=1)
    slots = jnp.arange(32, dtype=jnp.int32)
    undo = lambda o: (jnp.where(o == 0, 0, jnp.where(o == 1, 3, jnp.where(o == 2, 1, 2))))
    slot_first = (undo(slots // 2 % 4) + first_at) % SIDE
    slot_second = (undo(slots // 8) + second_at) % SIDE
    slot_y = jnp.where(core == 0, slot_second, slot_first)
    slot_x = jnp.where(core == 0, slot_first, slot_second)
    slot_cluster = (slots % 2 + core) % 2 * 16 + slot_y * SIDE + slot_x
    plane = lax.dynamic_slice(table, (z * 32, 0, core * HALF), (32, 4, HALF))
    sources = jnp.take(plane, slot_cluster, axis=0)
    places = jnp.arange(8, dtype=jnp.int32)
    place_row = (places % 4 + z) % SIDE * 2 + (places // 4 + core) % 2
    targets = jnp.take(table, place_row * 16 + col, axis=0)
    targets = jnp.concatenate([targets, jnp.zeros((8, 4, CS), f32)], axis=1)

    tables = (counts, sources, targets)
    low = jnp.concatenate([unit, from_below], axis=0)
    high = jnp.concatenate([from_above, from_across], axis=0)
    low_below = along_second(low, 1)
    high_above = along_second(high, -1)
    high_below = along_second(high, 1)
    low_above = along_second(low, -1)
    low_across = along_second(low_below, 1)
    high_across = along_second(high_above, -1)

    part = lambda a, b: blocks[:, a * RANK : b * RANK]
    acc = near(0, (low, high), None, False, *tables, part(0, 4))
    acc = near(4, (low_below, high_below, low_above, high_above), acc, False, *tables, part(4, 12))
    keep, send = near(12, (low_across, high_across), acc, True, *tables, part(12, 16))

    swapped = swap_core(send)
    both = [(keep[k] + swapped[k].astype(f32)).astype(bf16) for k in range(1, 4)]
    others = [along_z(both[k - 1], k) for k in range(1, 4)]
    return finish(keep[0], swapped[0], others, bases)


def solution(mesh):
    return jax.shard_map(
        local,
        mesh=mesh,
        in_specs=(
            P(("row", "col"), None, None, None),
            P(),
            P(),
            P(("row", "col"), None, None, None),
            P(),
            P(),
            P(),
        ),
        out_specs=P(("row", "col"), None, None, None),
        check_vma=False,
    )
```

```python
import functools

import jax
import jax.numpy as jnp
from jax import lax
from jax.experimental import pallas as pl
from jax.experimental.pallas import tpu as pltpu
from jax.sharding import PartitionSpec as P


CS = 256
LOADS = 128
RANK = 32
HALF = CS // 2
DENS = 3 * HALF
UNIT = 2 * DENS + RANK
FULL = 3 * CS + RANK
AXES = ("row", "col")
SIDE = 4

eps_square = 0.0004
lame_ratio = 1.8
kelvin_coef = 1.0 / (16.0 * 3.141592653589793 * 0.7)
VMEM_LIMIT = 16 * 1024 * 1024
bf16 = jnp.bfloat16
f32 = jnp.float32


def routes(move):
    pairs = []
    for z in range(SIDE):
        for core in range(2):
            for y in range(SIDE):
                for x in range(SIDE):
                    to_z, to_core, to_y, to_x = move(z, core, y, x)
                    source = (z * 2 + core) * 16 + y * SIDE + x
                    target = ((to_z % SIDE) * 2 + to_core) * 16 + (to_y % SIDE) * SIDE + to_x % SIDE
                    pairs.append((source, target))
    return pairs


def swap_core(value):
    return lax.ppermute(value, AXES, routes(lambda z, c, y, x: (z, 1 - c, y, x)))


def along_first(value, step):
    move = lambda z, c, y, x: (z, c, y, x + step) if c == 0 else (z, c, y + step, x)
    return lax.ppermute(value, AXES, routes(move))


def along_second(value, step):
    move = lambda z, c, y, x: (z, c, y + step, x) if c == 0 else (z, c, y, x + step)
    return lax.ppermute(value, AXES, routes(move))


def along_z(value, step):
    return lax.ppermute(value, AXES, routes(lambda z, c, y, x: (z + step, c, y, x)))


def whole(count):
    return [pl.BlockSpec(memory_space=pltpu.VMEM)] * count


def dot32(a, b):
    return jnp.dot(a, b, preferred_element_type=f32)


def moments_kernel(dens_ref, bases_ref, moments_ref):
    total = jnp.zeros((RANK, LOADS), f32)
    for j in range(3):
        total += dot32(bases_ref[0, j], dens_ref[0, j])
    moments_ref[...] = total.astype(bf16)


def moments_of(densities, bases):
    return pl.pallas_call(
        moments_kernel,
        out_shape=jax.ShapeDtypeStruct((RANK, LOADS), bf16),
        in_specs=whole(2),
        out_specs=whole(1)[0],
        name="moments",
    )(densities, bases)


def unit_kernel(core_ref, own_ref, partner_ref, moments_ref, unit_ref):
    half = pl.ds(pl.multiple_of(core_ref[0] * HALF, HALF), HALF)
    for j in range(3):
        unit_ref[j * HALF : (j + 1) * HALF] = jnp.transpose(own_ref[0, j, half, :])
        unit_ref[DENS + j * HALF : DENS + (j + 1) * HALF] = jnp.transpose(
            partner_ref[0, j, half, :]
        )
    unit_ref[2 * DENS :] = moments_ref[...]


def make_unit(core, own, partner, moments):
    return pl.pallas_call(
        unit_kernel,
        out_shape=jax.ShapeDtypeStruct((UNIT, LOADS), bf16),
        in_specs=[pl.BlockSpec(memory_space=pltpu.SMEM)] + whole(3),
        out_specs=whole(1)[0],
        name="unit",
    )(jnp.reshape(core, (1,)), own, partner, moments)


def tables_kernel(
    here_ref, forward_ref, backward_ref, couplings_ref, positions_ref, areas_ref,
    blocks_ref, spread_ref, targets_ref, columns,
):
    z, core, y, x = (here_ref[k] for k in range(4))
    for t in range(8):
        cluster = (((t & 3) + z) & 3) * 32 + (((t >> 2) + core) & 1) * 16 + y * SIDE + x
        for i in range(3):
            targets_ref[t, i : i + 1, :] = positions_ref[i, pl.ds(cluster, 1), :]
        targets_ref[t, 3:4, :] = areas_ref[pl.ds(cluster, 1), :]
    half = lambda whole_row: jnp.where(core == 0, whole_row[:, :HALF], whole_row[:, HALF:])
    back = (0, 3, 1, 2)
    for s in range(32):
        first, second = back[(s >> 1) & 3], back[s >> 3]
        on_x = (x + jnp.where(core == 0, first, second)) & 3
        on_y = (y + jnp.where(core == 0, second, first)) & 3
        cluster = z * 32 + ((s + core) & 1) * 16 + on_y * SIDE + on_x
        for i in range(3):
            columns[s, i : i + 1, :] = half(positions_ref[i, pl.ds(cluster, 1), :])
        columns[s, 3:4, :] = half(areas_ref[pl.ds(cluster, 1), :])
    for s in range(32):
        upright = jnp.transpose(columns[s])
        for i in range(4):
            spread_ref[s, i] = jnp.broadcast_to(upright[:, i : i + 1], (HALF, LOADS))
    iota = lambda shape, dim: lax.broadcasted_iota(jnp.int32, shape, dim)
    cells, width = 128, RANK * RANK
    far = couplings_ref.shape[0]

    def summed(cell_ref):
        marks = iota((cells, far), 0) == cell_ref[...]
        return dot32(jnp.where(marks, 1.0, 0.0).astype(bf16), couplings_ref[...])

    at, to = iota((width, width), 0), iota((width, width), 1)
    flip = jnp.where((at // RANK == to % RANK) & (at % RANK == to // RANK), 1.0, 0.0)
    total = summed(forward_ref) + dot32(summed(backward_ref).astype(bf16), flip.astype(bf16))
    total = total.astype(bf16)
    columns = 16 * RANK
    row, lane = iota((cells, columns), 0), iota((cells, columns), 1)
    same_unit = row % 16 == lane // RANK
    spread = [
        jnp.where(row == lane % RANK + RANK * k, 1.0, 0.0).astype(bf16) for k in range(4)
    ]
    place, cell = iota((16, 2 * cells), 0), iota((16, 2 * cells), 1)
    gather = jnp.where(place == cell // 16, 1.0, 0.0).astype(bf16)
    for pair in range(RANK // 2):
        parts = []
        for r in (2 * pair, 2 * pair + 1):
            at = r // 4 * 128
            wide = dot32(total[:, at : at + 128], spread[r % 4])
            parts.append(jnp.where(same_unit, wide, 0.0).astype(bf16))
        both = jnp.concatenate(parts, axis=0)
        blocks_ref[pair * 16 : (pair + 1) * 16] = dot32(gather, both).astype(bf16)


def make_tables(here, forward, backward, couplings, positions, areas):
    return pl.pallas_call(
        tables_kernel,
        out_shape=(
            jax.ShapeDtypeStruct((8 * RANK, 16 * RANK), bf16),
            jax.ShapeDtypeStruct((32, 4, HALF, LOADS), f32),
            jax.ShapeDtypeStruct((8, 8, CS), f32),
        ),
        in_specs=[pl.BlockSpec(memory_space=pltpu.SMEM)] + whole(5),
        out_specs=tuple(whole(3)),
        scratch_shapes=[pltpu.VMEM((32, 8, HALF), f32)],
        compiler_params=pltpu.CompilerParams(vmem_limit_bytes=VMEM_LIMIT),
        name="tables",
    )(here, forward[None, :], backward[None, :], couplings, positions, areas)


def near_kernel(first_unit, buffers, is_first, is_last, counts, targets, spread, blocks, *refs):
    units = 2 * buffers
    slots = 2 * units
    held = refs[:buffers]
    refs = refs[buffers:]
    if not is_first:
        carried, refs = refs[0], refs[1:]
    if is_last:
        keep, send, acc, refs = refs[0], refs[1], refs[2], refs[3:]
    else:
        acc, refs = refs[0], refs[1:]
    flat, tile_a, tile_b, far, entry, sems = refs

    copies = []
    for k in range(buffers):
        place = flat.at[k * 2 * UNIT : (k + 1) * 2 * UNIT]
        copies.append(pltpu.make_async_copy(held[k], place, sems.at[k]))
        copies[-1].start()

    def list_target(t, filled):
        for value in [counts[t, 2 * first_unit + s] for s in range(slots)]:
            entry[filled] = value
            filled = filled + jnp.where(value >= 4096, 1, 0)
        entry[filled] = t * 64 + 2 * first_unit
        return filled + (filled & 1)

    entries = lax.fori_loop(0, 8, list_target, 0)
    for k in range(6):
        entry[entries + k] = 2 * first_unit
    if is_first:
        acc[:, : 3 * CS] = jnp.zeros((8, 3 * CS, LOADS), f32)
    else:
        acc[...] = carried[...]
    for copy in copies:
        copy.wait()

    moments = jnp.concatenate(
        [flat[u * UNIT + 2 * DENS : (u + 1) * UNIT, :] for u in range(units)], axis=0
    )
    far[...] = dot32(blocks[...], moments)
    for t in range(8):
        part = far[pl.ds(t, RANK, stride=8), :]
        if is_first:
            acc[t, 3 * CS :] = part
        else:
            acc[t, 3 * CS :] += part

    def decode(k):
        both = [entry[2 * k + h] for h in range(2)]
        return (both[0] >> 6) & 7, [v & 63 for v in both], [v >> 12 for v in both]

    def make_tile(k, tile):
        t, slot, pairs = decode(k)
        amount = [p.astype(f32) * kelvin_coef for p in pairs]
        point = targets[t]
        step = 16
        for at in range(0, CS, step):
            side = at // HALF
            rows = slice(at % HALF, at % HALF + step)
            here = [spread[slot[side], i, rows] for i in range(4)]
            for h in range(2):
                lanes = slice(h * HALF, (h + 1) * HALF)
                dx, dy, dz = (here[i] - point[i : i + 1, lanes] for i in range(3))
                inverse = lax.rsqrt(dx * dx + dy * dy + dz * dz + eps_square)
                scaled = (here[3] * (point[3:4, lanes] * amount[side])) * inverse
                cubed = scaled * (inverse * inverse)
                level = lame_ratio * scaled
                ex, ey, ez = dx * cubed, dy * cubed, dz * cubed
                values = (dx * ex + level, dy * ey + level, dz * ez + level, dx * ey, dx * ez, dy * ez)
                for b in range(6):
                    tile[b, at : at + step, lanes] = values[b].astype(bf16)

    def add_products(k, tile):
        t, slot, _ = decode(k)
        f = []
        for j in range(3):
            parts = []
            for h in range(2):
                base = ((slot[h] >> 1) - first_unit) * UNIT + (slot[h] & 1) * DENS + j * HALF
                parts.append(flat[pl.ds(pl.multiple_of(base, 16), HALF), :])
            f.append(jnp.concatenate(parts, axis=1))
        f = jnp.concatenate(f, axis=1)
        order = ((0, 3, 4), (3, 1, 5), (4, 5, 2))
        sums = [
            dot32(f, jnp.concatenate([tile[b] for b in order[i]], axis=0)) for i in range(3)
        ]
        for i in range(3):
            for h in range(2):
                at = (2 * i + h) * HALF
                acc[t, at : at + HALF] += sums[i][:, h * HALF : (h + 1) * HALF]

    tasks = entries >> 1

    @pl.when(tasks > 0)
    def _():
        make_tile(0, tile_a)

        def two_tasks(k, carry):
            make_tile(2 * k + 1, tile_b)
            add_products(2 * k, tile_a)

            @pl.when(2 * k + 1 < tasks)
            def _():
                make_tile(2 * k + 2, tile_a)
                add_products(2 * k + 1, tile_b)

            return carry

        lax.fori_loop(0, (tasks + 1) >> 1, two_tasks, 0)

    if is_last:
        keep[...] = acc[:4]
        send[...] = acc[4:].astype(bf16)


def near(first_unit, buffers, carried, is_last, counts, targets, spread, blocks):
    count = len(buffers)
    slots = 4 * count
    is_first = carried is None
    if is_last:
        shapes = (
            jax.ShapeDtypeStruct((4, FULL, LOADS), f32),
            jax.ShapeDtypeStruct((4, FULL, LOADS), bf16),
        )
        out_specs = tuple(whole(2))
    else:
        shapes = jax.ShapeDtypeStruct((8, FULL, LOADS), f32)
        out_specs = whole(1)[0]
    operands = [counts, targets, spread, blocks] + list(buffers)
    specs = [pl.BlockSpec(memory_space=pltpu.SMEM)] + whole(3)
    specs += [pl.BlockSpec(memory_space=pl.ANY)] * count
    if not is_first:
        operands.append(carried)
        specs += whole(1)
    return pl.pallas_call(
        functools.partial(near_kernel, first_unit, count, is_first, is_last),
        out_shape=shapes,
        in_specs=specs,
        out_specs=out_specs,
        scratch_shapes=([pltpu.VMEM((8, FULL, LOADS), f32)] if is_last else [])
        + [
            pltpu.VMEM((count * 2 * UNIT, LOADS), bf16),
            pltpu.VMEM((6, CS, CS), bf16),
            pltpu.VMEM((6, CS, CS), bf16),
            pltpu.VMEM((8 * RANK, LOADS), f32),
            pltpu.SMEM((8 * slots + 16,), jnp.int32),
            pltpu.SemaphoreType.DMA((count,)),
        ],
        compiler_params=pltpu.CompilerParams(vmem_limit_bytes=VMEM_LIMIT),
        cost_estimate=pl.CostEstimate(
            flops=count * 1_000_000_000, bytes_accessed=8_000_000, transcendentals=count * 500_000
        ),
        name=f"near_from_{first_unit}",
    )(*operands)


def finish_kernel(keep, swapped, one, two, three, bases, out):
    def total(rows):
        return (
            keep[0, rows] + swapped[0, rows].astype(f32) + one[rows].astype(f32)
            + two[rows].astype(f32) + three[rows].astype(f32)
        )

    coefficients = total(slice(3 * CS, FULL))
    high = coefficients.astype(bf16)
    low = (coefficients - high.astype(f32)).astype(bf16)
    both = jnp.concatenate([high, low], axis=0)
    for j in range(3):
        basis = bases[0, j]
        twice = jnp.concatenate([basis, basis], axis=0)
        expanded = lax.dot_general(
            twice, both, (((0,), (0,)), ((), ())), preferred_element_type=f32
        )
        for h in range(2):
            at = (2 * j + h) * HALF
            near_part = jnp.transpose(total(slice(at, at + HALF)))
            panels = slice(h * HALF, (h + 1) * HALF)
            out[0, j, panels] = (near_part + expanded[panels]).astype(bf16)


def finish(keep, swapped, others, bases):
    return pl.pallas_call(
        finish_kernel,
        out_shape=jax.ShapeDtypeStruct((1, 3, CS, LOADS), bf16),
        in_specs=[pl.BlockSpec((1, FULL, LOADS), lambda i: (0, 0, 0))] * 2
        + [pl.BlockSpec((FULL, LOADS), lambda i: (0, 0))] * 3
        + [pl.BlockSpec((1, 3, RANK, CS), lambda i: (0, 0, 0, 0))],
        out_specs=pl.BlockSpec((1, 3, CS, LOADS), lambda i: (0, 0, 0, 0)),
        grid=(1,),
        name="sum_and_expand",
    )(keep, swapped, *others, bases)


def local(densities, positions, areas, bases, near_pairs, far_pairs, couplings):
    row = lax.axis_index("row")
    col = lax.axis_index("col")
    z, core = row >> 1, row & 1
    y, x = col >> 2, col & 3
    first_at = jnp.where(core == 0, x, y)
    second_at = jnp.where(core == 0, y, x)

    def unit_of(cluster):
        on_y, on_x = (cluster >> 2) & 3, cluster & 3
        first = (jnp.where(core == 0, on_x, on_y) - first_at) & 3
        second = (jnp.where(core == 0, on_y, on_x) - second_at) & 3
        put = lambda r: jnp.where(r == 0, 0, jnp.where(r == 1, 2, jnp.where(r == 2, 3, 1)))
        return put(second) * SIDE + put(first)

    def other_core(cluster):
        return ((cluster >> 4) + core) & 1

    def slot_of(cluster):
        return jnp.where(cluster >> 5 == z, unit_of(cluster) * 2 + other_core(cluster), -1)

    def target_of(cluster):
        place = other_core(cluster) * 4 + (((cluster >> 5) - z) & 3)
        return jnp.where((cluster & 15) == col, place, -1)

    bases = jnp.transpose(bases, (0, 2, 1, 3))
    positions = jnp.transpose(positions, (1, 0, 2))

    partner = swap_core(densities)
    moments = moments_of(densities, bases)
    unit = make_unit(core, densities, partner, moments)
    from_below = along_first(unit, 1)
    from_above = along_first(unit, -1)
    from_across = along_first(unit, 2)
    near_pairs, far_pairs, couplings, positions, areas, unit = lax.optimization_barrier(
        (near_pairs, far_pairs, couplings, positions, areas, unit)
    )

    heads, tails = near_pairs[:, 0], near_pairs[:, 1]
    mark = lambda index, size: index[None, :] == jnp.arange(size, dtype=jnp.int32)[:, None]
    to_targets = jnp.concatenate(
        [target_of(heads), jnp.where(heads != tails, target_of(tails), -1)]
    )
    from_slots = jnp.concatenate([slot_of(tails), slot_of(heads)])
    counts = lax.dot_general(
        mark(to_targets, 8).astype(bf16),
        mark(from_slots, 32).astype(bf16),
        (((1,), (1,)), ((), ())),
        preferred_element_type=f32,
    ).astype(jnp.int32)
    counts = counts * 4096 + jnp.arange(8, dtype=jnp.int32)[:, None] * 64 + jnp.arange(32, dtype=jnp.int32)

    far_heads, far_tails = far_pairs[:, 0], far_pairs[:, 1]

    def cell(target, source):
        ours = (target_of(target) >= 0) & (slot_of(source) >= 0) & (other_core(source) == 0)
        return jnp.where(ours, target_of(target) * 16 + unit_of(source), -1)

    back_cell = jnp.where(far_heads != far_tails, cell(far_tails, far_heads), -1)
    here = jnp.stack([z, core, y, x]).astype(jnp.int32)
    blocks, spread, targets = make_tables(
        here, cell(far_heads, far_tails), back_cell, couplings, positions, areas
    )

    (counts, targets, spread, blocks, unit, from_below, from_above, from_across) = (
        lax.optimization_barrier(
            (counts, targets, spread, blocks, unit, from_below, from_above, from_across)
        )
    )
    tables = (counts, targets, spread)
    low = jnp.concatenate([unit, from_below], axis=0)
    high = jnp.concatenate([from_above, from_across], axis=0)
    low_below = along_second(low, 1)
    high_above = along_second(high, -1)
    high_below = along_second(high, 1)
    low_above = along_second(low, -1)
    low_across = along_second(low_below, 1)
    high_across = along_second(high_above, -1)

    part = lambda a, b: blocks[:, a * RANK : b * RANK]
    acc = near(0, (low, high), None, False, *tables, part(0, 4))
    acc = near(4, (low_below, high_below, low_above, high_above), acc, False, *tables, part(4, 12))
    keep, send = near(12, (low_across, high_across), acc, True, *tables, part(12, 16))

    swapped = swap_core(send)
    both = [(keep[k] + swapped[k].astype(f32)).astype(bf16) for k in range(1, 4)]
    others = [along_z(both[k - 1], k) for k in range(1, 4)]
    return finish(keep, swapped, others, bases)


def solution(mesh):
    return jax.shard_map(
        local,
        mesh=mesh,
        in_specs=(
            P(("row", "col"), None, None, None),
            P(),
            P(),
            P(("row", "col"), None, None, None),
            P(),
            P(),
            P(),
        ),
        out_specs=P(("row", "col"), None, None, None),
        check_vma=False,
    )
```

```python
import functools

import jax
import jax.numpy as jnp
from jax import lax
from jax.experimental import pallas as pl
from jax.experimental.pallas import tpu as pltpu
from jax.sharding import PartitionSpec as P


CS = 256
LOADS = 128
RANK = 32
HALF = CS // 2
DENS = 3 * HALF
UNIT = 2 * DENS + RANK
FULL = 3 * CS + RANK
AXES = ("row", "col")
SIDE = 4

eps_square = 0.0004
lame_ratio = 1.8
kelvin_coef = 1.0 / (16.0 * 3.141592653589793 * 0.7)
VMEM_LIMIT = 16 * 1024 * 1024
bf16 = jnp.bfloat16
f32 = jnp.float32


def routes(move):
    pairs = []
    for z in range(SIDE):
        for core in range(2):
            for y in range(SIDE):
                for x in range(SIDE):
                    to_z, to_core, to_y, to_x = move(z, core, y, x)
                    source = (z * 2 + core) * 16 + y * SIDE + x
                    target = ((to_z % SIDE) * 2 + to_core) * 16 + (to_y % SIDE) * SIDE + to_x % SIDE
                    pairs.append((source, target))
    return pairs


def swap_core(value):
    return lax.ppermute(value, AXES, routes(lambda z, c, y, x: (z, 1 - c, y, x)))


def along_first(value, step):
    move = lambda z, c, y, x: (z, c, y, x + step) if c == 0 else (z, c, y + step, x)
    return lax.ppermute(value, AXES, routes(move))


def along_second(value, step):
    move = lambda z, c, y, x: (z, c, y + step, x) if c == 0 else (z, c, y, x + step)
    return lax.ppermute(value, AXES, routes(move))


def along_z(value, step):
    return lax.ppermute(value, AXES, routes(lambda z, c, y, x: (z + step, c, y, x)))


def whole(count):
    return [pl.BlockSpec(memory_space=pltpu.VMEM)] * count


def dot32(a, b):
    return jnp.dot(a, b, preferred_element_type=f32)


def iota(shape, dim):
    return lax.broadcasted_iota(jnp.int32, shape, dim)


def fetch(source, target, sem):
    copy = pltpu.make_async_copy(source, target, sem)
    copy.start()
    return copy


def moments_kernel(core_ref, dens_ref, bases_ref, own_ref, moments_ref, flip_ref, dens, bases, sems):
    copies = [fetch(dens_ref, dens, sems.at[0]), fetch(bases_ref, bases, sems.at[1])]
    width = RANK * RANK
    step = 128
    for at in range(0, width, step):
        source, target = iota((step, width), 0) + at, iota((step, width), 1)
        turned = ((target & (RANK - 1)) << 5) + (target >> 5)
        flip_ref[at : at + step] = jnp.where(source == turned, 1.0, 0.0).astype(bf16)
    half = pl.ds(pl.multiple_of(core_ref[0] * HALF, HALF), HALF)
    total = jnp.zeros((RANK, LOADS), f32)
    for copy in copies:
        copy.wait()
    for j in range(3):
        total += dot32(bases[0, j], dens[0, j])
        own_ref[j * HALF : (j + 1) * HALF] = jnp.transpose(dens[0, j, half, :])
    moments_ref[...] = total.astype(bf16)


def in_hbm(array):
    return pltpu.with_memory_space_constraint(array, pltpu.HBM)


def moments_of(core, densities, bases):
    width = RANK * RANK
    return pl.pallas_call(
        moments_kernel,
        out_shape=(
            jax.ShapeDtypeStruct((DENS, LOADS), bf16),
            jax.ShapeDtypeStruct((RANK, LOADS), bf16),
            jax.ShapeDtypeStruct((width, width), bf16),
        ),
        in_specs=[pl.BlockSpec(memory_space=pltpu.SMEM)] + [pl.BlockSpec(memory_space=pltpu.HBM)] * 2,
        out_specs=tuple(whole(3)),
        scratch_shapes=[
            pltpu.VMEM(densities.shape, bf16),
            pltpu.VMEM(bases.shape, bf16),
            pltpu.SemaphoreType.DMA((2,)),
        ],
        compiler_params=pltpu.CompilerParams(vmem_limit_bytes=VMEM_LIMIT),
        name="moments",
    )(jnp.reshape(core, (1,)), in_hbm(densities), in_hbm(bases))


def unit_kernel(core_ref, own_ref, partner_ref, moments_ref, unit_ref):
    half = pl.ds(pl.multiple_of(core_ref[0] * HALF, HALF), HALF)
    unit_ref[:DENS] = own_ref[...]
    for j in range(3):
        unit_ref[DENS + j * HALF : DENS + (j + 1) * HALF] = jnp.transpose(
            partner_ref[0, j, half, :]
        )
    unit_ref[2 * DENS :] = moments_ref[...]


def make_unit(core, own, partner, moments):
    return pl.pallas_call(
        unit_kernel,
        out_shape=jax.ShapeDtypeStruct((UNIT, LOADS), bf16),
        in_specs=[pl.BlockSpec(memory_space=pltpu.SMEM)] + whole(3),
        out_specs=whole(1)[0],
        compiler_params=pltpu.CompilerParams(vmem_limit_bytes=VMEM_LIMIT),
        name="unit",
    )(jnp.reshape(core, (1,)), own, partner, moments)


def points_kernel(
    here_ref, positions_ref, areas_ref, couplings_ref,
    spread_ref, targets_ref, held_couplings, columns, positions, areas, sems,
):
    first = [fetch(positions_ref, positions, sems.at[0]), fetch(areas_ref, areas, sems.at[1])]
    last = fetch(couplings_ref, held_couplings, sems.at[2])
    z, core, y, x = (here_ref[k] for k in range(4))
    half = lambda whole_row: jnp.where(core == 0, whole_row[:, :HALF], whole_row[:, HALF:])
    back = (0, 3, 1, 2)
    for copy in first:
        copy.wait()
    for t in range(8):
        cluster = (((t & 3) + z) & 3) * 32 + (((t >> 2) + core) & 1) * 16 + y * SIDE + x
        for i in range(3):
            targets_ref[t, i : i + 1, :] = positions[i, pl.ds(cluster, 1), :]
        targets_ref[t, 3:4, :] = areas[pl.ds(cluster, 1), :]
    for s in range(32):
        first, second = back[(s >> 1) & 3], back[s >> 3]
        on_x = (x + jnp.where(core == 0, first, second)) & 3
        on_y = (y + jnp.where(core == 0, second, first)) & 3
        cluster = z * 32 + ((s + core) & 1) * 16 + on_y * SIDE + on_x
        for i in range(3):
            columns[s, i : i + 1, :] = half(positions[i, pl.ds(cluster, 1), :])
        columns[s, 3:4, :] = half(areas[pl.ds(cluster, 1), :])
    for s in range(32):
        upright = jnp.transpose(columns[s])
        for i in range(4):
            spread_ref[s, i] = jnp.broadcast_to(upright[:, i : i + 1], (HALF, LOADS))
    last.wait()


def make_points(here, positions, areas, couplings):
    return pl.pallas_call(
        points_kernel,
        out_shape=(
            jax.ShapeDtypeStruct((32, 4, HALF, LOADS), f32),
            jax.ShapeDtypeStruct((8, 8, CS), f32),
            jax.ShapeDtypeStruct(couplings.shape, bf16),
        ),
        in_specs=[pl.BlockSpec(memory_space=pltpu.SMEM)] + [pl.BlockSpec(memory_space=pltpu.HBM)] * 3,
        out_specs=tuple(whole(3)),
        scratch_shapes=[
            pltpu.VMEM((32, 8, HALF), f32),
            pltpu.VMEM(positions.shape, f32),
            pltpu.VMEM(areas.shape, f32),
            pltpu.SemaphoreType.DMA((3,)),
        ],
        compiler_params=pltpu.CompilerParams(vmem_limit_bytes=VMEM_LIMIT),
        name="points",
    )(here, in_hbm(positions), in_hbm(areas), in_hbm(couplings))


def blocks_kernel(forward_ref, backward_ref, couplings_ref, flip_ref, blocks_ref):
    cells = 128
    far = couplings_ref.shape[0]

    def summed(cell_ref):
        marks = iota((cells, far), 0) == cell_ref[...]
        return dot32(jnp.where(marks, 1.0, 0.0).astype(bf16), couplings_ref[...])

    total = summed(forward_ref) + dot32(summed(backward_ref).astype(bf16), flip_ref[...])
    total = total.astype(bf16)
    columns = 16 * RANK
    row, lane = iota((cells, columns), 0), iota((cells, columns), 1)
    same_unit = (row & 15) == (lane >> 5)
    spread = [jnp.where(row == (lane & 31) + RANK * k, 1.0, 0.0).astype(bf16) for k in range(4)]
    place, cell = iota((16, 2 * cells), 0), iota((16, 2 * cells), 1)
    gather = jnp.where(place == (cell >> 4), 1.0, 0.0).astype(bf16)
    for pair in range(RANK // 2):
        parts = []
        for r in (2 * pair, 2 * pair + 1):
            at = r // 4 * 128
            wide = dot32(total[:, at : at + 128], spread[r % 4])
            parts.append(jnp.where(same_unit, wide, 0.0).astype(bf16))
        both = jnp.concatenate(parts, axis=0)
        blocks_ref[pair * 16 : (pair + 1) * 16] = dot32(gather, both).astype(bf16)


def make_blocks(forward, backward, couplings, flip):
    return pl.pallas_call(
        blocks_kernel,
        out_shape=jax.ShapeDtypeStruct((8 * RANK, 16 * RANK), bf16),
        in_specs=whole(4),
        out_specs=whole(1)[0],
        compiler_params=pltpu.CompilerParams(vmem_limit_bytes=VMEM_LIMIT),
        name="coupling_blocks",
    )(forward[None, :], backward[None, :], couplings, flip)


def near_kernel(first_unit, buffers, is_first, is_last, counts, targets, spread, blocks, *refs):
    units = 2 * buffers
    slots = 2 * units
    held = refs[:buffers]
    refs = refs[buffers:]
    if not is_first:
        carried, refs = refs[0], refs[1:]
    if is_last:
        keep, send, acc, refs = refs[0], refs[1], refs[2], refs[3:]
    else:
        acc, refs = refs[0], refs[1:]
    flat, tile_a, tile_b, far, entry = refs

    for k in range(buffers):
        flat[k * 2 * UNIT : (k + 1) * 2 * UNIT] = held[k][...]

    def list_target(t, filled):
        for value in [counts[t, 2 * first_unit + s] for s in range(slots)]:
            entry[filled] = value
            filled = filled + jnp.where(value >= 4096, 1, 0)
        entry[filled] = t * 64 + 2 * first_unit
        return filled + (filled & 1)

    entries = lax.fori_loop(0, 8, list_target, 0)
    for k in range(6):
        entry[entries + k] = 2 * first_unit
    if is_first:
        acc[:, : 3 * CS] = jnp.zeros((8, 3 * CS, LOADS), f32)
    else:
        acc[...] = carried[...]

    moments = jnp.concatenate(
        [flat[u * UNIT + 2 * DENS : (u + 1) * UNIT, :] for u in range(units)], axis=0
    )
    far[...] = dot32(blocks[...], moments)
    for t in range(8):
        part = far[pl.ds(t, RANK, stride=8), :]
        if is_first:
            acc[t, 3 * CS :] = part
        else:
            acc[t, 3 * CS :] += part

    def decode(k):
        both = [entry[2 * k + h] for h in range(2)]
        return (both[0] >> 6) & 7, [v & 63 for v in both], [v >> 12 for v in both]

    def make_tile(k, tile):
        t, slot, pairs = decode(k)
        amount = [p.astype(f32) * kelvin_coef for p in pairs]
        point = targets[t]
        step = 16
        for at in range(0, CS, step):
            side = at // HALF
            rows = slice(at % HALF, at % HALF + step)
            here = [spread[slot[side], i, rows] for i in range(4)]
            for h in range(2):
                lanes = slice(h * HALF, (h + 1) * HALF)
                dx, dy, dz = (here[i] - point[i : i + 1, lanes] for i in range(3))
                inverse = lax.rsqrt(dx * dx + dy * dy + dz * dz + eps_square)
                scaled = (here[3] * (point[3:4, lanes] * amount[side])) * inverse
                cubed = scaled * (inverse * inverse)
                level = lame_ratio * scaled
                ex, ey, ez = dx * cubed, dy * cubed, dz * cubed
                values = (dx * ex + level, dy * ey + level, dz * ez + level, dx * ey, dx * ez, dy * ez)
                for b in range(6):
                    tile[b, at : at + step, lanes] = values[b].astype(bf16)

    def add_products(k, tile):
        t, slot, _ = decode(k)
        f = []
        for j in range(3):
            parts = []
            for h in range(2):
                base = ((slot[h] >> 1) - first_unit) * UNIT + (slot[h] & 1) * DENS + j * HALF
                parts.append(flat[pl.ds(pl.multiple_of(base, 16), HALF), :])
            f.append(jnp.concatenate(parts, axis=1))
        f = jnp.concatenate(f, axis=1)
        order = ((0, 3, 4), (3, 1, 5), (4, 5, 2))
        sums = [
            dot32(f, jnp.concatenate([tile[b] for b in order[i]], axis=0)) for i in range(3)
        ]
        for i in range(3):
            for h in range(2):
                at = (2 * i + h) * HALF
                acc[t, at : at + HALF] += sums[i][:, h * HALF : (h + 1) * HALF]

    tasks = entries >> 1

    @pl.when(tasks > 0)
    def _():
        make_tile(0, tile_a)

        def two_tasks(k, carry):
            make_tile(2 * k + 1, tile_b)
            add_products(2 * k, tile_a)

            @pl.when(2 * k + 1 < tasks)
            def _():
                make_tile(2 * k + 2, tile_a)
                add_products(2 * k + 1, tile_b)

            return carry

        lax.fori_loop(0, (tasks + 1) >> 1, two_tasks, 0)

    if is_last:
        keep[...] = acc[:4]
        send[...] = acc[4:].astype(bf16)


def near(first_unit, buffers, carried, is_last, counts, targets, spread, blocks):
    count = len(buffers)
    slots = 4 * count
    is_first = carried is None
    operands = [counts, targets, spread, blocks] + list(buffers)
    specs = [pl.BlockSpec(memory_space=pltpu.SMEM)] + whole(3)
    specs += whole(count)
    if not is_first:
        operands.append(carried)
        specs += whole(1)
    if is_last:
        shapes = (
            jax.ShapeDtypeStruct((4, FULL, LOADS), f32),
            jax.ShapeDtypeStruct((4, FULL, LOADS), bf16),
        )
        out_specs = tuple(whole(2))
    else:
        shapes = jax.ShapeDtypeStruct((8, FULL, LOADS), f32)
        out_specs = whole(1)[0]
    return pl.pallas_call(
        functools.partial(near_kernel, first_unit, count, is_first, is_last),
        out_shape=shapes,
        in_specs=specs,
        out_specs=out_specs,
        scratch_shapes=([pltpu.VMEM((8, FULL, LOADS), f32)] if is_last else [])
        + [
            pltpu.VMEM((count * 2 * UNIT, LOADS), bf16),
            pltpu.VMEM((6, CS, CS), bf16),
            pltpu.VMEM((6, CS, CS), bf16),
            pltpu.VMEM((8 * RANK, LOADS), f32),
            pltpu.SMEM((8 * slots + 16,), jnp.int32),
        ],
        compiler_params=pltpu.CompilerParams(vmem_limit_bytes=VMEM_LIMIT),
        cost_estimate=pl.CostEstimate(
            flops=count * 1_000_000_000, bytes_accessed=8_000_000,
            transcendentals=count * 500_000,
        ),
        name=f"near_from_{first_unit}",
    )(*operands)


def finish_kernel(keep, swapped, one, two, three, bases, out):
    def total(rows):
        return (
            keep[0, rows] + swapped[0, rows].astype(f32) + one[rows].astype(f32)
            + two[rows].astype(f32) + three[rows].astype(f32)
        )

    coefficients = total(slice(3 * CS, FULL))
    high = coefficients.astype(bf16)
    low = (coefficients - high.astype(f32)).astype(bf16)
    both = jnp.concatenate([high, low], axis=0)
    for j in range(3):
        basis = bases[0, j]
        twice = jnp.concatenate([basis, basis], axis=0)
        expanded = lax.dot_general(
            twice, both, (((0,), (0,)), ((), ())), preferred_element_type=f32
        )
        for h in range(2):
            at = (2 * j + h) * HALF
            near_part = jnp.transpose(total(slice(at, at + HALF)))
            panels = slice(h * HALF, (h + 1) * HALF)
            out[0, j, panels] = (near_part + expanded[panels]).astype(bf16)


def finish(keep, swapped, others, bases):
    return pl.pallas_call(
        finish_kernel,
        out_shape=jax.ShapeDtypeStruct((1, 3, CS, LOADS), bf16),
        in_specs=whole(6),
        out_specs=whole(1)[0],
        compiler_params=pltpu.CompilerParams(vmem_limit_bytes=VMEM_LIMIT),
        name="sum_and_expand",
    )(keep, swapped, *others, bases)


def local(densities, positions, areas, bases, near_pairs, far_pairs, couplings):
    row = lax.axis_index("row")
    col = lax.axis_index("col")
    z, core = row >> 1, row & 1
    y, x = col >> 2, col & 3
    first_at = jnp.where(core == 0, x, y)
    second_at = jnp.where(core == 0, y, x)

    def unit_of(cluster):
        on_y, on_x = (cluster >> 2) & 3, cluster & 3
        first = (jnp.where(core == 0, on_x, on_y) - first_at) & 3
        second = (jnp.where(core == 0, on_y, on_x) - second_at) & 3
        put = lambda r: jnp.where(r == 0, 0, jnp.where(r == 1, 2, jnp.where(r == 2, 3, 1)))
        return put(second) * SIDE + put(first)

    def other_core(cluster):
        return ((cluster >> 4) + core) & 1

    def slot_of(cluster):
        return jnp.where(cluster >> 5 == z, unit_of(cluster) * 2 + other_core(cluster), -1)

    def target_of(cluster):
        place = other_core(cluster) * 4 + (((cluster >> 5) - z) & 3)
        return jnp.where((cluster & 15) == col, place, -1)

    bases = jnp.transpose(bases, (0, 2, 1, 3))
    positions = jnp.transpose(positions, (1, 0, 2))

    partner = swap_core(densities)
    own, moments, flip = moments_of(core, densities, bases)
    unit = make_unit(core, own, partner, moments)
    from_below = along_first(unit, 1)
    from_above = along_first(unit, -1)
    from_across = along_first(unit, 2)
    here = jnp.stack([z, core, y, x]).astype(jnp.int32)
    here, unit = lax.optimization_barrier((here, unit))
    spread, targets, couplings = make_points(here, positions, areas, couplings)
    (near_pairs, far_pairs, couplings, spread, targets, unit, from_below, from_above, from_across) = (
        lax.optimization_barrier(
            (near_pairs, far_pairs, couplings, spread, targets, unit)
            + (from_below, from_above, from_across)
        )
    )
    low = jnp.concatenate([unit, from_below], axis=0)
    high = jnp.concatenate([from_above, from_across], axis=0)
    low_below = along_second(low, 1)
    high_above = along_second(high, -1)
    high_below = along_second(high, 1)
    low_above = along_second(low, -1)

    heads, tails = near_pairs[:, 0], near_pairs[:, 1]
    mark = lambda index, size: index[None, :] == jnp.arange(size, dtype=jnp.int32)[:, None]
    to_targets = jnp.concatenate(
        [target_of(heads), jnp.where(heads != tails, target_of(tails), -1)]
    )
    from_slots = jnp.concatenate([slot_of(tails), slot_of(heads)])
    counts = lax.dot_general(
        mark(to_targets, 8).astype(bf16),
        mark(from_slots, 32).astype(bf16),
        (((1,), (1,)), ((), ())),
        preferred_element_type=f32,
    ).astype(jnp.int32)
    counts = counts * 4096 + jnp.arange(8, dtype=jnp.int32)[:, None] * 64 + jnp.arange(32, dtype=jnp.int32)

    far_heads, far_tails = far_pairs[:, 0], far_pairs[:, 1]

    def cell(target, source):
        ours = (target_of(target) >= 0) & (slot_of(source) >= 0) & (other_core(source) == 0)
        return jnp.where(ours, target_of(target) * 16 + unit_of(source), -1)

    back_cell = jnp.where(far_heads != far_tails, cell(far_tails, far_heads), -1)
    blocks = make_blocks(cell(far_heads, far_tails), back_cell, couplings, flip)
    tables = (counts, targets, spread)

    part = lambda a, b: blocks[:, a * RANK : b * RANK]
    acc = near(0, (low, high), None, False, *tables, part(0, 4))
    low_below, high_above, acc = lax.optimization_barrier((low_below, high_above, acc))
    low_across = along_second(low_below, 1)
    high_across = along_second(high_above, -1)
    acc = near(
        4, (low_below, high_below, low_above, high_above), acc, False, *tables, part(4, 12)
    )
    last = (low_across, high_across)
    keep, send = near(12, last, acc, True, *tables, part(12, 16))

    swapped = swap_core(send)
    both = [(keep[k] + swapped[k].astype(f32)).astype(bf16) for k in range(1, 4)]
    others = [along_z(both[k - 1], k) for k in range(1, 4)]
    return finish(keep, swapped, others, bases)


def solution(mesh):
    return jax.shard_map(
        local,
        mesh=mesh,
        in_specs=(
            P(("row", "col"), None, None, None),
            P(),
            P(),
            P(("row", "col"), None, None, None),
            P(),
            P(),
            P(),
        ),
        out_specs=P(("row", "col"), None, None, None),
        check_vma=False,
    )
```

```python
import functools

import jax
import jax.numpy as jnp
from jax import lax
from jax.experimental import pallas as pl
from jax.experimental.pallas import tpu as pltpu
from jax.sharding import PartitionSpec as P


CS = 256
LOADS = 128
RANK = 32
HALF = CS // 2
DENS = 3 * HALF
UNIT = 2 * DENS + RANK
FULL = 3 * CS + RANK
AXES = ("row", "col")
TARGETS = ((1, 0), (2, 0), (3, 0), (0, 1), (1, 1), (2, 1), (3, 1), (0, 0))
AWAY = 7
SPANS = {"first": (0, AWAY), "middle": (0, AWAY), "send": (3, AWAY), "keep": (0, 3), "own": (AWAY, 8)}
SIDE = 4

eps_square = 0.0004
lame_ratio = 1.8
kelvin_coef = 1.0 / (16.0 * 3.141592653589793 * 0.7)
VMEM_LIMIT = 16 * 1024 * 1024
bf16 = jnp.bfloat16
f32 = jnp.float32


def routes(move):
    pairs = []
    for z in range(SIDE):
        for core in range(2):
            for y in range(SIDE):
                for x in range(SIDE):
                    to_z, to_core, to_y, to_x = move(z, core, y, x)
                    source = (z * 2 + core) * 16 + y * SIDE + x
                    target = ((to_z % SIDE) * 2 + to_core) * 16 + (to_y % SIDE) * SIDE + to_x % SIDE
                    pairs.append((source, target))
    return pairs


def swap_core(value):
    return lax.ppermute(value, AXES, routes(lambda z, c, y, x: (z, 1 - c, y, x)))


def along_first(value, step):
    move = lambda z, c, y, x: (z, c, y, x + step) if c == 0 else (z, c, y + step, x)
    return lax.ppermute(value, AXES, routes(move))


def along_second(value, step):
    move = lambda z, c, y, x: (z, c, y + step, x) if c == 0 else (z, c, y, x + step)
    return lax.ppermute(value, AXES, routes(move))


def along_z(value, step):
    return lax.ppermute(value, AXES, routes(lambda z, c, y, x: (z + step, c, y, x)))


def whole(count):
    return [pl.BlockSpec(memory_space=pltpu.VMEM)] * count


def dot32(a, b):
    return jnp.dot(a, b, preferred_element_type=f32)


def iota(shape, dim):
    return lax.broadcasted_iota(jnp.int32, shape, dim)


def fetch(source, target, sem):
    copy = pltpu.make_async_copy(source, target, sem)
    copy.start()
    return copy


def moments_kernel(core_ref, dens_ref, bases_ref, own_ref, moments_ref, flip_ref, dens, bases, sems):
    copies = [fetch(dens_ref, dens, sems.at[0]), fetch(bases_ref, bases, sems.at[1])]
    width = RANK * RANK
    step = 128
    for at in range(0, width, step):
        source, target = iota((step, width), 0) + at, iota((step, width), 1)
        turned = ((target & (RANK - 1)) << 5) + (target >> 5)
        flip_ref[at : at + step] = jnp.where(source == turned, 1.0, 0.0).astype(bf16)
    half = pl.ds(pl.multiple_of(core_ref[0] * HALF, HALF), HALF)
    total = jnp.zeros((RANK, LOADS), f32)
    for copy in copies:
        copy.wait()
    for j in range(3):
        total += dot32(bases[0, j], dens[0, j])
        own_ref[j * HALF : (j + 1) * HALF] = jnp.transpose(dens[0, j, half, :])
    moments_ref[...] = total.astype(bf16)


def in_hbm(array):
    return pltpu.with_memory_space_constraint(array, pltpu.HBM)


def moments_of(core, densities, bases):
    width = RANK * RANK
    return pl.pallas_call(
        moments_kernel,
        out_shape=(
            jax.ShapeDtypeStruct((DENS, LOADS), bf16),
            jax.ShapeDtypeStruct((RANK, LOADS), bf16),
            jax.ShapeDtypeStruct((width, width), bf16),
        ),
        in_specs=[pl.BlockSpec(memory_space=pltpu.SMEM)] + [pl.BlockSpec(memory_space=pltpu.HBM)] * 2,
        out_specs=tuple(whole(3)),
        scratch_shapes=[
            pltpu.VMEM(densities.shape, bf16),
            pltpu.VMEM(bases.shape, bf16),
            pltpu.SemaphoreType.DMA((2,)),
        ],
        compiler_params=pltpu.CompilerParams(vmem_limit_bytes=VMEM_LIMIT),
        name="moments",
    )(jnp.reshape(core, (1,)), in_hbm(densities), in_hbm(bases))


def unit_kernel(core_ref, own_ref, partner_ref, moments_ref, unit_ref):
    half = pl.ds(pl.multiple_of(core_ref[0] * HALF, HALF), HALF)
    unit_ref[:DENS] = own_ref[...]
    for j in range(3):
        unit_ref[DENS + j * HALF : DENS + (j + 1) * HALF] = jnp.transpose(
            partner_ref[0, j, half, :]
        )
    unit_ref[2 * DENS :] = moments_ref[...]


def make_unit(core, own, partner, moments):
    return pl.pallas_call(
        unit_kernel,
        out_shape=jax.ShapeDtypeStruct((UNIT, LOADS), bf16),
        in_specs=[pl.BlockSpec(memory_space=pltpu.SMEM)] + whole(3),
        out_specs=whole(1)[0],
        compiler_params=pltpu.CompilerParams(vmem_limit_bytes=VMEM_LIMIT),
        name="unit",
    )(jnp.reshape(core, (1,)), own, partner, moments)


def points_kernel(
    here_ref, positions_ref, areas_ref, couplings_ref,
    spread_ref, targets_ref, held_couplings, columns, positions, areas, sems,
):
    first = [fetch(positions_ref, positions, sems.at[0]), fetch(areas_ref, areas, sems.at[1])]
    last = fetch(couplings_ref, held_couplings, sems.at[2])
    z, core, y, x = (here_ref[k] for k in range(4))
    half = lambda whole_row: jnp.where(core == 0, whole_row[:, :HALF], whole_row[:, HALF:])
    back = (0, 3, 1, 2)
    for copy in first:
        copy.wait()
    for t, (step, other) in enumerate(TARGETS):
        cluster = ((step + z) & 3) * 32 + ((other + core) & 1) * 16 + y * SIDE + x
        for i in range(3):
            targets_ref[t, i : i + 1, :] = positions[i, pl.ds(cluster, 1), :]
        targets_ref[t, 3:4, :] = areas[pl.ds(cluster, 1), :]
    for s in range(32):
        first, second = back[(s >> 1) & 3], back[s >> 3]
        on_x = (x + jnp.where(core == 0, first, second)) & 3
        on_y = (y + jnp.where(core == 0, second, first)) & 3
        cluster = z * 32 + ((s + core) & 1) * 16 + on_y * SIDE + on_x
        for i in range(3):
            columns[s, i : i + 1, :] = half(positions[i, pl.ds(cluster, 1), :])
        columns[s, 3:4, :] = half(areas[pl.ds(cluster, 1), :])
    for s in range(32):
        upright = jnp.transpose(columns[s])
        for i in range(4):
            spread_ref[s, i] = jnp.broadcast_to(upright[:, i : i + 1], (HALF, LOADS))
    last.wait()


def make_points(here, positions, areas, couplings):
    return pl.pallas_call(
        points_kernel,
        out_shape=(
            jax.ShapeDtypeStruct((32, 4, HALF, LOADS), f32),
            jax.ShapeDtypeStruct((8, 8, CS), f32),
            jax.ShapeDtypeStruct(couplings.shape, bf16),
        ),
        in_specs=[pl.BlockSpec(memory_space=pltpu.SMEM)] + [pl.BlockSpec(memory_space=pltpu.HBM)] * 3,
        out_specs=tuple(whole(3)),
        scratch_shapes=[
            pltpu.VMEM((32, 8, HALF), f32),
            pltpu.VMEM(positions.shape, f32),
            pltpu.VMEM(areas.shape, f32),
            pltpu.SemaphoreType.DMA((3,)),
        ],
        compiler_params=pltpu.CompilerParams(vmem_limit_bytes=VMEM_LIMIT),
        name="points",
    )(here, in_hbm(positions), in_hbm(areas), in_hbm(couplings))


def blocks_kernel(forward_ref, backward_ref, couplings_ref, flip_ref, blocks_ref):
    cells = 128
    far = couplings_ref.shape[0]

    def summed(cell_ref):
        marks = iota((cells, far), 0) == cell_ref[...]
        return dot32(jnp.where(marks, 1.0, 0.0).astype(bf16), couplings_ref[...])

    total = summed(forward_ref) + dot32(summed(backward_ref).astype(bf16), flip_ref[...])
    for u in range(16):
        unit = total[u * 8 : (u + 1) * 8]
        for g in range(0, 8, 2):
            two = [unit[:, k * 128 : (k + 1) * 128] for k in (g, g + 1)]
            lanes = slice(u * 128, (u + 1) * 128)
            blocks_ref[g * 8 : (g + 2) * 8, lanes] = jnp.concatenate(two, axis=0).astype(bf16)


def make_blocks(forward, backward, couplings, flip):
    return pl.pallas_call(
        blocks_kernel,
        out_shape=jax.ShapeDtypeStruct((64, 16 * 128), bf16),
        in_specs=whole(4),
        out_specs=whole(1)[0],
        compiler_params=pltpu.CompilerParams(vmem_limit_bytes=VMEM_LIMIT),
        name="coupling_blocks",
    )(forward[None, :], backward[None, :], couplings, flip)


def near_kernel(first_unit, buffers, part, counts, targets, spread, *refs):
    units = 2 * buffers
    slots = 2 * units
    held, refs = refs[:buffers], refs[buffers:]
    low, high = SPANS[part]
    sums_far = part in ("first", "middle", "send")
    if sums_far:
        blocks, refs = refs[0], refs[1:]
    if part in ("middle", "send"):
        carried, carried_far, refs = refs[0], refs[1], refs[2:]
    elif part == "keep":
        carried, far, refs = refs[0], refs[1], refs[2:]
    elif part == "own":
        far, refs = refs[0], refs[1:]
    if part == "send":
        send, far, acc, refs = refs[0], refs[1], refs[2], refs[3:]
    elif sums_far:
        acc, far, refs = refs[0], refs[1], refs[2:]
    else:
        acc, refs = refs[0], refs[1:]
    flat, tile_a, tile_b, entry = refs[:4]

    for k in range(buffers):
        flat[k * 2 * UNIT : (k + 1) * 2 * UNIT] = held[k][...]

    def list_target(t, filled):
        for value in [counts[t, 2 * first_unit + s] for s in range(slots)]:
            entry[filled] = value
            filled = filled + jnp.where(value >= 4096, 1, 0)
        entry[filled] = t * 64 + 2 * first_unit
        return filled + (filled & 1)

    entries = lax.fori_loop(low, high, list_target, 0)
    for k in range(6):
        entry[entries + k] = low * 64 + 2 * first_unit
    near_rows = slice(0, 3 * CS)
    if part in ("first", "own"):
        acc[:, near_rows] = jnp.zeros((high - low, 3 * CS, LOADS), f32)
    else:
        acc[:, near_rows] = carried[low:high]

    if sums_far:
        wide = refs[4]
        wide[...] = jnp.zeros(wide.shape, bf16)
        for u in range(units):
            moments = flat[u * UNIT + 2 * DENS : (u + 1) * UNIT, :]
            for k in range(4):
                at = u * 128 + k * RANK
                wide[at : at + RANK, k * LOADS : (k + 1) * LOADS] = moments
        coefficients = dot32(blocks[...], wide[...])
        for k in range(4):
            piece = coefficients[:, k * LOADS : (k + 1) * LOADS]
            far[k] = piece if part == "first" else carried_far[k] + piece

    def coefficients_of(t):
        return jnp.concatenate([far[k, pl.ds(t, 8, stride=8), :] for k in range(4)], axis=0)

    def decode(k):
        both = [entry[2 * k + h] for h in range(2)]
        return (both[0] >> 6) & 7, [v & 63 for v in both], [v >> 12 for v in both]

    def make_tile(k, tile):
        t, slot, pairs = decode(k)
        amount = [p.astype(f32) * kelvin_coef for p in pairs]
        point = targets[t]
        step = 16
        for at in range(0, CS, step):
            side = at // HALF
            rows = slice(at % HALF, at % HALF + step)
            here = [spread[slot[side], i, rows] for i in range(4)]
            for h in range(2):
                lanes = slice(h * HALF, (h + 1) * HALF)
                dx, dy, dz = (here[i] - point[i : i + 1, lanes] for i in range(3))
                inverse = lax.rsqrt(dx * dx + dy * dy + dz * dz + eps_square)
                scaled = (here[3] * (point[3:4, lanes] * amount[side])) * inverse
                cubed = scaled * (inverse * inverse)
                level = lame_ratio * scaled
                ex, ey, ez = dx * cubed, dy * cubed, dz * cubed
                values = (dx * ex + level, dy * ey + level, dz * ez + level, dx * ey, dx * ez, dy * ez)
                for b in range(6):
                    tile[b, at : at + step, lanes] = values[b].astype(bf16)

    def add_products(k, tile):
        t, slot, _ = decode(k)
        f = []
        for j in range(3):
            parts = []
            for h in range(2):
                base = ((slot[h] >> 1) - first_unit) * UNIT + (slot[h] & 1) * DENS + j * HALF
                parts.append(flat[pl.ds(pl.multiple_of(base, 16), HALF), :])
            f.append(jnp.concatenate(parts, axis=1))
        f = jnp.concatenate(f, axis=1)
        order = ((0, 3, 4), (3, 1, 5), (4, 5, 2))
        sums = [
            dot32(f, jnp.concatenate([tile[b] for b in order[i]], axis=0)) for i in range(3)
        ]
        for i in range(3):
            for h in range(2):
                at = (2 * i + h) * HALF
                acc[t - low, at : at + HALF] += sums[i][:, h * HALF : (h + 1) * HALF]

    tasks = entries >> 1

    @pl.when(tasks > 0)
    def _():
        make_tile(0, tile_a)

        def two_tasks(k, carry):
            make_tile(2 * k + 1, tile_b)
            add_products(2 * k, tile_a)

            @pl.when(2 * k + 1 < tasks)
            def _():
                make_tile(2 * k + 2, tile_a)
                add_products(2 * k + 1, tile_b)

            return carry

        lax.fori_loop(0, (tasks + 1) >> 1, two_tasks, 0)

    if part == "send":
        for t in range(low, high):
            send[t - low, : 3 * CS] = acc[t - low].astype(bf16)
            send[t - low, 3 * CS :] = coefficients_of(t).astype(bf16)
    elif not sums_far:
        for t in range(low, high):
            acc[t - low, 3 * CS :] = coefficients_of(t)


def near(part, first_unit, buffers, carried, counts, targets, spread, blocks):
    count = len(buffers)
    slots = 4 * count
    sums = jax.ShapeDtypeStruct((AWAY, 3 * CS, LOADS), f32)
    far = jax.ShapeDtypeStruct((4, 64, LOADS), f32)
    scratch = [
        pltpu.VMEM((count * 2 * UNIT, LOADS), bf16),
        pltpu.VMEM((6, CS, CS), bf16),
        pltpu.VMEM((6, CS, CS), bf16),
        pltpu.SMEM((8 * slots + 16,), jnp.int32),
    ]
    operands = [counts, targets, spread, *buffers]
    low, high = SPANS[part]
    if part in ("keep", "own"):
        shapes = (jax.ShapeDtypeStruct((high - low, FULL, LOADS), f32),)
    else:
        operands.append(blocks[:, first_unit * 128 : (first_unit + 2 * count) * 128])
        scratch.append(pltpu.VMEM((2 * count * 128, 4 * LOADS), bf16))
        shapes = (sums, far)
        if part == "send":
            shapes = (jax.ShapeDtypeStruct((high - low, FULL, LOADS), bf16), far)
            scratch = [pltpu.VMEM((high - low, 3 * CS, LOADS), f32)] + scratch
    operands += carried
    return pl.pallas_call(
        functools.partial(near_kernel, first_unit, count, part),
        out_shape=shapes,
        in_specs=[pl.BlockSpec(memory_space=pltpu.SMEM)] + whole(len(operands) - 1),
        out_specs=tuple(whole(len(shapes))),
        scratch_shapes=scratch,
        compiler_params=pltpu.CompilerParams(vmem_limit_bytes=VMEM_LIMIT),
        cost_estimate=pl.CostEstimate(
            flops=count * 1_000_000_000, bytes_accessed=8_000_000, transcendentals=count * 500_000
        ),
        name=f"near_{part}",
    )(*operands)


def finish_kernel(keep, swapped, one, two, three, bases, out):
    def total(rows):
        return (
            keep[0, rows] + swapped[0, rows].astype(f32) + one[rows].astype(f32)
            + two[rows].astype(f32) + three[rows].astype(f32)
        )

    coefficients = total(slice(3 * CS, FULL))
    high = coefficients.astype(bf16)
    low = (coefficients - high.astype(f32)).astype(bf16)
    both = jnp.concatenate([high, low], axis=0)
    row, held = iota((2 * RANK, 2 * RANK), 0), iota((2 * RANK, 2 * RANK), 1)
    from_row = (row & 32) + ((row & 3) << 3) + ((row & 31) >> 2)
    order = jnp.where(held == from_row, 1.0, 0.0).astype(bf16)
    both = dot32(order, both).astype(bf16)
    for j in range(3):
        basis = bases[0, j]
        twice = jnp.concatenate([basis, basis], axis=0)
        expanded = lax.dot_general(
            twice, both, (((0,), (0,)), ((), ())), preferred_element_type=f32
        )
        for h in range(2):
            at = (2 * j + h) * HALF
            near_part = jnp.transpose(total(slice(at, at + HALF)))
            panels = slice(h * HALF, (h + 1) * HALF)
            out[0, j, panels] = (near_part + expanded[panels]).astype(bf16)


def finish(keep, swapped, others, bases):
    return pl.pallas_call(
        finish_kernel,
        out_shape=jax.ShapeDtypeStruct((1, 3, CS, LOADS), bf16),
        in_specs=whole(6),
        out_specs=whole(1)[0],
        compiler_params=pltpu.CompilerParams(vmem_limit_bytes=VMEM_LIMIT),
        name="sum_and_expand",
    )(keep, swapped, *others, bases)


def local(densities, positions, areas, bases, near_pairs, far_pairs, couplings):
    row = lax.axis_index("row")
    col = lax.axis_index("col")
    z, core = row >> 1, row & 1
    y, x = col >> 2, col & 3
    first_at = jnp.where(core == 0, x, y)
    second_at = jnp.where(core == 0, y, x)

    def unit_of(cluster):
        on_y, on_x = (cluster >> 2) & 3, cluster & 3
        first = (jnp.where(core == 0, on_x, on_y) - first_at) & 3
        second = (jnp.where(core == 0, on_y, on_x) - second_at) & 3
        put = lambda r: jnp.where(r == 0, 0, jnp.where(r == 1, 2, jnp.where(r == 2, 3, 1)))
        return put(second) * SIDE + put(first)

    def other_core(cluster):
        return ((cluster >> 4) + core) & 1

    def slot_of(cluster):
        return jnp.where(cluster >> 5 == z, unit_of(cluster) * 2 + other_core(cluster), -1)

    def target_of(cluster):
        step, other = ((cluster >> 5) - z) & 3, other_core(cluster)
        place = jnp.where(step + other == 0, AWAY, other * 4 + step - 1)
        return jnp.where((cluster & 15) == col, place, -1)

    bases = jnp.transpose(bases, (0, 2, 1, 3))
    positions = jnp.transpose(positions, (1, 0, 2))

    partner = swap_core(densities)
    own, moments, flip = moments_of(core, densities, bases)
    unit = make_unit(core, own, partner, moments)
    from_below = along_first(unit, 1)
    from_above = along_first(unit, -1)
    from_across = along_first(unit, 2)
    here = jnp.stack([z, core, y, x]).astype(jnp.int32)
    here, unit = lax.optimization_barrier((here, unit))
    spread, targets, couplings = make_points(here, positions, areas, couplings)
    (near_pairs, far_pairs, couplings, spread, targets, unit, from_below, from_above, from_across) = (
        lax.optimization_barrier(
            (near_pairs, far_pairs, couplings, spread, targets, unit)
            + (from_below, from_above, from_across)
        )
    )
    low = jnp.concatenate([unit, from_below], axis=0)
    high = jnp.concatenate([from_above, from_across], axis=0)
    low_below = along_second(low, 1)
    high_above = along_second(high, -1)

    heads, tails = near_pairs[:, 0], near_pairs[:, 1]
    mark = lambda index, size: index[None, :] == jnp.arange(size, dtype=jnp.int32)[:, None]
    to_targets = jnp.concatenate(
        [target_of(heads), jnp.where(heads != tails, target_of(tails), -1)]
    )
    from_slots = jnp.concatenate([slot_of(tails), slot_of(heads)])
    counts = lax.dot_general(
        mark(to_targets, 8).astype(bf16),
        mark(from_slots, 32).astype(bf16),
        (((1,), (1,)), ((), ())),
        preferred_element_type=f32,
    ).astype(jnp.int32)
    counts = counts * 4096 + jnp.arange(8, dtype=jnp.int32)[:, None] * 64 + jnp.arange(32, dtype=jnp.int32)

    far_heads, far_tails = far_pairs[:, 0], far_pairs[:, 1]

    def cell(target, source):
        ours = (target_of(target) >= 0) & (slot_of(source) >= 0) & (other_core(source) == 0)
        return jnp.where(ours, unit_of(source) * 8 + target_of(target), -1)

    back_cell = jnp.where(far_heads != far_tails, cell(far_tails, far_heads), -1)
    blocks = make_blocks(cell(far_heads, far_tails), back_cell, couplings, flip)
    blocks, low_later, high_later = lax.optimization_barrier((blocks, low, high))
    high_below = along_second(high_later, 1)
    low_above = along_second(low_later, -1)
    tables = (counts, targets, spread)

    carried = near("first", 0, (low, high), (), *tables, blocks)
    low_below, high_above, carried = lax.optimization_barrier((low_below, high_above, carried))
    low_across = along_second(low_below, 1)
    high_across = along_second(high_above, -1)
    beside = (low_below, high_below, low_above, high_above)
    carried = near("middle", 4, beside, carried, *tables, blocks)
    across = (low_across, high_across)
    send, far = near("send", 12, across, carried, *tables, blocks)
    swapped = swap_core(send)
    (keep,) = near("keep", 12, across, (carried[0], far), *tables, blocks)
    both = [(keep[k] + swapped[k + 1].astype(f32)).astype(bf16) for k in range(3)]
    both, far = lax.optimization_barrier((both, far))
    others = [along_z(both[k], k + 1) for k in range(3)]
    everything = (low, high) + beside + across
    (own,) = near("own", 0, everything, (far,), *tables, blocks)
    return finish(own, swapped, others, bases)


def solution(mesh):
    return jax.shard_map(
        local,
        mesh=mesh,
        in_specs=(
            P(("row", "col"), None, None, None),
            P(),
            P(),
            P(("row", "col"), None, None, None),
            P(),
            P(),
            P(),
        ),
        out_specs=P(("row", "col"), None, None, None),
        check_vma=False,
    )
```

```python
import functools

import jax
import jax.numpy as jnp
from jax import lax
from jax.experimental import pallas as pl
from jax.experimental.pallas import tpu as pltpu
from jax.sharding import PartitionSpec as P


CS = 256
LOADS = 128
RANK = 32
HALF = CS // 2
DENS = 3 * HALF
UNIT = 2 * DENS + RANK
FULL = 3 * CS + RANK
AXES = ("row", "col")
TARGETS = ((1, 0), (2, 0), (3, 0), (1, 1), (2, 1), (3, 1), (0, 0), (0, 1))
AWAY = 6
SPANS = {"first": (0, AWAY), "middle": (0, AWAY), "send": (3, AWAY), "keep": (0, 3), "own": (AWAY, 8)}
SIDE = 4

eps_square = 0.0004
lame_ratio = 1.8
kelvin_coef = 1.0 / (16.0 * 3.141592653589793 * 0.7)
VMEM_LIMIT = 16 * 1024 * 1024
bf16 = jnp.bfloat16
f32 = jnp.float32


def routes(move):
    pairs = []
    for z in range(SIDE):
        for core in range(2):
            for y in range(SIDE):
                for x in range(SIDE):
                    to_z, to_core, to_y, to_x = move(z, core, y, x)
                    source = (z * 2 + core) * 16 + y * SIDE + x
                    target = ((to_z % SIDE) * 2 + to_core) * 16 + (to_y % SIDE) * SIDE + to_x % SIDE
                    pairs.append((source, target))
    return pairs


def swap_core(value):
    return lax.ppermute(value, AXES, routes(lambda z, c, y, x: (z, 1 - c, y, x)))


def along_first(value, step):
    move = lambda z, c, y, x: (z, c, y, x + step) if c == 0 else (z, c, y + step, x)
    return lax.ppermute(value, AXES, routes(move))


def along_second(value, step):
    move = lambda z, c, y, x: (z, c, y + step, x) if c == 0 else (z, c, y, x + step)
    return lax.ppermute(value, AXES, routes(move))


def along_z(value, step):
    return lax.ppermute(value, AXES, routes(lambda z, c, y, x: (z + step, c, y, x)))


def whole(count):
    return [pl.BlockSpec(memory_space=pltpu.VMEM)] * count


def dot32(a, b):
    return jnp.dot(a, b, preferred_element_type=f32)


def iota(shape, dim):
    return lax.broadcasted_iota(jnp.int32, shape, dim)


def fetch(source, target, sem):
    copy = pltpu.make_async_copy(source, target, sem)
    copy.start()
    return copy


def moments_kernel(core_ref, dens_ref, bases_ref, own_ref, moments_ref, flip_ref, dens, bases, sems):
    copies = [fetch(dens_ref, dens, sems.at[0]), fetch(bases_ref, bases, sems.at[1])]
    width = RANK * RANK
    step = 128
    for at in range(0, width, step):
        source, target = iota((step, width), 0) + at, iota((step, width), 1)
        turned = ((target & (RANK - 1)) << 5) + (target >> 5)
        flip_ref[at : at + step] = jnp.where(source == turned, 1.0, 0.0).astype(bf16)
    half = pl.ds(pl.multiple_of(core_ref[0] * HALF, HALF), HALF)
    total = jnp.zeros((RANK, LOADS), f32)
    for copy in copies:
        copy.wait()
    for j in range(3):
        total += dot32(bases[0, j], dens[0, j])
        own_ref[j * HALF : (j + 1) * HALF] = jnp.transpose(dens[0, j, half, :])
    moments_ref[...] = total.astype(bf16)


def in_hbm(array):
    return pltpu.with_memory_space_constraint(array, pltpu.HBM)


def moments_of(core, densities, bases):
    width = RANK * RANK
    return pl.pallas_call(
        moments_kernel,
        out_shape=(
            jax.ShapeDtypeStruct((DENS, LOADS), bf16),
            jax.ShapeDtypeStruct((RANK, LOADS), bf16),
            jax.ShapeDtypeStruct((width, width), bf16),
        ),
        in_specs=[pl.BlockSpec(memory_space=pltpu.SMEM)] + [pl.BlockSpec(memory_space=pltpu.HBM)] * 2,
        out_specs=tuple(whole(3)),
        scratch_shapes=[
            pltpu.VMEM(densities.shape, bf16),
            pltpu.VMEM(bases.shape, bf16),
            pltpu.SemaphoreType.DMA((2,)),
        ],
        compiler_params=pltpu.CompilerParams(vmem_limit_bytes=VMEM_LIMIT),
        name="moments",
    )(jnp.reshape(core, (1,)), in_hbm(densities), in_hbm(bases))


def unit_kernel(core_ref, own_ref, partner_ref, moments_ref, unit_ref):
    half = pl.ds(pl.multiple_of(core_ref[0] * HALF, HALF), HALF)
    unit_ref[:DENS] = own_ref[...]
    for j in range(3):
        unit_ref[DENS + j * HALF : DENS + (j + 1) * HALF] = jnp.transpose(
            partner_ref[0, j, half, :]
        )
    unit_ref[2 * DENS :] = moments_ref[...]


def make_unit(core, own, partner, moments):
    return pl.pallas_call(
        unit_kernel,
        out_shape=jax.ShapeDtypeStruct((UNIT, LOADS), bf16),
        in_specs=[pl.BlockSpec(memory_space=pltpu.SMEM)] + whole(3),
        out_specs=whole(1)[0],
        compiler_params=pltpu.CompilerParams(vmem_limit_bytes=VMEM_LIMIT),
        name="unit",
    )(jnp.reshape(core, (1,)), own, partner, moments)


def points_kernel(
    here_ref, positions_ref, areas_ref, couplings_ref,
    spread_ref, targets_ref, held_couplings, columns, positions, areas, sems,
):
    first = [fetch(positions_ref, positions, sems.at[0]), fetch(areas_ref, areas, sems.at[1])]
    last = fetch(couplings_ref, held_couplings, sems.at[2])
    z, core, y, x = (here_ref[k] for k in range(4))
    half = lambda whole_row: jnp.where(core == 0, whole_row[:, :HALF], whole_row[:, HALF:])
    back = (0, 3, 1, 2)
    for copy in first:
        copy.wait()
    for t, (step, other) in enumerate(TARGETS):
        cluster = ((step + z) & 3) * 32 + ((other + core) & 1) * 16 + y * SIDE + x
        for i in range(3):
            targets_ref[t, i : i + 1, :] = positions[i, pl.ds(cluster, 1), :]
        targets_ref[t, 3:4, :] = areas[pl.ds(cluster, 1), :]
    for s in range(32):
        first, second = back[(s >> 1) & 3], back[s >> 3]
        on_x = (x + jnp.where(core == 0, first, second)) & 3
        on_y = (y + jnp.where(core == 0, second, first)) & 3
        cluster = z * 32 + ((s + core) & 1) * 16 + on_y * SIDE + on_x
        for i in range(3):
            columns[s, i : i + 1, :] = half(positions[i, pl.ds(cluster, 1), :])
        columns[s, 3:4, :] = half(areas[pl.ds(cluster, 1), :])
    for s in range(32):
        upright = jnp.transpose(columns[s])
        for i in range(4):
            spread_ref[s, i] = jnp.broadcast_to(upright[:, i : i + 1], (HALF, LOADS))
    last.wait()


def make_points(here, positions, areas, couplings):
    return pl.pallas_call(
        points_kernel,
        out_shape=(
            jax.ShapeDtypeStruct((32, 4, HALF, LOADS), f32),
            jax.ShapeDtypeStruct((8, 8, CS), f32),
            jax.ShapeDtypeStruct(couplings.shape, bf16),
        ),
        in_specs=[pl.BlockSpec(memory_space=pltpu.SMEM)] + [pl.BlockSpec(memory_space=pltpu.HBM)] * 3,
        out_specs=tuple(whole(3)),
        scratch_shapes=[
            pltpu.VMEM((32, 8, HALF), f32),
            pltpu.VMEM(positions.shape, f32),
            pltpu.VMEM(areas.shape, f32),
            pltpu.SemaphoreType.DMA((3,)),
        ],
        compiler_params=pltpu.CompilerParams(vmem_limit_bytes=VMEM_LIMIT),
        name="points",
    )(here, in_hbm(positions), in_hbm(areas), in_hbm(couplings))


def blocks_kernel(forward_ref, backward_ref, couplings_ref, flip_ref, blocks_ref):
    cells = 128
    far = couplings_ref.shape[0]

    def summed(cell_ref):
        marks = iota((cells, far), 0) == cell_ref[...]
        return dot32(jnp.where(marks, 1.0, 0.0).astype(bf16), couplings_ref[...])

    total = summed(forward_ref) + dot32(summed(backward_ref).astype(bf16), flip_ref[...])
    for u in range(16):
        unit = total[u * 8 : (u + 1) * 8]
        for g in range(0, 8, 2):
            two = [unit[:, k * 128 : (k + 1) * 128] for k in (g, g + 1)]
            lanes = slice(u * 128, (u + 1) * 128)
            blocks_ref[g * 8 : (g + 2) * 8, lanes] = jnp.concatenate(two, axis=0).astype(bf16)


def make_blocks(forward, backward, couplings, flip):
    return pl.pallas_call(
        blocks_kernel,
        out_shape=jax.ShapeDtypeStruct((64, 16 * 128), bf16),
        in_specs=whole(4),
        out_specs=whole(1)[0],
        compiler_params=pltpu.CompilerParams(vmem_limit_bytes=VMEM_LIMIT),
        name="coupling_blocks",
    )(forward[None, :], backward[None, :], couplings, flip)


def near_kernel(first_unit, buffers, part, counts, targets, spread, *refs):
    units = 2 * buffers
    slots = 2 * units
    held, refs = refs[:buffers], refs[buffers:]
    low, high = SPANS[part]
    sums_far = part in ("first", "middle", "send")
    if sums_far:
        blocks, refs = refs[0], refs[1:]
    if part in ("middle", "send"):
        carried, carried_far, refs = refs[0], refs[1], refs[2:]
    elif part == "keep":
        carried, far, refs = refs[0], refs[1], refs[2:]
    elif part == "own":
        far, refs = refs[0], refs[1:]
    if part == "send":
        send, far, acc, refs = refs[0], refs[1], refs[2], refs[3:]
    elif sums_far:
        acc, far, refs = refs[0], refs[1], refs[2:]
    elif part == "keep":
        acc, refs = refs[0], refs[1:]
    else:
        acc, pair, refs = refs[0], refs[1], refs[2:]
    flat, tile_a, tile_b, entry = refs[:4]

    for k in range(buffers):
        flat[k * 2 * UNIT : (k + 1) * 2 * UNIT] = held[k][...]

    def list_target(t, filled):
        for value in [counts[t, 2 * first_unit + s] for s in range(slots)]:
            entry[filled] = value
            filled = filled + jnp.where(value >= 4096, 1, 0)
        entry[filled] = t * 64 + 2 * first_unit
        return filled + (filled & 1)

    entries = lax.fori_loop(low, high, list_target, 0)
    for k in range(6):
        entry[entries + k] = low * 64 + 2 * first_unit
    near_rows = slice(0, 3 * CS)
    if part in ("first", "own"):
        acc[:, near_rows] = jnp.zeros((high - low, 3 * CS, LOADS), f32)
    else:
        acc[:, near_rows] = carried[low:high]

    if sums_far:
        wide = refs[4]
        wide[...] = jnp.zeros(wide.shape, bf16)
        for u in range(units):
            moments = flat[u * UNIT + 2 * DENS : (u + 1) * UNIT, :]
            for k in range(4):
                at = u * 128 + k * RANK
                wide[at : at + RANK, k * LOADS : (k + 1) * LOADS] = moments
        coefficients = dot32(blocks[...], wide[...])
        for k in range(4):
            piece = coefficients[:, k * LOADS : (k + 1) * LOADS]
            far[k] = piece if part == "first" else carried_far[k] + piece

    def coefficients_of(t):
        return jnp.concatenate([far[k, pl.ds(t, 8, stride=8), :] for k in range(4)], axis=0)

    def decode(k):
        both = [entry[2 * k + h] for h in range(2)]
        return (both[0] >> 6) & 7, [v & 63 for v in both], [v >> 12 for v in both]

    def make_tile(k, tile):
        t, slot, pairs = decode(k)
        amount = [p.astype(f32) * kelvin_coef for p in pairs]
        point = targets[t]
        step = 16
        for at in range(0, CS, step):
            side = at // HALF
            rows = slice(at % HALF, at % HALF + step)
            here = [spread[slot[side], i, rows] for i in range(4)]
            for h in range(2):
                lanes = slice(h * HALF, (h + 1) * HALF)
                dx, dy, dz = (here[i] - point[i : i + 1, lanes] for i in range(3))
                inverse = lax.rsqrt(dx * dx + dy * dy + dz * dz + eps_square)
                scaled = (here[3] * (point[3:4, lanes] * amount[side])) * inverse
                cubed = scaled * (inverse * inverse)
                level = lame_ratio * scaled
                ex, ey, ez = dx * cubed, dy * cubed, dz * cubed
                values = (dx * ex + level, dy * ey + level, dz * ez + level, dx * ey, dx * ez, dy * ez)
                for b in range(6):
                    tile[b, at : at + step, lanes] = values[b].astype(bf16)

    def add_products(k, tile):
        t, slot, _ = decode(k)
        f = []
        for j in range(3):
            parts = []
            for h in range(2):
                base = ((slot[h] >> 1) - first_unit) * UNIT + (slot[h] & 1) * DENS + j * HALF
                parts.append(flat[pl.ds(pl.multiple_of(base, 16), HALF), :])
            f.append(jnp.concatenate(parts, axis=1))
        f = jnp.concatenate(f, axis=1)
        order = ((0, 3, 4), (3, 1, 5), (4, 5, 2))
        sums = [
            dot32(f, jnp.concatenate([tile[b] for b in order[i]], axis=0)) for i in range(3)
        ]
        for i in range(3):
            for h in range(2):
                at = (2 * i + h) * HALF
                acc[t - low, at : at + HALF] += sums[i][:, h * HALF : (h + 1) * HALF]

    tasks = entries >> 1

    @pl.when(tasks > 0)
    def _():
        make_tile(0, tile_a)

        def two_tasks(k, carry):
            make_tile(2 * k + 1, tile_b)
            add_products(2 * k, tile_a)

            @pl.when(2 * k + 1 < tasks)
            def _():
                make_tile(2 * k + 2, tile_a)
                add_products(2 * k + 1, tile_b)

            return carry

        lax.fori_loop(0, (tasks + 1) >> 1, two_tasks, 0)

    if part == "send":
        for t in range(low, high):
            send[t - low, : 3 * CS] = acc[t - low].astype(bf16)
            send[t - low, 3 * CS :] = coefficients_of(t).astype(bf16)
    elif not sums_far:
        for t in range(low, high):
            acc[t - low, 3 * CS :] = coefficients_of(t)
    if part == "own":
        for k in range(2):
            pair[k] = acc[1].astype(bf16)


def near(part, first_unit, buffers, carried, counts, targets, spread, blocks):
    count = len(buffers)
    slots = 4 * count
    sums = jax.ShapeDtypeStruct((AWAY, 3 * CS, LOADS), f32)
    far = jax.ShapeDtypeStruct((4, 64, LOADS), f32)
    scratch = [
        pltpu.VMEM((count * 2 * UNIT, LOADS), bf16),
        pltpu.VMEM((6, CS, CS), bf16),
        pltpu.VMEM((6, CS, CS), bf16),
        pltpu.SMEM((8 * slots + 16,), jnp.int32),
    ]
    operands = [counts, targets, spread, *buffers]
    low, high = SPANS[part]
    if part in ("keep", "own"):
        shapes = (jax.ShapeDtypeStruct((high - low, FULL, LOADS), f32),)
        if part == "own":
            shapes += (jax.ShapeDtypeStruct((2, FULL, LOADS), bf16),)
    else:
        operands.append(blocks[:, first_unit * 128 : (first_unit + 2 * count) * 128])
        scratch.append(pltpu.VMEM((2 * count * 128, 4 * LOADS), bf16))
        shapes = (sums, far)
        if part == "send":
            shapes = (jax.ShapeDtypeStruct((high - low, FULL, LOADS), bf16), far)
            scratch = [pltpu.VMEM((high - low, 3 * CS, LOADS), f32)] + scratch
    operands += carried
    return pl.pallas_call(
        functools.partial(near_kernel, first_unit, count, part),
        out_shape=shapes,
        in_specs=[pl.BlockSpec(memory_space=pltpu.SMEM)] + whole(len(operands) - 1),
        out_specs=tuple(whole(len(shapes))),
        scratch_shapes=scratch,
        compiler_params=pltpu.CompilerParams(vmem_limit_bytes=VMEM_LIMIT),
        cost_estimate=pl.CostEstimate(
            flops=count * 1_000_000_000, bytes_accessed=8_000_000, transcendentals=count * 500_000
        ),
        name=f"near_{part}",
    )(*operands)


def finish_kernel(core, keep, swapped, one, two, three, bases, out):
    def total(rows):
        return (
            keep[0, rows] + swapped[1 - core[0], rows].astype(f32) + one[rows].astype(f32)
            + two[rows].astype(f32) + three[rows].astype(f32)
        )

    coefficients = total(slice(3 * CS, FULL))
    high = coefficients.astype(bf16)
    low = (coefficients - high.astype(f32)).astype(bf16)
    both = jnp.concatenate([high, low], axis=0)
    row, held = iota((2 * RANK, 2 * RANK), 0), iota((2 * RANK, 2 * RANK), 1)
    from_row = (row & 32) + ((row & 3) << 3) + ((row & 31) >> 2)
    order = jnp.where(held == from_row, 1.0, 0.0).astype(bf16)
    both = dot32(order, both).astype(bf16)
    for j in range(3):
        basis = bases[0, j]
        twice = jnp.concatenate([basis, basis], axis=0)
        expanded = lax.dot_general(
            twice, both, (((0,), (0,)), ((), ())), preferred_element_type=f32
        )
        for h in range(2):
            at = (2 * j + h) * HALF
            near_part = jnp.transpose(total(slice(at, at + HALF)))
            panels = slice(h * HALF, (h + 1) * HALF)
            out[0, j, panels] = (near_part + expanded[panels]).astype(bf16)


def finish(core, keep, swapped, others, bases):
    return pl.pallas_call(
        finish_kernel,
        out_shape=jax.ShapeDtypeStruct((1, 3, CS, LOADS), bf16),
        in_specs=[pl.BlockSpec(memory_space=pltpu.SMEM)] + whole(6),
        out_specs=whole(1)[0],
        compiler_params=pltpu.CompilerParams(vmem_limit_bytes=VMEM_LIMIT),
        name="sum_and_expand",
    )(jnp.reshape(core, (1,)), keep, swapped, *others, bases)


def local(densities, positions, areas, bases, near_pairs, far_pairs, couplings):
    row = lax.axis_index("row")
    col = lax.axis_index("col")
    z, core = row >> 1, row & 1
    y, x = col >> 2, col & 3
    first_at = jnp.where(core == 0, x, y)
    second_at = jnp.where(core == 0, y, x)

    def unit_of(cluster):
        on_y, on_x = (cluster >> 2) & 3, cluster & 3
        first = (jnp.where(core == 0, on_x, on_y) - first_at) & 3
        second = (jnp.where(core == 0, on_y, on_x) - second_at) & 3
        put = lambda r: jnp.where(r == 0, 0, jnp.where(r == 1, 2, jnp.where(r == 2, 3, 1)))
        return put(second) * SIDE + put(first)

    def other_core(cluster):
        return ((cluster >> 4) + core) & 1

    def slot_of(cluster):
        return jnp.where(cluster >> 5 == z, unit_of(cluster) * 2 + other_core(cluster), -1)

    def target_of(cluster):
        step, other = ((cluster >> 5) - z) & 3, other_core(cluster)
        place = jnp.where(step == 0, AWAY + other, other * 3 + step - 1)
        return jnp.where((cluster & 15) == col, place, -1)

    bases = jnp.transpose(bases, (0, 2, 1, 3))
    positions = jnp.transpose(positions, (1, 0, 2))

    partner = swap_core(densities)
    own, moments, flip = moments_of(core, densities, bases)
    unit = make_unit(core, own, partner, moments)
    from_below = along_first(unit, 1)
    from_above = along_first(unit, -1)
    from_across = along_first(unit, 2)
    here = jnp.stack([z, core, y, x]).astype(jnp.int32)
    here, unit = lax.optimization_barrier((here, unit))
    spread, targets, couplings = make_points(here, positions, areas, couplings)
    (near_pairs, far_pairs, couplings, spread, targets, unit, from_below, from_above, from_across) = (
        lax.optimization_barrier(
            (near_pairs, far_pairs, couplings, spread, targets, unit)
            + (from_below, from_above, from_across)
        )
    )
    low = jnp.concatenate([unit, from_below], axis=0)
    high = jnp.concatenate([from_above, from_across], axis=0)
    low_below = along_second(low, 1)
    high_above = along_second(high, -1)

    heads, tails = near_pairs[:, 0], near_pairs[:, 1]
    mark = lambda index, size: index[None, :] == jnp.arange(size, dtype=jnp.int32)[:, None]
    to_targets = jnp.concatenate(
        [target_of(heads), jnp.where(heads != tails, target_of(tails), -1)]
    )
    from_slots = jnp.concatenate([slot_of(tails), slot_of(heads)])
    counts = lax.dot_general(
        mark(to_targets, 8).astype(bf16),
        mark(from_slots, 32).astype(bf16),
        (((1,), (1,)), ((), ())),
        preferred_element_type=f32,
    ).astype(jnp.int32)
    counts = counts * 4096 + jnp.arange(8, dtype=jnp.int32)[:, None] * 64 + jnp.arange(32, dtype=jnp.int32)

    far_heads, far_tails = far_pairs[:, 0], far_pairs[:, 1]

    def cell(target, source):
        ours = (target_of(target) >= 0) & (slot_of(source) >= 0) & (other_core(source) == 0)
        return jnp.where(ours, unit_of(source) * 8 + target_of(target), -1)

    back_cell = jnp.where(far_heads != far_tails, cell(far_tails, far_heads), -1)
    blocks = make_blocks(cell(far_heads, far_tails), back_cell, couplings, flip)
    blocks, low_later, high_later = lax.optimization_barrier((blocks, low, high))
    high_below = along_second(high_later, 1)
    low_above = along_second(low_later, -1)
    tables = (counts, targets, spread)

    carried = near("first", 0, (low, high), (), *tables, blocks)
    low_below, high_above, carried = lax.optimization_barrier((low_below, high_above, carried))
    low_across = along_second(low_below, 1)
    high_across = along_second(high_above, -1)
    beside = (low_below, high_below, low_above, high_above)
    carried = near("middle", 4, beside, carried, *tables, blocks)
    across = (low_across, high_across)
    send, far = near("send", 12, across, carried, *tables, blocks)
    swapped = swap_core(send)
    (keep,) = near("keep", 12, across, (carried[0], far), *tables, blocks)
    both = [(keep[k] + swapped[k].astype(f32)).astype(bf16) for k in range(3)]
    both, far = lax.optimization_barrier((both, far))
    others = [along_z(both[0], 1), along_z(both[2], 3)]
    others.append(along_z(both[1], 2))
    everything = (low, high) + beside + across
    own, pair = near("own", 0, everything, (far,), *tables, blocks)
    chips = [[2 * k, 2 * k + 1] for k in range(SIDE)]
    swapped = lax.all_to_all(pair, "row", 0, 0, axis_index_groups=chips, tiled=True)
    return finish(core, own, swapped, others, bases)


def solution(mesh):
    return jax.shard_map(
        local,
        mesh=mesh,
        in_specs=(
            P(("row", "col"), None, None, None),
            P(),
            P(),
            P(("row", "col"), None, None, None),
            P(),
            P(),
            P(),
        ),
        out_specs=P(("row", "col"), None, None, None),
        check_vma=False,
    )
```

```python
import functools

import jax
import jax.numpy as jnp
from jax import lax
from jax.experimental import pallas as pl
from jax.experimental.pallas import tpu as pltpu
from jax.sharding import PartitionSpec as P


CS = 256
LOADS = 128
RANK = 32
HALF = CS // 2
DENS = 3 * HALF
UNIT = 2 * DENS + RANK
FULL = 3 * CS + RANK
AXES = ("row", "col")
TARGETS = ((1, 0), (2, 0), (3, 0), (1, 1), (2, 1), (3, 1), (0, 0), (0, 1))
AWAY = 6
LINE, OUTER, INNER = 0, 5, 2
SPANS = {"first": (0, 8), "middle": (0, AWAY), "send": (3, AWAY), "keep": (0, 3), "own": (AWAY, 8)}
SIDE = 4

eps_square = 0.0004
lame_ratio = 1.8
kelvin_coef = 1.0 / (16.0 * 3.141592653589793 * 0.7)
VMEM_LIMIT = 16 * 1024 * 1024
bf16 = jnp.bfloat16
f32 = jnp.float32


def routes(move):
    pairs = []
    for z in range(SIDE):
        for core in range(2):
            for y in range(SIDE):
                for x in range(SIDE):
                    to_z, to_core, to_y, to_x = move(z, core, y, x)
                    source = (z * 2 + core) * 16 + y * SIDE + x
                    target = ((to_z % SIDE) * 2 + to_core) * 16 + (to_y % SIDE) * SIDE + to_x % SIDE
                    pairs.append((source, target))
    return pairs


def swap_core(value):
    return lax.ppermute(value, AXES, routes(lambda z, c, y, x: (z, 1 - c, y, x)))


def along_first(value, step):
    move = lambda z, c, y, x: (z, c, y + step, x) if c == 0 else (z + step, c, y, x)
    return lax.ppermute(value, AXES, routes(move))


def along_second(value, step):
    move = lambda z, c, y, x: (z + step, c, y, x) if c == 0 else (z, c, y + step, x)
    return lax.ppermute(value, AXES, routes(move))


def along_line(value, step):
    return lax.ppermute(value, AXES, routes(lambda z, c, y, x: (z, c, y, x + step)))


def whole(count):
    return [pl.BlockSpec(memory_space=pltpu.VMEM)] * count


def dot32(a, b):
    return jnp.dot(a, b, preferred_element_type=f32)


def iota(shape, dim):
    return lax.broadcasted_iota(jnp.int32, shape, dim)


def fetch(source, target, sem):
    copy = pltpu.make_async_copy(source, target, sem)
    copy.start()
    return copy


def moments_kernel(core_ref, dens_ref, bases_ref, own_ref, moments_ref, flip_ref, dens, bases, sems):
    copies = [fetch(dens_ref, dens, sems.at[0]), fetch(bases_ref, bases, sems.at[1])]
    width = RANK * RANK
    step = 128
    for at in range(0, width, step):
        source, target = iota((step, width), 0) + at, iota((step, width), 1)
        turned = ((target & (RANK - 1)) << 5) + (target >> 5)
        flip_ref[at : at + step] = jnp.where(source == turned, 1.0, 0.0).astype(bf16)
    half = pl.ds(pl.multiple_of(core_ref[0] * HALF, HALF), HALF)
    total = jnp.zeros((RANK, LOADS), f32)
    for copy in copies:
        copy.wait()
    for j in range(3):
        total += dot32(bases[0, j], dens[0, j])
        own_ref[j * HALF : (j + 1) * HALF] = jnp.transpose(dens[0, j, half, :])
    moments_ref[...] = total.astype(bf16)


def in_hbm(array):
    return pltpu.with_memory_space_constraint(array, pltpu.HBM)


def moments_of(core, densities, bases):
    width = RANK * RANK
    return pl.pallas_call(
        moments_kernel,
        out_shape=(
            jax.ShapeDtypeStruct((DENS, LOADS), bf16),
            jax.ShapeDtypeStruct((RANK, LOADS), bf16),
            jax.ShapeDtypeStruct((width, width), bf16),
        ),
        in_specs=[pl.BlockSpec(memory_space=pltpu.SMEM)] + [pl.BlockSpec(memory_space=pltpu.HBM)] * 2,
        out_specs=tuple(whole(3)),
        scratch_shapes=[
            pltpu.VMEM(densities.shape, bf16),
            pltpu.VMEM(bases.shape, bf16),
            pltpu.SemaphoreType.DMA((2,)),
        ],
        compiler_params=pltpu.CompilerParams(vmem_limit_bytes=VMEM_LIMIT),
        name="moments",
    )(jnp.reshape(core, (1,)), in_hbm(densities), in_hbm(bases))


def unit_kernel(core_ref, own_ref, partner_ref, moments_ref, unit_ref):
    half = pl.ds(pl.multiple_of(core_ref[0] * HALF, HALF), HALF)
    unit_ref[:DENS] = own_ref[...]
    for j in range(3):
        unit_ref[DENS + j * HALF : DENS + (j + 1) * HALF] = jnp.transpose(
            partner_ref[0, j, half, :]
        )
    unit_ref[2 * DENS :] = moments_ref[...]


def make_unit(core, own, partner, moments):
    return pl.pallas_call(
        unit_kernel,
        out_shape=jax.ShapeDtypeStruct((UNIT, LOADS), bf16),
        in_specs=[pl.BlockSpec(memory_space=pltpu.SMEM)] + whole(3),
        out_specs=whole(1)[0],
        compiler_params=pltpu.CompilerParams(vmem_limit_bytes=VMEM_LIMIT),
        name="unit",
    )(jnp.reshape(core, (1,)), own, partner, moments)


def points_kernel(
    here_ref, positions_ref, areas_ref, couplings_ref,
    spread_ref, targets_ref, held_couplings, columns, positions, areas, sems,
):
    first = [fetch(positions_ref, positions, sems.at[0]), fetch(areas_ref, areas, sems.at[1])]
    last = fetch(couplings_ref, held_couplings, sems.at[2])
    z, core, y, x = (here_ref[k] for k in range(4))
    half = lambda whole_row: jnp.where(core == 0, whole_row[:, :HALF], whole_row[:, HALF:])
    back = (0, 3, 1, 2)
    for copy in first:
        copy.wait()
    for t, (step, other) in enumerate(TARGETS):
        cluster = (((step + z) & 3) << LINE) + ((other + core) & 1) * 16 + (y << OUTER) + (x << INNER)
        for i in range(3):
            targets_ref[t, i : i + 1, :] = positions[i, pl.ds(cluster, 1), :]
        targets_ref[t, 3:4, :] = areas[pl.ds(cluster, 1), :]
    for s in range(32):
        first, second = back[(s >> 1) & 3], back[s >> 3]
        on_x = (x + jnp.where(core == 0, first, second)) & 3
        on_y = (y + jnp.where(core == 0, second, first)) & 3
        cluster = (z << LINE) + ((s + core) & 1) * 16 + (on_y << OUTER) + (on_x << INNER)
        for i in range(3):
            columns[s, i : i + 1, :] = half(positions[i, pl.ds(cluster, 1), :])
        columns[s, 3:4, :] = half(areas[pl.ds(cluster, 1), :])
    for s in range(32):
        upright = jnp.transpose(columns[s])
        for i in range(4):
            spread_ref[s, i] = jnp.broadcast_to(upright[:, i : i + 1], (HALF, LOADS))
    last.wait()


def make_points(here, positions, areas, couplings):
    return pl.pallas_call(
        points_kernel,
        out_shape=(
            jax.ShapeDtypeStruct((32, 4, HALF, LOADS), f32),
            jax.ShapeDtypeStruct((8, 8, CS), f32),
            jax.ShapeDtypeStruct(couplings.shape, bf16),
        ),
        in_specs=[pl.BlockSpec(memory_space=pltpu.SMEM)] + [pl.BlockSpec(memory_space=pltpu.HBM)] * 3,
        out_specs=tuple(whole(3)),
        scratch_shapes=[
            pltpu.VMEM((32, 8, HALF), f32),
            pltpu.VMEM(positions.shape, f32),
            pltpu.VMEM(areas.shape, f32),
            pltpu.SemaphoreType.DMA((3,)),
        ],
        compiler_params=pltpu.CompilerParams(vmem_limit_bytes=VMEM_LIMIT),
        name="points",
    )(here, in_hbm(positions), in_hbm(areas), in_hbm(couplings))


def blocks_kernel(forward_ref, backward_ref, couplings_ref, flip_ref, blocks_ref):
    cells = 128
    far = couplings_ref.shape[0]

    def summed(cell_ref):
        marks = iota((cells, far), 0) == cell_ref[...]
        return dot32(jnp.where(marks, 1.0, 0.0).astype(bf16), couplings_ref[...])

    total = summed(forward_ref) + dot32(summed(backward_ref).astype(bf16), flip_ref[...])
    for u in range(16):
        unit = total[u * 8 : (u + 1) * 8]
        for g in range(0, 8, 2):
            two = [unit[:, k * 128 : (k + 1) * 128] for k in (g, g + 1)]
            lanes = slice(u * 128, (u + 1) * 128)
            blocks_ref[g * 8 : (g + 2) * 8, lanes] = jnp.concatenate(two, axis=0).astype(bf16)


def make_blocks(forward, backward, couplings, flip):
    return pl.pallas_call(
        blocks_kernel,
        out_shape=jax.ShapeDtypeStruct((64, 16 * 128), bf16),
        in_specs=whole(4),
        out_specs=whole(1)[0],
        compiler_params=pltpu.CompilerParams(vmem_limit_bytes=VMEM_LIMIT),
        name="coupling_blocks",
    )(forward[None, :], backward[None, :], couplings, flip)


def near_kernel(first_unit, buffers, part, counts, targets, spread, *refs):
    units = 2 * buffers
    slots = 2 * units
    held, refs = refs[:buffers], refs[buffers:]
    low, high = SPANS[part]
    sums_far = part in ("first", "middle", "send")
    if sums_far:
        blocks, refs = refs[0], refs[1:]
    if part in ("middle", "send"):
        carried, carried_far, refs = refs[0], refs[1], refs[2:]
    elif part == "keep":
        carried, far, refs = refs[0], refs[1], refs[2:]
    elif part == "own":
        carried, far, refs = refs[0], refs[1], refs[2:]
    if part == "send":
        send, far, acc, refs = refs[0], refs[1], refs[2], refs[3:]
    elif sums_far:
        acc, far, refs = refs[0], refs[1], refs[2:]
    elif part == "keep":
        acc, refs = refs[0], refs[1:]
    else:
        acc, pair, refs = refs[0], refs[1], refs[2:]
    flat, tile_a, tile_b, entry = refs[:4]

    for k in range(buffers):
        flat[k * 2 * UNIT : (k + 1) * 2 * UNIT] = held[k][...]

    def list_target(t, filled):
        for value in [counts[t, 2 * first_unit + s] for s in range(slots)]:
            entry[filled] = value
            filled = filled + jnp.where(value >= 4096, 1, 0)
        entry[filled] = t * 64 + 2 * first_unit
        return filled + (filled & 1)

    entries = lax.fori_loop(low, high, list_target, 0)
    for k in range(6):
        entry[entries + k] = low * 64 + 2 * first_unit
    near_rows = slice(0, 3 * CS)
    if part == "first":
        acc[:, near_rows] = jnp.zeros((high - low, 3 * CS, LOADS), f32)
    else:
        acc[:, near_rows] = carried[low:high]

    if sums_far:
        wide = refs[4]
        wide[...] = jnp.zeros(wide.shape, bf16)
        for u in range(units):
            moments = flat[u * UNIT + 2 * DENS : (u + 1) * UNIT, :]
            for k in range(4):
                at = u * 128 + k * RANK
                wide[at : at + RANK, k * LOADS : (k + 1) * LOADS] = moments
        coefficients = dot32(
            blocks[:, first_unit * 128 : (first_unit + units) * 128], wide[...]
        )
        for k in range(4):
            piece = coefficients[:, k * LOADS : (k + 1) * LOADS]
            far[k] = piece if part == "first" else carried_far[k] + piece

    def coefficients_of(t):
        return jnp.concatenate([far[k, pl.ds(t, 8, stride=8), :] for k in range(4)], axis=0)

    def decode(k):
        both = [entry[2 * k + h] for h in range(2)]
        return (both[0] >> 6) & 7, [v & 63 for v in both], [v >> 12 for v in both]

    def make_tile(k, tile):
        t, slot, pairs = decode(k)
        amount = [p.astype(f32) * kelvin_coef for p in pairs]
        point = targets[t]
        step = 16
        for at in range(0, CS, step):
            side = at // HALF
            rows = slice(at % HALF, at % HALF + step)
            here = [spread[slot[side], i, rows] for i in range(4)]
            for h in range(2):
                lanes = slice(h * HALF, (h + 1) * HALF)
                dx, dy, dz = (here[i] - point[i : i + 1, lanes] for i in range(3))
                inverse = lax.rsqrt(dx * dx + dy * dy + dz * dz + eps_square)
                scaled = (here[3] * (point[3:4, lanes] * amount[side])) * inverse
                cubed = scaled * (inverse * inverse)
                level = lame_ratio * scaled
                ex, ey, ez = dx * cubed, dy * cubed, dz * cubed
                values = (dx * ex + level, dy * ey + level, dz * ez + level, dx * ey, dx * ez, dy * ez)
                for b in range(6):
                    tile[b, at : at + step, lanes] = values[b].astype(bf16)

    def add_products(k, tile):
        t, slot, _ = decode(k)
        f = []
        for j in range(3):
            parts = []
            for h in range(2):
                base = ((slot[h] >> 1) - first_unit) * UNIT + (slot[h] & 1) * DENS + j * HALF
                parts.append(flat[pl.ds(pl.multiple_of(base, 16), HALF), :])
            f.append(jnp.concatenate(parts, axis=1))
        f = jnp.concatenate(f, axis=1)
        order = ((0, 3, 4), (3, 1, 5), (4, 5, 2))
        sums = [
            dot32(f, jnp.concatenate([tile[b] for b in order[i]], axis=0)) for i in range(3)
        ]
        for i in range(3):
            for h in range(2):
                at = (2 * i + h) * HALF
                acc[t - low, at : at + HALF] += sums[i][:, h * HALF : (h + 1) * HALF]

    tasks = entries >> 1

    @pl.when(tasks > 0)
    def _():
        make_tile(0, tile_a)

        def two_tasks(k, carry):
            make_tile(2 * k + 1, tile_b)
            add_products(2 * k, tile_a)

            @pl.when(2 * k + 1 < tasks)
            def _():
                make_tile(2 * k + 2, tile_a)
                add_products(2 * k + 1, tile_b)

            return carry

        lax.fori_loop(0, (tasks + 1) >> 1, two_tasks, 0)

    if part == "send":
        for t in range(low, high):
            send[t - low, : 3 * CS] = acc[t - low].astype(bf16)
            send[t - low, 3 * CS :] = coefficients_of(t).astype(bf16)
    elif not sums_far:
        for t in range(low, high):
            acc[t - low, 3 * CS :] = coefficients_of(t)
    if part == "own":
        for k in range(2):
            pair[k] = acc[1].astype(bf16)


def near(part, first_unit, buffers, carried, counts, targets, spread, blocks):
    count = len(buffers)
    slots = 4 * count
    sums = jax.ShapeDtypeStruct((SPANS[part][1], 3 * CS, LOADS), f32)
    far = jax.ShapeDtypeStruct((4, 64, LOADS), f32)
    scratch = [
        pltpu.VMEM((count * 2 * UNIT, LOADS), bf16),
        pltpu.VMEM((6, CS, CS), bf16),
        pltpu.VMEM((6, CS, CS), bf16),
        pltpu.SMEM((8 * slots + 16,), jnp.int32),
    ]
    operands = [counts, targets, spread, *buffers]
    low, high = SPANS[part]
    if part in ("keep", "own"):
        shapes = (jax.ShapeDtypeStruct((high - low, FULL, LOADS), f32),)
        if part == "own":
            shapes += (jax.ShapeDtypeStruct((2, FULL, LOADS), bf16),)
    else:
        operands.append(blocks)
        scratch.append(pltpu.VMEM((2 * count * 128, 4 * LOADS), bf16))
        shapes = (sums, far)
        if part == "send":
            shapes = (jax.ShapeDtypeStruct((high - low, FULL, LOADS), bf16), far)
            scratch = [pltpu.VMEM((high - low, 3 * CS, LOADS), f32)] + scratch
    operands += carried
    return pl.pallas_call(
        functools.partial(near_kernel, first_unit, count, part),
        out_shape=shapes,
        in_specs=[pl.BlockSpec(memory_space=pltpu.SMEM)] + whole(len(operands) - 1),
        out_specs=tuple(whole(len(shapes))),
        scratch_shapes=scratch,
        compiler_params=pltpu.CompilerParams(vmem_limit_bytes=VMEM_LIMIT),
        cost_estimate=pl.CostEstimate(
            flops=count * 1_000_000_000, bytes_accessed=8_000_000, transcendentals=count * 500_000
        ),
        name=f"near_{part}",
    )(*operands)


def finish_kernel(core, keep, swapped, one, two, three, bases, out):
    def total(rows):
        return (
            keep[0, rows] + swapped[1 - core[0], rows].astype(f32) + one[rows].astype(f32)
            + two[rows].astype(f32) + three[rows].astype(f32)
        )

    coefficients = total(slice(3 * CS, FULL))
    high = coefficients.astype(bf16)
    low = (coefficients - high.astype(f32)).astype(bf16)
    both = jnp.concatenate([high, low], axis=0)
    row, held = iota((2 * RANK, 2 * RANK), 0), iota((2 * RANK, 2 * RANK), 1)
    from_row = (row & 32) + ((row & 3) << 3) + ((row & 31) >> 2)
    order = jnp.where(held == from_row, 1.0, 0.0).astype(bf16)
    both = dot32(order, both).astype(bf16)
    for j in range(3):
        basis = bases[0, j]
        twice = jnp.concatenate([basis, basis], axis=0)
        expanded = lax.dot_general(
            twice, both, (((0,), (0,)), ((), ())), preferred_element_type=f32
        )
        for h in range(2):
            at = (2 * j + h) * HALF
            near_part = jnp.transpose(total(slice(at, at + HALF)))
            panels = slice(h * HALF, (h + 1) * HALF)
            out[0, j, panels] = (near_part + expanded[panels]).astype(bf16)


def finish(core, keep, swapped, others, bases):
    return pl.pallas_call(
        finish_kernel,
        out_shape=jax.ShapeDtypeStruct((1, 3, CS, LOADS), bf16),
        in_specs=[pl.BlockSpec(memory_space=pltpu.SMEM)] + whole(6),
        out_specs=whole(1)[0],
        compiler_params=pltpu.CompilerParams(vmem_limit_bytes=VMEM_LIMIT),
        name="sum_and_expand",
    )(jnp.reshape(core, (1,)), keep, swapped, *others, bases)


def local(densities, positions, areas, bases, near_pairs, far_pairs, couplings):
    row = lax.axis_index("row")
    col = lax.axis_index("col")
    core, here = row & 1, (row >> 1) * 32 + col
    z, y, x = ((here >> shift) & 3 for shift in (LINE, OUTER, INNER))
    first_at = jnp.where(core == 0, x, y)
    second_at = jnp.where(core == 0, y, x)

    def unit_of(cluster):
        on_y, on_x = (cluster >> OUTER) & 3, (cluster >> INNER) & 3
        first = (jnp.where(core == 0, on_x, on_y) - first_at) & 3
        second = (jnp.where(core == 0, on_y, on_x) - second_at) & 3
        put = lambda r: jnp.where(r == 0, 0, jnp.where(r == 1, 2, jnp.where(r == 2, 3, 1)))
        return put(second) * SIDE + put(first)

    def other_core(cluster):
        return ((cluster >> 4) + core) & 1

    def slot_of(cluster):
        return jnp.where(((cluster >> LINE) & 3) == z, unit_of(cluster) * 2 + other_core(cluster), -1)

    def target_of(cluster):
        step, other = ((cluster >> LINE) - z) & 3, other_core(cluster)
        place = jnp.where(step == 0, AWAY + other, other * 3 + step - 1)
        same = (((cluster >> OUTER) & 3) == y) & (((cluster >> INNER) & 3) == x)
        return jnp.where(same, place, -1)

    bases = jnp.transpose(bases, (0, 2, 1, 3))
    positions = jnp.transpose(positions, (1, 0, 2))

    partner = swap_core(densities)
    own, moments, flip = moments_of(core, densities, bases)
    unit = make_unit(core, own, partner, moments)
    from_across = along_first(unit, 2)
    from_above = along_first(unit, -1)
    from_below = along_first(unit, 1)
    here = jnp.stack([z, core, y, x]).astype(jnp.int32)
    here, unit = lax.optimization_barrier((here, unit))
    spread, targets, couplings = make_points(here, positions, areas, couplings)
    near_pairs, far_pairs, spread = lax.optimization_barrier((near_pairs, far_pairs, spread))

    heads, tails = near_pairs[:, 0], near_pairs[:, 1]
    mark = lambda index, size: index[None, :] == jnp.arange(size, dtype=jnp.int32)[:, None]
    to_targets = jnp.concatenate(
        [target_of(heads), jnp.where(heads != tails, target_of(tails), -1)]
    )
    from_slots = jnp.concatenate([slot_of(tails), slot_of(heads)])
    counts = lax.dot_general(
        mark(to_targets, 8).astype(bf16),
        mark(from_slots, 32).astype(bf16),
        (((1,), (1,)), ((), ())),
        preferred_element_type=f32,
    ).astype(jnp.int32)
    counts = counts * 4096 + jnp.arange(8, dtype=jnp.int32)[:, None] * 64 + jnp.arange(32, dtype=jnp.int32)

    far_heads, far_tails = far_pairs[:, 0], far_pairs[:, 1]

    def cell(target, source):
        ours = (target_of(target) >= 0) & (slot_of(source) >= 0) & (other_core(source) == 0)
        return jnp.where(ours, unit_of(source) * 8 + target_of(target), -1)

    back_cell = jnp.where(far_heads != far_tails, cell(far_tails, far_heads), -1)
    blocks = make_blocks(cell(far_heads, far_tails), back_cell, couplings, flip)
    (spread, targets, counts, blocks, unit, from_below, from_above, from_across) = (
        lax.optimization_barrier(
            (spread, targets, counts, blocks, unit, from_below, from_above, from_across)
        )
    )
    low = jnp.concatenate([unit, from_below], axis=0)
    high = jnp.concatenate([from_above, from_across], axis=0)
    low_below = along_second(low, 1)
    high_above = along_second(high, -1)

    high_below = along_second(high, 1)
    low_above = along_second(low, -1)
    tables = (counts, targets, spread)

    carried = near("first", 0, (low, high), (), *tables, blocks)
    started = carried[0]
    low_below, high_above, carried = lax.optimization_barrier((low_below, high_above, carried))
    low_across = along_second(low_below, 1)
    high_across = along_second(high_above, -1)
    beside = (low_below, high_below, low_above, high_above)
    carried = near("middle", 4, beside, carried, *tables, blocks)
    across = (low_across, high_across)
    send, far = near("send", 12, across, carried, *tables, blocks)
    swapped = swap_core(send)
    (keep,) = near("keep", 12, across, (carried[0], far), *tables, blocks)
    both = [(keep[k] + swapped[k].astype(f32)).astype(bf16) for k in range(3)]
    both, far = lax.optimization_barrier((both, far))
    two_hops = along_line(both[1], 2)
    others = [two_hops, along_line(both[0], 1), along_line(both[2], 3)]
    own, pair = near("own", 4, beside + across, (started, far), *tables, blocks)
    chips = [[2 * k, 2 * k + 1] for k in range(SIDE)]
    swapped = lax.all_to_all(pair, "row", 0, 0, axis_index_groups=chips, tiled=True)
    return finish(core, own, swapped, others, bases)


def solution(mesh):
    return jax.shard_map(
        local,
        mesh=mesh,
        in_specs=(
            P(("row", "col"), None, None, None),
            P(),
            P(),
            P(("row", "col"), None, None, None),
            P(),
            P(),
            P(),
        ),
        out_specs=P(("row", "col"), None, None, None),
        check_vma=False,
    )
```

```python
import functools

import jax
import jax.numpy as jnp
from jax import lax
from jax.experimental import pallas as pl
from jax.experimental.pallas import tpu as pltpu
from jax.sharding import PartitionSpec as P


CS = 256
LOADS = 128
RANK = 32
HALF = CS // 2
DENS = 3 * HALF
UNIT = 2 * DENS + RANK
FULL = 3 * CS + RANK
AXES = ("row", "col")
TARGETS = ((1, 0), (2, 0), (3, 0), (1, 1), (2, 1), (3, 1), (0, 0), (0, 1))
AWAY = 6
SPANS = {"first": (0, AWAY), "middle": (0, AWAY), "send": (3, AWAY), "keep": (0, 3), "own": (AWAY, 8)}
SIDE = 4

eps_square = 0.0004
lame_ratio = 1.8
kelvin_coef = 1.0 / (16.0 * 3.141592653589793 * 0.7)
VMEM_LIMIT = 16 * 1024 * 1024
bf16 = jnp.bfloat16
f32 = jnp.float32


def routes(move):
    pairs = []
    for z in range(SIDE):
        for core in range(2):
            for y in range(SIDE):
                for x in range(SIDE):
                    to_z, to_core, to_y, to_x = move(z, core, y, x)
                    source = (z * 2 + core) * 16 + y * SIDE + x
                    target = ((to_z % SIDE) * 2 + to_core) * 16 + (to_y % SIDE) * SIDE + to_x % SIDE
                    pairs.append((source, target))
    return pairs


def swap_core(value):
    return lax.ppermute(value, AXES, routes(lambda z, c, y, x: (z, 1 - c, y, x)))


def along_first(value, step):
    move = lambda z, c, y, x: (z, c, y, x + step) if c == 0 else (z, c, y + step, x)
    return lax.ppermute(value, AXES, routes(move))


def along_second(value, step):
    move = lambda z, c, y, x: (z, c, y + step, x) if c == 0 else (z, c, y, x + step)
    return lax.ppermute(value, AXES, routes(move))


def along_z(value, step):
    return lax.ppermute(value, AXES, routes(lambda z, c, y, x: (z + step, c, y, x)))


def whole(count):
    return [pl.BlockSpec(memory_space=pltpu.VMEM)] * count


def dot32(a, b):
    return jnp.dot(a, b, preferred_element_type=f32)


def iota(shape, dim):
    return lax.broadcasted_iota(jnp.int32, shape, dim)


def fetch(source, target, sem):
    copy = pltpu.make_async_copy(source, target, sem)
    copy.start()
    return copy


def moments_kernel(core_ref, dens_ref, bases_ref, own_ref, moments_ref, flip_ref, dens, bases, sems):
    copies = [fetch(dens_ref, dens, sems.at[0]), fetch(bases_ref, bases, sems.at[1])]
    width = RANK * RANK
    step = 128
    for at in range(0, width, step):
        source, target = iota((step, width), 0) + at, iota((step, width), 1)
        turned = ((target & (RANK - 1)) << 5) + (target >> 5)
        flip_ref[at : at + step] = jnp.where(source == turned, 1.0, 0.0).astype(bf16)
    half = pl.ds(pl.multiple_of(core_ref[0] * HALF, HALF), HALF)
    total = jnp.zeros((RANK, LOADS), f32)
    for copy in copies:
        copy.wait()
    for j in range(3):
        total += dot32(bases[0, j], dens[0, j])
        own_ref[j * HALF : (j + 1) * HALF] = jnp.transpose(dens[0, j, half, :])
    moments_ref[...] = total.astype(bf16)


def in_hbm(array):
    return pltpu.with_memory_space_constraint(array, pltpu.HBM)


def moments_of(core, densities, bases):
    width = RANK * RANK
    return pl.pallas_call(
        moments_kernel,
        out_shape=(
            jax.ShapeDtypeStruct((DENS, LOADS), bf16),
            jax.ShapeDtypeStruct((RANK, LOADS), bf16),
            jax.ShapeDtypeStruct((width, width), bf16),
        ),
        in_specs=[pl.BlockSpec(memory_space=pltpu.SMEM)] + [pl.BlockSpec(memory_space=pltpu.HBM)] * 2,
        out_specs=tuple(whole(3)),
        scratch_shapes=[
            pltpu.VMEM(densities.shape, bf16),
            pltpu.VMEM(bases.shape, bf16),
            pltpu.SemaphoreType.DMA((2,)),
        ],
        compiler_params=pltpu.CompilerParams(vmem_limit_bytes=VMEM_LIMIT),
        name="moments",
    )(jnp.reshape(core, (1,)), in_hbm(densities), in_hbm(bases))


def unit_kernel(core_ref, own_ref, partner_ref, moments_ref, unit_ref):
    half = pl.ds(pl.multiple_of(core_ref[0] * HALF, HALF), HALF)
    unit_ref[:DENS] = own_ref[...]
    for j in range(3):
        unit_ref[DENS + j * HALF : DENS + (j + 1) * HALF] = jnp.transpose(
            partner_ref[0, j, half, :]
        )
    unit_ref[2 * DENS :] = moments_ref[...]


def make_unit(core, own, partner, moments):
    return pl.pallas_call(
        unit_kernel,
        out_shape=jax.ShapeDtypeStruct((UNIT, LOADS), bf16),
        in_specs=[pl.BlockSpec(memory_space=pltpu.SMEM)] + whole(3),
        out_specs=whole(1)[0],
        compiler_params=pltpu.CompilerParams(vmem_limit_bytes=VMEM_LIMIT),
        name="unit",
    )(jnp.reshape(core, (1,)), own, partner, moments)


def points_kernel(
    here_ref, positions_ref, areas_ref, couplings_ref,
    spread_ref, targets_ref, held_couplings, columns, positions, areas, sems,
):
    first = [fetch(positions_ref, positions, sems.at[0]), fetch(areas_ref, areas, sems.at[1])]
    last = fetch(couplings_ref, held_couplings, sems.at[2])
    z, core, y, x = (here_ref[k] for k in range(4))
    half = lambda whole_row: jnp.where(core == 0, whole_row[:, :HALF], whole_row[:, HALF:])
    back = (0, 3, 1, 2)
    for copy in first:
        copy.wait()
    for t, (step, other) in enumerate(TARGETS):
        cluster = ((step + z) & 3) * 32 + ((other + core) & 1) * 16 + y * SIDE + x
        for i in range(3):
            targets_ref[t, i : i + 1, :] = positions[i, pl.ds(cluster, 1), :]
        targets_ref[t, 3:4, :] = areas[pl.ds(cluster, 1), :]
    for s in range(32):
        first, second = back[(s >> 1) & 3], back[s >> 3]
        on_x = (x + jnp.where(core == 0, first, second)) & 3
        on_y = (y + jnp.where(core == 0, second, first)) & 3
        cluster = z * 32 + ((s + core) & 1) * 16 + on_y * SIDE + on_x
        for i in range(3):
            columns[s, i : i + 1, :] = half(positions[i, pl.ds(cluster, 1), :])
        columns[s, 3:4, :] = half(areas[pl.ds(cluster, 1), :])
    for s in range(32):
        upright = jnp.transpose(columns[s])
        for i in range(4):
            spread_ref[s, i] = jnp.broadcast_to(upright[:, i : i + 1], (HALF, LOADS))
    last.wait()


def make_points(here, positions, areas, couplings):
    return pl.pallas_call(
        points_kernel,
        out_shape=(
            jax.ShapeDtypeStruct((32, 4, HALF, LOADS), f32),
            jax.ShapeDtypeStruct((8, 8, CS), f32),
            jax.ShapeDtypeStruct(couplings.shape, bf16),
        ),
        in_specs=[pl.BlockSpec(memory_space=pltpu.SMEM)] + [pl.BlockSpec(memory_space=pltpu.HBM)] * 3,
        out_specs=tuple(whole(3)),
        scratch_shapes=[
            pltpu.VMEM((32, 8, HALF), f32),
            pltpu.VMEM(positions.shape, f32),
            pltpu.VMEM(areas.shape, f32),
            pltpu.SemaphoreType.DMA((3,)),
        ],
        compiler_params=pltpu.CompilerParams(vmem_limit_bytes=VMEM_LIMIT),
        name="points",
    )(here, in_hbm(positions), in_hbm(areas), in_hbm(couplings))


def blocks_kernel(forward_ref, backward_ref, couplings_ref, flip_ref, blocks_ref):
    cells = 128
    far = couplings_ref.shape[0]

    def summed(cell_ref):
        marks = iota((cells, far), 0) == cell_ref[...]
        return dot32(jnp.where(marks, 1.0, 0.0).astype(bf16), couplings_ref[...])

    total = summed(forward_ref) + dot32(summed(backward_ref).astype(bf16), flip_ref[...])
    for u in range(16):
        unit = total[u * 8 : (u + 1) * 8]
        for g in range(0, 8, 2):
            two = [unit[:, k * 128 : (k + 1) * 128] for k in (g, g + 1)]
            lanes = slice(u * 128, (u + 1) * 128)
            blocks_ref[g * 8 : (g + 2) * 8, lanes] = jnp.concatenate(two, axis=0).astype(bf16)


def make_blocks(forward, backward, couplings, flip):
    return pl.pallas_call(
        blocks_kernel,
        out_shape=jax.ShapeDtypeStruct((64, 16 * 128), bf16),
        in_specs=whole(4),
        out_specs=whole(1)[0],
        compiler_params=pltpu.CompilerParams(vmem_limit_bytes=VMEM_LIMIT),
        name="coupling_blocks",
    )(forward[None, :], backward[None, :], couplings, flip)


def near_kernel(first_unit, buffers, part, counts, targets, spread, *refs):
    units = 2 * buffers
    slots = 2 * units
    held, refs = refs[:buffers], refs[buffers:]
    low, high = SPANS[part]
    sums_far = part in ("first", "middle", "send")
    if sums_far:
        blocks, refs = refs[0], refs[1:]
    if part in ("middle", "send"):
        carried, carried_far, refs = refs[0], refs[1], refs[2:]
    elif part == "keep":
        carried, far, refs = refs[0], refs[1], refs[2:]
    elif part == "own":
        far, refs = refs[0], refs[1:]
    if part == "send":
        send, far, acc, refs = refs[0], refs[1], refs[2], refs[3:]
    elif sums_far:
        acc, far, refs = refs[0], refs[1], refs[2:]
    elif part == "keep":
        acc, refs = refs[0], refs[1:]
    else:
        acc, pair, refs = refs[0], refs[1], refs[2:]
    flat, tile_a, tile_b, entry = refs[:4]

    for k in range(buffers):
        flat[k * 2 * UNIT : (k + 1) * 2 * UNIT] = held[k][...]

    def list_target(t, filled):
        for value in [counts[t, 2 * first_unit + s] for s in range(slots)]:
            entry[filled] = value
            filled = filled + jnp.where(value >= 4096, 1, 0)
        entry[filled] = t * 64 + 2 * first_unit
        return filled + (filled & 1)

    entries = lax.fori_loop(low, high, list_target, 0)
    for k in range(6):
        entry[entries + k] = low * 64 + 2 * first_unit
    near_rows = slice(0, 3 * CS)
    if part in ("first", "own"):
        acc[:, near_rows] = jnp.zeros((high - low, 3 * CS, LOADS), f32)
    else:
        acc[:, near_rows] = carried[low:high]

    if sums_far:
        wide = refs[4]
        wide[...] = jnp.zeros(wide.shape, bf16)
        for u in range(units):
            moments = flat[u * UNIT + 2 * DENS : (u + 1) * UNIT, :]
            for k in range(4):
                at = u * 128 + k * RANK
                wide[at : at + RANK, k * LOADS : (k + 1) * LOADS] = moments
        coefficients = dot32(
            blocks[:, first_unit * 128 : (first_unit + units) * 128], wide[...]
        )
        for k in range(4):
            piece = coefficients[:, k * LOADS : (k + 1) * LOADS]
            far[k] = piece if part == "first" else carried_far[k] + piece

    def coefficients_of(t):
        return jnp.concatenate([far[k, pl.ds(t, 8, stride=8), :] for k in range(4)], axis=0)

    def decode(k):
        both = [entry[2 * k + h] for h in range(2)]
        return (both[0] >> 6) & 7, [v & 63 for v in both], [v >> 12 for v in both]

    def make_tile(k, tile):
        t, slot, pairs = decode(k)
        amount = [p.astype(f32) * kelvin_coef for p in pairs]
        point = targets[t]
        step = 16
        for at in range(0, CS, step):
            side = at // HALF
            rows = slice(at % HALF, at % HALF + step)
            here = [spread[slot[side], i, rows] for i in range(4)]
            for h in range(2):
                lanes = slice(h * HALF, (h + 1) * HALF)
                dx, dy, dz = (here[i] - point[i : i + 1, lanes] for i in range(3))
                inverse = lax.rsqrt(dx * dx + dy * dy + dz * dz + eps_square)
                scaled = (here[3] * (point[3:4, lanes] * amount[side])) * inverse
                cubed = scaled * (inverse * inverse)
                level = lame_ratio * scaled
                ex, ey, ez = dx * cubed, dy * cubed, dz * cubed
                values = (dx * ex + level, dy * ey + level, dz * ez + level, dx * ey, dx * ez, dy * ez)
                for b in range(6):
                    tile[b, at : at + step, lanes] = values[b].astype(bf16)

    def add_products(k, tile):
        t, slot, _ = decode(k)
        f = []
        for j in range(3):
            parts = []
            for h in range(2):
                base = ((slot[h] >> 1) - first_unit) * UNIT + (slot[h] & 1) * DENS + j * HALF
                parts.append(flat[pl.ds(pl.multiple_of(base, 16), HALF), :])
            f.append(jnp.concatenate(parts, axis=1))
        f = jnp.concatenate(f, axis=1)
        order = ((0, 3, 4), (3, 1, 5), (4, 5, 2))
        sums = [
            dot32(f, jnp.concatenate([tile[b] for b in order[i]], axis=0)) for i in range(3)
        ]
        for i in range(3):
            for h in range(2):
                at = (2 * i + h) * HALF
                acc[t - low, at : at + HALF] += sums[i][:, h * HALF : (h + 1) * HALF]

    tasks = entries >> 1

    @pl.when(tasks > 0)
    def _():
        make_tile(0, tile_a)

        def two_tasks(k, carry):
            make_tile(2 * k + 1, tile_b)
            add_products(2 * k, tile_a)

            @pl.when(2 * k + 1 < tasks)
            def _():
                make_tile(2 * k + 2, tile_a)
                add_products(2 * k + 1, tile_b)

            return carry

        lax.fori_loop(0, (tasks + 1) >> 1, two_tasks, 0)

    if part == "send":
        for t in range(low, high):
            send[t - low, : 3 * CS] = acc[t - low].astype(bf16)
            send[t - low, 3 * CS :] = coefficients_of(t).astype(bf16)
    elif not sums_far:
        for t in range(low, high):
            acc[t - low, 3 * CS :] = coefficients_of(t)
    if part == "own":
        for k in range(2):
            pair[k] = acc[1].astype(bf16)


def near(part, first_unit, buffers, carried, counts, targets, spread, blocks):
    count = len(buffers)
    slots = 4 * count
    sums = jax.ShapeDtypeStruct((AWAY, 3 * CS, LOADS), f32)
    far = jax.ShapeDtypeStruct((4, 64, LOADS), f32)
    scratch = [
        pltpu.VMEM((count * 2 * UNIT, LOADS), bf16),
        pltpu.VMEM((6, CS, CS), bf16),
        pltpu.VMEM((6, CS, CS), bf16),
        pltpu.SMEM((8 * slots + 16,), jnp.int32),
    ]
    operands = [counts, targets, spread, *buffers]
    low, high = SPANS[part]
    if part in ("keep", "own"):
        shapes = (jax.ShapeDtypeStruct((high - low, FULL, LOADS), f32),)
        if part == "own":
            shapes += (jax.ShapeDtypeStruct((2, FULL, LOADS), bf16),)
    else:
        operands.append(blocks)
        scratch.append(pltpu.VMEM((2 * count * 128, 4 * LOADS), bf16))
        shapes = (sums, far)
        if part == "send":
            shapes = (jax.ShapeDtypeStruct((high - low, FULL, LOADS), bf16), far)
            scratch = [pltpu.VMEM((high - low, 3 * CS, LOADS), f32)] + scratch
    operands += carried
    return pl.pallas_call(
        functools.partial(near_kernel, first_unit, count, part),
        out_shape=shapes,
        in_specs=[pl.BlockSpec(memory_space=pltpu.SMEM)] + whole(len(operands) - 1),
        out_specs=tuple(whole(len(shapes))),
        scratch_shapes=scratch,
        compiler_params=pltpu.CompilerParams(vmem_limit_bytes=VMEM_LIMIT),
        cost_estimate=pl.CostEstimate(
            flops=count * 1_000_000_000, bytes_accessed=8_000_000, transcendentals=count * 500_000
        ),
        name=f"near_{part}",
    )(*operands)


def finish_kernel(core, keep, swapped, one, two, three, bases, out):
    def total(rows):
        return (
            keep[0, rows] + swapped[1 - core[0], rows].astype(f32) + one[rows].astype(f32)
            + two[rows].astype(f32) + three[rows].astype(f32)
        )

    coefficients = total(slice(3 * CS, FULL))
    high = coefficients.astype(bf16)
    low = (coefficients - high.astype(f32)).astype(bf16)
    both = jnp.concatenate([high, low], axis=0)
    row, held = iota((2 * RANK, 2 * RANK), 0), iota((2 * RANK, 2 * RANK), 1)
    from_row = (row & 32) + ((row & 3) << 3) + ((row & 31) >> 2)
    order = jnp.where(held == from_row, 1.0, 0.0).astype(bf16)
    both = dot32(order, both).astype(bf16)
    for j in range(3):
        basis = bases[0, j]
        twice = jnp.concatenate([basis, basis], axis=0)
        expanded = lax.dot_general(
            twice, both, (((0,), (0,)), ((), ())), preferred_element_type=f32
        )
        for h in range(2):
            at = (2 * j + h) * HALF
            near_part = jnp.transpose(total(slice(at, at + HALF)))
            panels = slice(h * HALF, (h + 1) * HALF)
            out[0, j, panels] = (near_part + expanded[panels]).astype(bf16)


def finish(core, keep, swapped, others, bases):
    return pl.pallas_call(
        finish_kernel,
        out_shape=jax.ShapeDtypeStruct((1, 3, CS, LOADS), bf16),
        in_specs=[pl.BlockSpec(memory_space=pltpu.SMEM)] + whole(6),
        out_specs=whole(1)[0],
        compiler_params=pltpu.CompilerParams(vmem_limit_bytes=VMEM_LIMIT),
        name="sum_and_expand",
    )(jnp.reshape(core, (1,)), keep, swapped, *others, bases)


def local(densities, positions, areas, bases, near_pairs, far_pairs, couplings):
    row = lax.axis_index("row")
    col = lax.axis_index("col")
    z, core = row >> 1, row & 1
    y, x = col >> 2, col & 3
    first_at = jnp.where(core == 0, x, y)
    second_at = jnp.where(core == 0, y, x)

    def unit_of(cluster):
        on_y, on_x = (cluster >> 2) & 3, cluster & 3
        first = (jnp.where(core == 0, on_x, on_y) - first_at) & 3
        second = (jnp.where(core == 0, on_y, on_x) - second_at) & 3
        put = lambda r: jnp.where(r == 0, 0, jnp.where(r == 1, 2, jnp.where(r == 2, 3, 1)))
        return put(second) * SIDE + put(first)

    def other_core(cluster):
        return ((cluster >> 4) + core) & 1

    def slot_of(cluster):
        return jnp.where(cluster >> 5 == z, unit_of(cluster) * 2 + other_core(cluster), -1)

    def target_of(cluster):
        step, other = ((cluster >> 5) - z) & 3, other_core(cluster)
        place = jnp.where(step == 0, AWAY + other, other * 3 + step - 1)
        return jnp.where((cluster & 15) == col, place, -1)

    bases = jnp.transpose(bases, (0, 2, 1, 3))
    positions = jnp.transpose(positions, (1, 0, 2))

    partner = swap_core(densities)
    own, moments, flip = moments_of(core, densities, bases)
    unit = make_unit(core, own, partner, moments)
    from_across = along_first(unit, 2)
    from_above = along_first(unit, -1)
    from_below = along_first(unit, 1)
    here = jnp.stack([z, core, y, x]).astype(jnp.int32)
    here, unit = lax.optimization_barrier((here, unit))
    spread, targets, couplings = make_points(here, positions, areas, couplings)
    near_pairs, far_pairs, spread = lax.optimization_barrier((near_pairs, far_pairs, spread))

    heads, tails = near_pairs[:, 0], near_pairs[:, 1]
    mark = lambda index, size: index[None, :] == jnp.arange(size, dtype=jnp.int32)[:, None]
    to_targets = jnp.concatenate(
        [target_of(heads), jnp.where(heads != tails, target_of(tails), -1)]
    )
    from_slots = jnp.concatenate([slot_of(tails), slot_of(heads)])
    counts = lax.dot_general(
        mark(to_targets, 8).astype(bf16),
        mark(from_slots, 32).astype(bf16),
        (((1,), (1,)), ((), ())),
        preferred_element_type=f32,
    ).astype(jnp.int32)
    counts = counts * 4096 + jnp.arange(8, dtype=jnp.int32)[:, None] * 64 + jnp.arange(32, dtype=jnp.int32)

    far_heads, far_tails = far_pairs[:, 0], far_pairs[:, 1]

    def cell(target, source):
        ours = (target_of(target) >= 0) & (slot_of(source) >= 0) & (other_core(source) == 0)
        return jnp.where(ours, unit_of(source) * 8 + target_of(target), -1)

    back_cell = jnp.where(far_heads != far_tails, cell(far_tails, far_heads), -1)
    blocks = make_blocks(cell(far_heads, far_tails), back_cell, couplings, flip)
    (spread, targets, counts, blocks, unit, from_below, from_above, from_across) = (
        lax.optimization_barrier(
            (spread, targets, counts, blocks, unit, from_below, from_above, from_across)
        )
    )
    low = jnp.concatenate([unit, from_below], axis=0)
    high = jnp.concatenate([from_above, from_across], axis=0)
    low_below = along_second(low, 1)
    high_above = along_second(high, -1)

    high_below = along_second(high, 1)
    low_above = along_second(low, -1)
    tables = (counts, targets, spread)

    carried = near("first", 0, (low, high), (), *tables, blocks)
    low_below, high_above, carried = lax.optimization_barrier((low_below, high_above, carried))
    low_across = along_second(low_below, 1)
    high_across = along_second(high_above, -1)
    beside = (low_below, high_below, low_above, high_above)
    carried = near("middle", 4, beside, carried, *tables, blocks)
    across = (low_across, high_across)
    send, far = near("send", 12, across, carried, *tables, blocks)
    swapped = swap_core(send)
    (keep,) = near("keep", 12, across, (carried[0], far), *tables, blocks)
    both = [(keep[k] + swapped[k].astype(f32)).astype(bf16) for k in range(3)]
    both, far = lax.optimization_barrier((both, far))
    others = [along_z(both[0], 1), along_z(both[2], 3)]
    others.append(along_z(both[1], 2))
    everything = (low, high) + beside + across
    own, pair = near("own", 0, everything, (far,), *tables, blocks)
    chips = [[2 * k, 2 * k + 1] for k in range(SIDE)]
    swapped = lax.all_to_all(pair, "row", 0, 0, axis_index_groups=chips, tiled=True)
    return finish(core, own, swapped, others, bases)


def solution(mesh):
    return jax.shard_map(
        local,
        mesh=mesh,
        in_specs=(
            P(("row", "col"), None, None, None),
            P(),
            P(),
            P(("row", "col"), None, None, None),
            P(),
            P(),
            P(),
        ),
        out_specs=P(("row", "col"), None, None, None),
        check_vma=False,
    )
```

```python
import functools

import jax
import jax.numpy as jnp
from jax import lax
from jax.experimental import pallas as pl
from jax.experimental.pallas import tpu as pltpu
from jax.sharding import PartitionSpec as P


CS = 256
LOADS = 128
RANK = 32
HALF = CS // 2
DENS = 3 * HALF
UNIT = 2 * DENS + RANK
FULL = 3 * CS + RANK
AXES = ("row", "col")
TARGETS = ((1, 0), (2, 0), (3, 0), (1, 1), (2, 1), (3, 1), (0, 0), (0, 1))
AWAY = 6
SPANS = {"first": (0, AWAY), "middle": (0, AWAY), "send": (3, AWAY), "keep": (0, 3), "own": (AWAY, 8)}
SIDE = 4

eps_square = 0.0004
lame_ratio = 1.8
kelvin_coef = 1.0 / (16.0 * 3.141592653589793 * 0.7)
VMEM_LIMIT = 16 * 1024 * 1024
bf16 = jnp.bfloat16
f32 = jnp.float32


def routes(move):
    pairs = []
    for z in range(SIDE):
        for core in range(2):
            for y in range(SIDE):
                for x in range(SIDE):
                    to_z, to_core, to_y, to_x = move(z, core, y, x)
                    source = (z * 2 + core) * 16 + y * SIDE + x
                    target = ((to_z % SIDE) * 2 + to_core) * 16 + (to_y % SIDE) * SIDE + to_x % SIDE
                    pairs.append((source, target))
    return pairs


def swap_core(value):
    return lax.ppermute(value, AXES, routes(lambda z, c, y, x: (z, 1 - c, y, x)))


def along_first(value, step):
    move = lambda z, c, y, x: (z, c, y, x + step) if c == 0 else (z, c, y + step, x)
    return lax.ppermute(value, AXES, routes(move))


def along_second(value, step):
    move = lambda z, c, y, x: (z, c, y + step, x) if c == 0 else (z, c, y, x + step)
    return lax.ppermute(value, AXES, routes(move))


def along_z(value, step):
    return lax.ppermute(value, AXES, routes(lambda z, c, y, x: (z + step, c, y, x)))


def whole(count):
    return [pl.BlockSpec(memory_space=pltpu.VMEM)] * count


def dot32(a, b):
    return jnp.dot(a, b, preferred_element_type=f32)


def iota(shape, dim):
    return lax.broadcasted_iota(jnp.int32, shape, dim)


def fetch(source, target, sem):
    copy = pltpu.make_async_copy(source, target, sem)
    copy.start()
    return copy


def moments_kernel(core_ref, dens_ref, bases_ref, own_ref, moments_ref, flip_ref, dens, bases, sems):
    copies = [fetch(dens_ref, dens, sems.at[0]), fetch(bases_ref, bases, sems.at[1])]
    width = RANK * RANK
    step = 128
    for at in range(0, width, step):
        source, target = iota((step, width), 0) + at, iota((step, width), 1)
        turned = ((target & (RANK - 1)) << 5) + (target >> 5)
        flip_ref[at : at + step] = jnp.where(source == turned, 1.0, 0.0).astype(bf16)
    half = pl.ds(pl.multiple_of(core_ref[0] * HALF, HALF), HALF)
    total = jnp.zeros((RANK, LOADS), f32)
    for copy in copies:
        copy.wait()
    for j in range(3):
        total += dot32(bases[0, j], dens[0, j])
        own_ref[j * HALF : (j + 1) * HALF] = jnp.transpose(dens[0, j, half, :])
    moments_ref[...] = total.astype(bf16)


def in_hbm(array):
    return pltpu.with_memory_space_constraint(array, pltpu.HBM)


def moments_of(core, densities, bases):
    width = RANK * RANK
    return pl.pallas_call(
        moments_kernel,
        out_shape=(
            jax.ShapeDtypeStruct((DENS, LOADS), bf16),
            jax.ShapeDtypeStruct((RANK, LOADS), bf16),
            jax.ShapeDtypeStruct((width, width), bf16),
        ),
        in_specs=[pl.BlockSpec(memory_space=pltpu.SMEM)] + [pl.BlockSpec(memory_space=pltpu.HBM)] * 2,
        out_specs=tuple(whole(3)),
        scratch_shapes=[
            pltpu.VMEM(densities.shape, bf16),
            pltpu.VMEM(bases.shape, bf16),
            pltpu.SemaphoreType.DMA((2,)),
        ],
        compiler_params=pltpu.CompilerParams(vmem_limit_bytes=VMEM_LIMIT),
        name="moments",
    )(jnp.reshape(core, (1,)), in_hbm(densities), in_hbm(bases))


def unit_kernel(core_ref, own_ref, partner_ref, moments_ref, unit_ref):
    half = pl.ds(pl.multiple_of(core_ref[0] * HALF, HALF), HALF)
    unit_ref[:DENS] = own_ref[...]
    for j in range(3):
        unit_ref[DENS + j * HALF : DENS + (j + 1) * HALF] = jnp.transpose(
            partner_ref[0, j, half, :]
        )
    unit_ref[2 * DENS :] = moments_ref[...]


def make_unit(core, own, partner, moments):
    return pl.pallas_call(
        unit_kernel,
        out_shape=jax.ShapeDtypeStruct((UNIT, LOADS), bf16),
        in_specs=[pl.BlockSpec(memory_space=pltpu.SMEM)] + whole(3),
        out_specs=whole(1)[0],
        compiler_params=pltpu.CompilerParams(vmem_limit_bytes=VMEM_LIMIT),
        name="unit",
    )(jnp.reshape(core, (1,)), own, partner, moments)


def points_kernel(
    here_ref, positions_ref, areas_ref, couplings_ref,
    spread_ref, targets_ref, held_couplings, columns, positions, areas, sems,
):
    first = [fetch(positions_ref, positions, sems.at[0]), fetch(areas_ref, areas, sems.at[1])]
    last = fetch(couplings_ref, held_couplings, sems.at[2])
    z, core, y, x = (here_ref[k] for k in range(4))
    half = lambda whole_row: jnp.where(core == 0, whole_row[:, :HALF], whole_row[:, HALF:])
    back = (0, 3, 1, 2)
    for copy in first:
        copy.wait()
    for t, (step, other) in enumerate(TARGETS):
        cluster = ((step + z) & 3) * 32 + ((other + core) & 1) * 16 + y * SIDE + x
        for i in range(3):
            targets_ref[t, i : i + 1, :] = positions[i, pl.ds(cluster, 1), :]
        targets_ref[t, 3:4, :] = areas[pl.ds(cluster, 1), :]
    for s in range(32):
        first, second = back[(s >> 1) & 3], back[s >> 3]
        on_x = (x + jnp.where(core == 0, first, second)) & 3
        on_y = (y + jnp.where(core == 0, second, first)) & 3
        cluster = z * 32 + ((s + core) & 1) * 16 + on_y * SIDE + on_x
        for i in range(3):
            columns[s, i : i + 1, :] = half(positions[i, pl.ds(cluster, 1), :])
        columns[s, 3:4, :] = half(areas[pl.ds(cluster, 1), :])
    for s in range(32):
        upright = jnp.transpose(columns[s])
        for i in range(4):
            spread_ref[s, i] = jnp.broadcast_to(upright[:, i : i + 1], (HALF, LOADS))
    last.wait()


def make_points(here, positions, areas, couplings):
    return pl.pallas_call(
        points_kernel,
        out_shape=(
            jax.ShapeDtypeStruct((32, 4, HALF, LOADS), f32),
            jax.ShapeDtypeStruct((8, 8, CS), f32),
            jax.ShapeDtypeStruct(couplings.shape, bf16),
        ),
        in_specs=[pl.BlockSpec(memory_space=pltpu.SMEM)] + [pl.BlockSpec(memory_space=pltpu.HBM)] * 3,
        out_specs=tuple(whole(3)),
        scratch_shapes=[
            pltpu.VMEM((32, 8, HALF), f32),
            pltpu.VMEM(positions.shape, f32),
            pltpu.VMEM(areas.shape, f32),
            pltpu.SemaphoreType.DMA((3,)),
        ],
        compiler_params=pltpu.CompilerParams(vmem_limit_bytes=VMEM_LIMIT),
        name="points",
    )(here, in_hbm(positions), in_hbm(areas), in_hbm(couplings))


def blocks_kernel(forward_ref, backward_ref, couplings_ref, flip_ref, blocks_ref):
    cells = 128
    far = couplings_ref.shape[0]

    def summed(cell_ref):
        marks = iota((cells, far), 0) == cell_ref[...]
        return dot32(jnp.where(marks, 1.0, 0.0).astype(bf16), couplings_ref[...])

    total = summed(forward_ref) + dot32(summed(backward_ref).astype(bf16), flip_ref[...])
    for u in range(16):
        unit = total[u * 8 : (u + 1) * 8]
        for g in range(0, 8, 2):
            two = [unit[:, k * 128 : (k + 1) * 128] for k in (g, g + 1)]
            lanes = slice(u * 128, (u + 1) * 128)
            blocks_ref[g * 8 : (g + 2) * 8, lanes] = jnp.concatenate(two, axis=0).astype(bf16)


def make_blocks(forward, backward, couplings, flip):
    return pl.pallas_call(
        blocks_kernel,
        out_shape=jax.ShapeDtypeStruct((64, 16 * 128), bf16),
        in_specs=whole(4),
        out_specs=whole(1)[0],
        compiler_params=pltpu.CompilerParams(vmem_limit_bytes=VMEM_LIMIT),
        name="coupling_blocks",
    )(forward[None, :], backward[None, :], couplings, flip)


def near_kernel(first_unit, buffers, part, counts, targets, spread, *refs):
    units = 2 * buffers
    slots = 2 * units
    held, refs = refs[:buffers], refs[buffers:]
    low, high = SPANS[part]
    sums_far = part in ("first", "middle", "send")
    if sums_far:
        blocks, refs = refs[0], refs[1:]
    if part in ("middle", "send"):
        carried, carried_far, refs = refs[0], refs[1], refs[2:]
    elif part == "keep":
        carried, far, refs = refs[0], refs[1], refs[2:]
    elif part == "own":
        far, refs = refs[0], refs[1:]
    if part == "send":
        send, far, acc, refs = refs[0], refs[1], refs[2], refs[3:]
    elif sums_far:
        acc, far, refs = refs[0], refs[1], refs[2:]
    elif part == "keep":
        acc, refs = refs[0], refs[1:]
    else:
        acc, pair, refs = refs[0], refs[1], refs[2:]
    flat, tile_a, tile_b, entry = refs[:4]

    for k in range(buffers):
        flat[k * 2 * UNIT : (k + 1) * 2 * UNIT] = held[k][...]

    def list_target(t, filled):
        for value in [counts[t, 2 * first_unit + s] for s in range(slots)]:
            entry[filled] = value
            filled = filled + jnp.where(value >= 4096, 1, 0)
        entry[filled] = t * 64 + 2 * first_unit
        return filled + (filled & 1)

    entries = lax.fori_loop(low, high, list_target, 0)
    for k in range(6):
        entry[entries + k] = low * 64 + 2 * first_unit
    near_rows = slice(0, 3 * CS)
    if part in ("first", "own"):
        acc[:, near_rows] = jnp.zeros((high - low, 3 * CS, LOADS), f32)
    else:
        acc[:, near_rows] = carried[low:high]

    if sums_far:
        wide = refs[4]
        wide[...] = jnp.zeros(wide.shape, bf16)
        for u in range(units):
            moments = flat[u * UNIT + 2 * DENS : (u + 1) * UNIT, :]
            for k in range(4):
                at = u * 128 + k * RANK
                wide[at : at + RANK, k * LOADS : (k + 1) * LOADS] = moments
        coefficients = dot32(
            blocks[:, first_unit * 128 : (first_unit + units) * 128], wide[...]
        )
        for k in range(4):
            piece = coefficients[:, k * LOADS : (k + 1) * LOADS]
            far[k] = piece if part == "first" else carried_far[k] + piece

    def coefficients_of(t):
        return jnp.concatenate([far[k, pl.ds(t, 8, stride=8), :] for k in range(4)], axis=0)

    def decode(k):
        both = [entry[2 * k + h] for h in range(2)]
        return (both[0] >> 6) & 7, [v & 63 for v in both], [v >> 12 for v in both]

    def make_tile(k, tile):
        t, slot, pairs = decode(k)
        amount = [p.astype(f32) * kelvin_coef for p in pairs]
        point = targets[t]
        step = 16
        for at in range(0, CS, step):
            side = at // HALF
            rows = slice(at % HALF, at % HALF + step)
            here = [spread[slot[side], i, rows] for i in range(4)]
            for h in range(2):
                lanes = slice(h * HALF, (h + 1) * HALF)
                dx, dy, dz = (here[i] - point[i : i + 1, lanes] for i in range(3))
                inverse = lax.rsqrt(dx * dx + dy * dy + dz * dz + eps_square)
                scaled = (here[3] * (point[3:4, lanes] * amount[side])) * inverse
                cubed = scaled * (inverse * inverse)
                level = lame_ratio * scaled
                ex, ey, ez = dx * cubed, dy * cubed, dz * cubed
                values = (dx * ex + level, dy * ey + level, dz * ez + level, dx * ey, dx * ez, dy * ez)
                for b in range(6):
                    tile[b, at : at + step, lanes] = values[b].astype(bf16)

    def add_products(k, tile):
        t, slot, _ = decode(k)
        f = []
        for j in range(3):
            parts = []
            for h in range(2):
                base = ((slot[h] >> 1) - first_unit) * UNIT + (slot[h] & 1) * DENS + j * HALF
                parts.append(flat[pl.ds(pl.multiple_of(base, 16), HALF), :])
            f.append(jnp.concatenate(parts, axis=1))
        f = jnp.concatenate(f, axis=1)
        order = ((0, 3, 4), (3, 1, 5), (4, 5, 2))
        sums = [
            dot32(f, jnp.concatenate([tile[b] for b in order[i]], axis=0)) for i in range(3)
        ]
        for i in range(3):
            for h in range(2):
                at = (2 * i + h) * HALF
                acc[t - low, at : at + HALF] += sums[i][:, h * HALF : (h + 1) * HALF]

    tasks = entries >> 1

    @pl.when(tasks > 0)
    def _():
        make_tile(0, tile_a)

        def two_tasks(k, carry):
            make_tile(2 * k + 1, tile_b)
            add_products(2 * k, tile_a)

            @pl.when(2 * k + 1 < tasks)
            def _():
                make_tile(2 * k + 2, tile_a)
                add_products(2 * k + 1, tile_b)

            return carry

        lax.fori_loop(0, (tasks + 1) >> 1, two_tasks, 0)

    if part == "send":
        for t in range(low, high):
            send[t - low, : 3 * CS] = acc[t - low].astype(bf16)
            send[t - low, 3 * CS :] = coefficients_of(t).astype(bf16)
    elif not sums_far:
        for t in range(low, high):
            acc[t - low, 3 * CS :] = coefficients_of(t)
    if part == "own":
        for k in range(2):
            pair[k] = acc[1].astype(bf16)


def near(part, first_unit, buffers, carried, counts, targets, spread, blocks):
    count = len(buffers)
    slots = 4 * count
    sums = jax.ShapeDtypeStruct((AWAY, 3 * CS, LOADS), f32)
    far = jax.ShapeDtypeStruct((4, 64, LOADS), f32)
    scratch = [
        pltpu.VMEM((count * 2 * UNIT, LOADS), bf16),
        pltpu.VMEM((6, CS, CS), bf16),
        pltpu.VMEM((6, CS, CS), bf16),
        pltpu.SMEM((8 * slots + 16,), jnp.int32),
    ]
    operands = [counts, targets, spread, *buffers]
    low, high = SPANS[part]
    if part in ("keep", "own"):
        shapes = (jax.ShapeDtypeStruct((high - low, FULL, LOADS), f32),)
        if part == "own":
            shapes += (jax.ShapeDtypeStruct((2, FULL, LOADS), bf16),)
    else:
        operands.append(blocks)
        scratch.append(pltpu.VMEM((2 * count * 128, 4 * LOADS), bf16))
        shapes = (sums, far)
        if part == "send":
            shapes = (jax.ShapeDtypeStruct((high - low, FULL, LOADS), bf16), far)
            scratch = [pltpu.VMEM((high - low, 3 * CS, LOADS), f32)] + scratch
    operands += carried
    return pl.pallas_call(
        functools.partial(near_kernel, first_unit, count, part),
        out_shape=shapes,
        in_specs=[pl.BlockSpec(memory_space=pltpu.SMEM)] + whole(len(operands) - 1),
        out_specs=tuple(whole(len(shapes))),
        scratch_shapes=scratch,
        compiler_params=pltpu.CompilerParams(vmem_limit_bytes=VMEM_LIMIT),
        cost_estimate=pl.CostEstimate(
            flops=count * 1_000_000_000, bytes_accessed=8_000_000, transcendentals=count * 500_000
        ),
        name=f"near_{part}",
    )(*operands)


def finish_kernel(core, keep, swapped, one, two, three, bases, out):
    def total(rows):
        return (
            keep[0, rows] + swapped[1 - core[0], rows].astype(f32) + one[rows].astype(f32)
            + two[rows].astype(f32) + three[rows].astype(f32)
        )

    coefficients = total(slice(3 * CS, FULL))
    high = coefficients.astype(bf16)
    low = (coefficients - high.astype(f32)).astype(bf16)
    both = jnp.concatenate([high, low], axis=0)
    row, held = iota((2 * RANK, 2 * RANK), 0), iota((2 * RANK, 2 * RANK), 1)
    from_row = (row & 32) + ((row & 3) << 3) + ((row & 31) >> 2)
    order = jnp.where(held == from_row, 1.0, 0.0).astype(bf16)
    both = dot32(order, both).astype(bf16)
    for j in range(3):
        basis = bases[0, j]
        twice = jnp.concatenate([basis, basis], axis=0)
        expanded = lax.dot_general(
            twice, both, (((0,), (0,)), ((), ())), preferred_element_type=f32
        )
        for h in range(2):
            at = (2 * j + h) * HALF
            near_part = jnp.transpose(total(slice(at, at + HALF)))
            panels = slice(h * HALF, (h + 1) * HALF)
            out[0, j, panels] = (near_part + expanded[panels]).astype(bf16)


def finish(core, keep, swapped, others, bases):
    return pl.pallas_call(
        finish_kernel,
        out_shape=jax.ShapeDtypeStruct((1, 3, CS, LOADS), bf16),
        in_specs=[pl.BlockSpec(memory_space=pltpu.SMEM)] + whole(6),
        out_specs=whole(1)[0],
        compiler_params=pltpu.CompilerParams(vmem_limit_bytes=VMEM_LIMIT),
        name="sum_and_expand",
    )(jnp.reshape(core, (1,)), keep, swapped, *others, bases)


def local(densities, positions, areas, bases, near_pairs, far_pairs, couplings):
    row = lax.axis_index("row")
    col = lax.axis_index("col")
    z, core = row >> 1, row & 1
    y, x = col >> 2, col & 3
    first_at = jnp.where(core == 0, x, y)
    second_at = jnp.where(core == 0, y, x)

    def unit_of(cluster):
        on_y, on_x = (cluster >> 2) & 3, cluster & 3
        first = (jnp.where(core == 0, on_x, on_y) - first_at) & 3
        second = (jnp.where(core == 0, on_y, on_x) - second_at) & 3
        put = lambda r: jnp.where(r == 0, 0, jnp.where(r == 1, 2, jnp.where(r == 2, 3, 1)))
        return put(second) * SIDE + put(first)

    def other_core(cluster):
        return ((cluster >> 4) + core) & 1

    def slot_of(cluster):
        return jnp.where(cluster >> 5 == z, unit_of(cluster) * 2 + other_core(cluster), -1)

    def target_of(cluster):
        step, other = ((cluster >> 5) - z) & 3, other_core(cluster)
        place = jnp.where(step == 0, AWAY + other, other * 3 + step - 1)
        return jnp.where((cluster & 15) == col, place, -1)

    bases = jnp.transpose(bases, (0, 2, 1, 3))
    positions = jnp.transpose(positions, (1, 0, 2))

    partner = swap_core(densities)
    own, moments, flip = moments_of(core, densities, bases)
    unit = make_unit(core, own, partner, moments)
    from_below = along_first(unit, 1)
    from_above = along_first(unit, -1)
    from_across = along_first(unit, 2)
    here = jnp.stack([z, core, y, x]).astype(jnp.int32)
    here, unit = lax.optimization_barrier((here, unit))
    spread, targets, couplings = make_points(here, positions, areas, couplings)
    (near_pairs, far_pairs, couplings, spread, targets, unit, from_below, from_above, from_across) = (
        lax.optimization_barrier(
            (near_pairs, far_pairs, couplings, spread, targets, unit)
            + (from_below, from_above, from_across)
        )
    )
    low = jnp.concatenate([unit, from_below], axis=0)
    high = jnp.concatenate([from_above, from_across], axis=0)
    low_below = along_second(low, 1)
    high_above = along_second(high, -1)

    heads, tails = near_pairs[:, 0], near_pairs[:, 1]
    mark = lambda index, size: index[None, :] == jnp.arange(size, dtype=jnp.int32)[:, None]
    to_targets = jnp.concatenate(
        [target_of(heads), jnp.where(heads != tails, target_of(tails), -1)]
    )
    from_slots = jnp.concatenate([slot_of(tails), slot_of(heads)])
    counts = lax.dot_general(
        mark(to_targets, 8).astype(bf16),
        mark(from_slots, 32).astype(bf16),
        (((1,), (1,)), ((), ())),
        preferred_element_type=f32,
    ).astype(jnp.int32)
    counts = counts * 4096 + jnp.arange(8, dtype=jnp.int32)[:, None] * 64 + jnp.arange(32, dtype=jnp.int32)

    far_heads, far_tails = far_pairs[:, 0], far_pairs[:, 1]

    def cell(target, source):
        ours = (target_of(target) >= 0) & (slot_of(source) >= 0) & (other_core(source) == 0)
        return jnp.where(ours, unit_of(source) * 8 + target_of(target), -1)

    back_cell = jnp.where(far_heads != far_tails, cell(far_tails, far_heads), -1)
    blocks = make_blocks(cell(far_heads, far_tails), back_cell, couplings, flip)
    blocks, low_later, high_later = lax.optimization_barrier((blocks, low, high))
    high_below = along_second(high_later, 1)
    low_above = along_second(low_later, -1)
    tables = (counts, targets, spread)

    carried = near("first", 0, (low, high), (), *tables, blocks)
    low_below, high_above, carried = lax.optimization_barrier((low_below, high_above, carried))
    low_across = along_second(low_below, 1)
    high_across = along_second(high_above, -1)
    beside = (low_below, high_below, low_above, high_above)
    carried = near("middle", 4, beside, carried, *tables, blocks)
    across = (low_across, high_across)
    send, far = near("send", 12, across, carried, *tables, blocks)
    swapped = swap_core(send)
    (keep,) = near("keep", 12, across, (carried[0], far), *tables, blocks)
    both = [(keep[k] + swapped[k].astype(f32)).astype(bf16) for k in range(3)]
    both, far = lax.optimization_barrier((both, far))
    others = [along_z(both[0], 1), along_z(both[2], 3)]
    others.append(along_z(both[1], 2))
    everything = (low, high) + beside + across
    own, pair = near("own", 0, everything, (far,), *tables, blocks)
    chips = [[2 * k, 2 * k + 1] for k in range(SIDE)]
    swapped = lax.all_to_all(pair, "row", 0, 0, axis_index_groups=chips, tiled=True)
    return finish(core, own, swapped, others, bases)


def solution(mesh):
    return jax.shard_map(
        local,
        mesh=mesh,
        in_specs=(
            P(("row", "col"), None, None, None),
            P(),
            P(),
            P(("row", "col"), None, None, None),
            P(),
            P(),
            P(),
        ),
        out_specs=P(("row", "col"), None, None, None),
        check_vma=False,
    )
```

```python
import functools

import jax
import jax.numpy as jnp
from jax import lax
from jax.experimental import pallas as pl
from jax.experimental.pallas import tpu as pltpu
from jax.sharding import PartitionSpec as P


CS = 256
LOADS = 128
RANK = 32
HALF = CS // 2
DENS = 3 * HALF
UNIT = 2 * DENS + RANK
FULL = 3 * CS + RANK
AXES = ("row", "col")
TARGETS = ((1, 0), (2, 0), (3, 0), (1, 1), (2, 1), (3, 1), (0, 0), (0, 1))
AWAY = 6
SPANS = {"first": (0, 8), "middle": (0, AWAY), "send": (3, AWAY), "keep": (0, 3), "own": (AWAY, 8)}
SIDE = 4

eps_square = 0.0004
lame_ratio = 1.8
kelvin_coef = 1.0 / (16.0 * 3.141592653589793 * 0.7)
VMEM_LIMIT = 16 * 1024 * 1024
bf16 = jnp.bfloat16
f32 = jnp.float32


def routes(move):
    pairs = []
    for z in range(SIDE):
        for core in range(2):
            for y in range(SIDE):
                for x in range(SIDE):
                    to_z, to_core, to_y, to_x = move(z, core, y, x)
                    source = (z * 2 + core) * 16 + y * SIDE + x
                    target = ((to_z % SIDE) * 2 + to_core) * 16 + (to_y % SIDE) * SIDE + to_x % SIDE
                    pairs.append((source, target))
    return pairs


def swap_core(value):
    return lax.ppermute(value, AXES, routes(lambda z, c, y, x: (z, 1 - c, y, x)))


def along_first(value, step):
    move = lambda z, c, y, x: (z, c, y, x + step) if c == 0 else (z, c, y + step, x)
    return lax.ppermute(value, AXES, routes(move))


def along_second(value, step):
    move = lambda z, c, y, x: (z, c, y + step, x) if c == 0 else (z, c, y, x + step)
    return lax.ppermute(value, AXES, routes(move))


def along_z(value, step):
    return lax.ppermute(value, AXES, routes(lambda z, c, y, x: (z + step, c, y, x)))


def whole(count):
    return [pl.BlockSpec(memory_space=pltpu.VMEM)] * count


def dot32(a, b):
    return jnp.dot(a, b, preferred_element_type=f32)


def iota(shape, dim):
    return lax.broadcasted_iota(jnp.int32, shape, dim)


def fetch(source, target, sem):
    copy = pltpu.make_async_copy(source, target, sem)
    copy.start()
    return copy


def moments_kernel(core_ref, dens_ref, bases_ref, own_ref, moments_ref, flip_ref, dens, bases, sems):
    copies = [fetch(dens_ref, dens, sems.at[0]), fetch(bases_ref, bases, sems.at[1])]
    width = RANK * RANK
    step = 128
    for at in range(0, width, step):
        source, target = iota((step, width), 0) + at, iota((step, width), 1)
        turned = ((target & (RANK - 1)) << 5) + (target >> 5)
        flip_ref[at : at + step] = jnp.where(source == turned, 1.0, 0.0).astype(bf16)
    half = pl.ds(pl.multiple_of(core_ref[0] * HALF, HALF), HALF)
    total = jnp.zeros((RANK, LOADS), f32)
    for copy in copies:
        copy.wait()
    for j in range(3):
        total += dot32(bases[0, j], dens[0, j])
        own_ref[j * HALF : (j + 1) * HALF] = jnp.transpose(dens[0, j, half, :])
    moments_ref[...] = total.astype(bf16)


def in_hbm(array):
    return pltpu.with_memory_space_constraint(array, pltpu.HBM)


def moments_of(core, densities, bases):
    width = RANK * RANK
    return pl.pallas_call(
        moments_kernel,
        out_shape=(
            jax.ShapeDtypeStruct((DENS, LOADS), bf16),
            jax.ShapeDtypeStruct((RANK, LOADS), bf16),
            jax.ShapeDtypeStruct((width, width), bf16),
        ),
        in_specs=[pl.BlockSpec(memory_space=pltpu.SMEM)] + [pl.BlockSpec(memory_space=pltpu.HBM)] * 2,
        out_specs=tuple(whole(3)),
        scratch_shapes=[
            pltpu.VMEM(densities.shape, bf16),
            pltpu.VMEM(bases.shape, bf16),
            pltpu.SemaphoreType.DMA((2,)),
        ],
        compiler_params=pltpu.CompilerParams(vmem_limit_bytes=VMEM_LIMIT),
        name="moments",
    )(jnp.reshape(core, (1,)), in_hbm(densities), in_hbm(bases))


def unit_kernel(core_ref, own_ref, partner_ref, moments_ref, unit_ref):
    half = pl.ds(pl.multiple_of(core_ref[0] * HALF, HALF), HALF)
    unit_ref[:DENS] = own_ref[...]
    for j in range(3):
        unit_ref[DENS + j * HALF : DENS + (j + 1) * HALF] = jnp.transpose(
            partner_ref[0, j, half, :]
        )
    unit_ref[2 * DENS :] = moments_ref[...]


def make_unit(core, own, partner, moments):
    return pl.pallas_call(
        unit_kernel,
        out_shape=jax.ShapeDtypeStruct((UNIT, LOADS), bf16),
        in_specs=[pl.BlockSpec(memory_space=pltpu.SMEM)] + whole(3),
        out_specs=whole(1)[0],
        compiler_params=pltpu.CompilerParams(vmem_limit_bytes=VMEM_LIMIT),
        name="unit",
    )(jnp.reshape(core, (1,)), own, partner, moments)


def points_kernel(
    here_ref, positions_ref, areas_ref, couplings_ref,
    spread_ref, targets_ref, held_couplings, columns, positions, areas, sems,
):
    first = [fetch(positions_ref, positions, sems.at[0]), fetch(areas_ref, areas, sems.at[1])]
    last = fetch(couplings_ref, held_couplings, sems.at[2])
    z, core, y, x = (here_ref[k] for k in range(4))
    half = lambda whole_row: jnp.where(core == 0, whole_row[:, :HALF], whole_row[:, HALF:])
    back = (0, 3, 1, 2)
    for copy in first:
        copy.wait()
    for t, (step, other) in enumerate(TARGETS):
        cluster = ((step + z) & 3) * 32 + ((other + core) & 1) * 16 + y * SIDE + x
        for i in range(3):
            targets_ref[t, i : i + 1, :] = positions[i, pl.ds(cluster, 1), :]
        targets_ref[t, 3:4, :] = areas[pl.ds(cluster, 1), :]
    for s in range(32):
        first, second = back[(s >> 1) & 3], back[s >> 3]
        on_x = (x + jnp.where(core == 0, first, second)) & 3
        on_y = (y + jnp.where(core == 0, second, first)) & 3
        cluster = z * 32 + ((s + core) & 1) * 16 + on_y * SIDE + on_x
        for i in range(3):
            columns[s, i : i + 1, :] = half(positions[i, pl.ds(cluster, 1), :])
        columns[s, 3:4, :] = half(areas[pl.ds(cluster, 1), :])
    for s in range(32):
        upright = jnp.transpose(columns[s])
        for i in range(4):
            spread_ref[s, i] = jnp.broadcast_to(upright[:, i : i + 1], (HALF, LOADS))
    last.wait()


def make_points(here, positions, areas, couplings):
    return pl.pallas_call(
        points_kernel,
        out_shape=(
            jax.ShapeDtypeStruct((32, 4, HALF, LOADS), f32),
            jax.ShapeDtypeStruct((8, 8, CS), f32),
            jax.ShapeDtypeStruct(couplings.shape, bf16),
        ),
        in_specs=[pl.BlockSpec(memory_space=pltpu.SMEM)] + [pl.BlockSpec(memory_space=pltpu.HBM)] * 3,
        out_specs=tuple(whole(3)),
        scratch_shapes=[
            pltpu.VMEM((32, 8, HALF), f32),
            pltpu.VMEM(positions.shape, f32),
            pltpu.VMEM(areas.shape, f32),
            pltpu.SemaphoreType.DMA((3,)),
        ],
        compiler_params=pltpu.CompilerParams(vmem_limit_bytes=VMEM_LIMIT),
        name="points",
    )(here, in_hbm(positions), in_hbm(areas), in_hbm(couplings))


def blocks_kernel(forward_ref, backward_ref, couplings_ref, flip_ref, blocks_ref):
    cells = 128
    far = couplings_ref.shape[0]

    def summed(cell_ref):
        marks = iota((cells, far), 0) == cell_ref[...]
        return dot32(jnp.where(marks, 1.0, 0.0).astype(bf16), couplings_ref[...])

    total = summed(forward_ref) + dot32(summed(backward_ref).astype(bf16), flip_ref[...])
    for u in range(16):
        unit = total[u * 8 : (u + 1) * 8]
        for g in range(0, 8, 2):
            two = [unit[:, k * 128 : (k + 1) * 128] for k in (g, g + 1)]
            lanes = slice(u * 128, (u + 1) * 128)
            blocks_ref[g * 8 : (g + 2) * 8, lanes] = jnp.concatenate(two, axis=0).astype(bf16)


def make_blocks(forward, backward, couplings, flip):
    return pl.pallas_call(
        blocks_kernel,
        out_shape=jax.ShapeDtypeStruct((64, 16 * 128), bf16),
        in_specs=whole(4),
        out_specs=whole(1)[0],
        compiler_params=pltpu.CompilerParams(vmem_limit_bytes=VMEM_LIMIT),
        name="coupling_blocks",
    )(forward[None, :], backward[None, :], couplings, flip)


def near_kernel(first_unit, buffers, part, counts, targets, spread, *refs):
    units = 2 * buffers
    slots = 2 * units
    held, refs = refs[:buffers], refs[buffers:]
    low, high = SPANS[part]
    sums_far = part in ("first", "middle", "send")
    if sums_far:
        blocks, refs = refs[0], refs[1:]
    if part in ("middle", "send"):
        carried, carried_far, refs = refs[0], refs[1], refs[2:]
    elif part == "keep":
        carried, far, refs = refs[0], refs[1], refs[2:]
    elif part == "own":
        carried, far, refs = refs[0], refs[1], refs[2:]
    if part == "send":
        send, far, acc, refs = refs[0], refs[1], refs[2], refs[3:]
    elif sums_far:
        acc, far, refs = refs[0], refs[1], refs[2:]
    elif part == "keep":
        acc, refs = refs[0], refs[1:]
    else:
        acc, pair, refs = refs[0], refs[1], refs[2:]
    flat, tile_a, tile_b, entry = refs[:4]

    for k in range(buffers):
        flat[k * 2 * UNIT : (k + 1) * 2 * UNIT] = held[k][...]

    def list_target(t, filled):
        for value in [counts[t, 2 * first_unit + s] for s in range(slots)]:
            entry[filled] = value
            filled = filled + jnp.where(value >= 4096, 1, 0)
        entry[filled] = t * 64 + 2 * first_unit
        return filled + (filled & 1)

    entries = lax.fori_loop(low, high, list_target, 0)
    for k in range(6):
        entry[entries + k] = low * 64 + 2 * first_unit
    near_rows = slice(0, 3 * CS)
    if part == "first":
        acc[:, near_rows] = jnp.zeros((high - low, 3 * CS, LOADS), f32)
    else:
        acc[:, near_rows] = carried[low:high]

    if sums_far:
        wide = refs[4]
        wide[...] = jnp.zeros(wide.shape, bf16)
        for u in range(units):
            moments = flat[u * UNIT + 2 * DENS : (u + 1) * UNIT, :]
            for k in range(4):
                at = u * 128 + k * RANK
                wide[at : at + RANK, k * LOADS : (k + 1) * LOADS] = moments
        coefficients = dot32(blocks[...], wide[...])
        for k in range(4):
            piece = coefficients[:, k * LOADS : (k + 1) * LOADS]
            far[k] = piece if part == "first" else carried_far[k] + piece

    def coefficients_of(t):
        return jnp.concatenate([far[k, pl.ds(t, 8, stride=8), :] for k in range(4)], axis=0)

    def decode(k):
        both = [entry[2 * k + h] for h in range(2)]
        return (both[0] >> 6) & 7, [v & 63 for v in both], [v >> 12 for v in both]

    def make_tile(k, tile):
        t, slot, pairs = decode(k)
        amount = [p.astype(f32) * kelvin_coef for p in pairs]
        point = targets[t]
        step = 16
        for at in range(0, CS, step):
            side = at // HALF
            rows = slice(at % HALF, at % HALF + step)
            here = [spread[slot[side], i, rows] for i in range(4)]
            for h in range(2):
                lanes = slice(h * HALF, (h + 1) * HALF)
                dx, dy, dz = (here[i] - point[i : i + 1, lanes] for i in range(3))
                inverse = lax.rsqrt(dx * dx + dy * dy + dz * dz + eps_square)
                scaled = (here[3] * (point[3:4, lanes] * amount[side])) * inverse
                cubed = scaled * (inverse * inverse)
                level = lame_ratio * scaled
                ex, ey, ez = dx * cubed, dy * cubed, dz * cubed
                values = (dx * ex + level, dy * ey + level, dz * ez + level, dx * ey, dx * ez, dy * ez)
                for b in range(6):
                    tile[b, at : at + step, lanes] = values[b].astype(bf16)

    def add_products(k, tile):
        t, slot, _ = decode(k)
        f = []
        for j in range(3):
            parts = []
            for h in range(2):
                base = ((slot[h] >> 1) - first_unit) * UNIT + (slot[h] & 1) * DENS + j * HALF
                parts.append(flat[pl.ds(pl.multiple_of(base, 16), HALF), :])
            f.append(jnp.concatenate(parts, axis=1))
        f = jnp.concatenate(f, axis=1)
        order = ((0, 3, 4), (3, 1, 5), (4, 5, 2))
        sums = [
            dot32(f, jnp.concatenate([tile[b] for b in order[i]], axis=0)) for i in range(3)
        ]
        for i in range(3):
            for h in range(2):
                at = (2 * i + h) * HALF
                acc[t - low, at : at + HALF] += sums[i][:, h * HALF : (h + 1) * HALF]

    tasks = entries >> 1

    @pl.when(tasks > 0)
    def _():
        make_tile(0, tile_a)

        def two_tasks(k, carry):
            make_tile(2 * k + 1, tile_b)
            add_products(2 * k, tile_a)

            @pl.when(2 * k + 1 < tasks)
            def _():
                make_tile(2 * k + 2, tile_a)
                add_products(2 * k + 1, tile_b)

            return carry

        lax.fori_loop(0, (tasks + 1) >> 1, two_tasks, 0)

    if part == "send":
        for t in range(low, high):
            send[t - low, : 3 * CS] = acc[t - low].astype(bf16)
            send[t - low, 3 * CS :] = coefficients_of(t).astype(bf16)
    elif not sums_far:
        for t in range(low, high):
            acc[t - low, 3 * CS :] = coefficients_of(t)
    if part == "own":
        for k in range(2):
            pair[k] = acc[1].astype(bf16)


def near(part, first_unit, buffers, carried, counts, targets, spread, blocks):
    count = len(buffers)
    slots = 4 * count
    sums = jax.ShapeDtypeStruct((SPANS[part][1], 3 * CS, LOADS), f32)
    far = jax.ShapeDtypeStruct((4, 64, LOADS), f32)
    scratch = [
        pltpu.VMEM((count * 2 * UNIT, LOADS), bf16),
        pltpu.VMEM((6, CS, CS), bf16),
        pltpu.VMEM((6, CS, CS), bf16),
        pltpu.SMEM((8 * slots + 16,), jnp.int32),
    ]
    operands = [counts, targets, spread, *buffers]
    low, high = SPANS[part]
    if part in ("keep", "own"):
        shapes = (jax.ShapeDtypeStruct((high - low, FULL, LOADS), f32),)
        if part == "own":
            shapes += (jax.ShapeDtypeStruct((2, FULL, LOADS), bf16),)
    else:
        operands.append(blocks[:, first_unit * 128 : (first_unit + 2 * count) * 128])
        scratch.append(pltpu.VMEM((2 * count * 128, 4 * LOADS), bf16))
        shapes = (sums, far)
        if part == "send":
            shapes = (jax.ShapeDtypeStruct((high - low, FULL, LOADS), bf16), far)
            scratch = [pltpu.VMEM((high - low, 3 * CS, LOADS), f32)] + scratch
    operands += carried
    return pl.pallas_call(
        functools.partial(near_kernel, first_unit, count, part),
        out_shape=shapes,
        in_specs=[pl.BlockSpec(memory_space=pltpu.SMEM)] + whole(len(operands) - 1),
        out_specs=tuple(whole(len(shapes))),
        scratch_shapes=scratch,
        compiler_params=pltpu.CompilerParams(vmem_limit_bytes=VMEM_LIMIT),
        cost_estimate=pl.CostEstimate(
            flops=count * 1_000_000_000, bytes_accessed=8_000_000, transcendentals=count * 500_000
        ),
        name=f"near_{part}",
    )(*operands)


def finish_kernel(core, keep, swapped, one, two, three, bases, out):
    def total(rows):
        return (
            keep[0, rows] + swapped[1 - core[0], rows].astype(f32) + one[rows].astype(f32)
            + two[rows].astype(f32) + three[rows].astype(f32)
        )

    coefficients = total(slice(3 * CS, FULL))
    high = coefficients.astype(bf16)
    low = (coefficients - high.astype(f32)).astype(bf16)
    both = jnp.concatenate([high, low], axis=0)
    row, held = iota((2 * RANK, 2 * RANK), 0), iota((2 * RANK, 2 * RANK), 1)
    from_row = (row & 32) + ((row & 3) << 3) + ((row & 31) >> 2)
    order = jnp.where(held == from_row, 1.0, 0.0).astype(bf16)
    both = dot32(order, both).astype(bf16)
    for j in range(3):
        basis = bases[0, j]
        twice = jnp.concatenate([basis, basis], axis=0)
        expanded = lax.dot_general(
            twice, both, (((0,), (0,)), ((), ())), preferred_element_type=f32
        )
        for h in range(2):
            at = (2 * j + h) * HALF
            near_part = jnp.transpose(total(slice(at, at + HALF)))
            panels = slice(h * HALF, (h + 1) * HALF)
            out[0, j, panels] = (near_part + expanded[panels]).astype(bf16)


def finish(core, keep, swapped, others, bases):
    return pl.pallas_call(
        finish_kernel,
        out_shape=jax.ShapeDtypeStruct((1, 3, CS, LOADS), bf16),
        in_specs=[pl.BlockSpec(memory_space=pltpu.SMEM)] + whole(6),
        out_specs=whole(1)[0],
        compiler_params=pltpu.CompilerParams(vmem_limit_bytes=VMEM_LIMIT),
        name="sum_and_expand",
    )(jnp.reshape(core, (1,)), keep, swapped, *others, bases)


def local(densities, positions, areas, bases, near_pairs, far_pairs, couplings):
    row = lax.axis_index("row")
    col = lax.axis_index("col")
    z, core = row >> 1, row & 1
    y, x = col >> 2, col & 3
    first_at = jnp.where(core == 0, x, y)
    second_at = jnp.where(core == 0, y, x)

    def unit_of(cluster):
        on_y, on_x = (cluster >> 2) & 3, cluster & 3
        first = (jnp.where(core == 0, on_x, on_y) - first_at) & 3
        second = (jnp.where(core == 0, on_y, on_x) - second_at) & 3
        put = lambda r: jnp.where(r == 0, 0, jnp.where(r == 1, 2, jnp.where(r == 2, 3, 1)))
        return put(second) * SIDE + put(first)

    def other_core(cluster):
        return ((cluster >> 4) + core) & 1

    def slot_of(cluster):
        return jnp.where(cluster >> 5 == z, unit_of(cluster) * 2 + other_core(cluster), -1)

    def target_of(cluster):
        step, other = ((cluster >> 5) - z) & 3, other_core(cluster)
        place = jnp.where(step == 0, AWAY + other, other * 3 + step - 1)
        return jnp.where((cluster & 15) == col, place, -1)

    bases = jnp.transpose(bases, (0, 2, 1, 3))
    positions = jnp.transpose(positions, (1, 0, 2))

    partner = swap_core(densities)
    own, moments, flip = moments_of(core, densities, bases)
    unit = make_unit(core, own, partner, moments)
    from_below = along_first(unit, 1)
    from_above = along_first(unit, -1)
    from_across = along_first(unit, 2)
    here = jnp.stack([z, core, y, x]).astype(jnp.int32)
    here, unit = lax.optimization_barrier((here, unit))
    spread, targets, couplings = make_points(here, positions, areas, couplings)
    (near_pairs, far_pairs, couplings, spread, targets, unit, from_below, from_above, from_across) = (
        lax.optimization_barrier(
            (near_pairs, far_pairs, couplings, spread, targets, unit)
            + (from_below, from_above, from_across)
        )
    )
    low = jnp.concatenate([unit, from_below], axis=0)
    high = jnp.concatenate([from_above, from_across], axis=0)
    low_below = along_second(low, 1)
    high_above = along_second(high, -1)

    heads, tails = near_pairs[:, 0], near_pairs[:, 1]
    mark = lambda index, size: index[None, :] == jnp.arange(size, dtype=jnp.int32)[:, None]
    to_targets = jnp.concatenate(
        [target_of(heads), jnp.where(heads != tails, target_of(tails), -1)]
    )
    from_slots = jnp.concatenate([slot_of(tails), slot_of(heads)])
    counts = lax.dot_general(
        mark(to_targets, 8).astype(bf16),
        mark(from_slots, 32).astype(bf16),
        (((1,), (1,)), ((), ())),
        preferred_element_type=f32,
    ).astype(jnp.int32)
    counts = counts * 4096 + jnp.arange(8, dtype=jnp.int32)[:, None] * 64 + jnp.arange(32, dtype=jnp.int32)

    far_heads, far_tails = far_pairs[:, 0], far_pairs[:, 1]

    def cell(target, source):
        ours = (target_of(target) >= 0) & (slot_of(source) >= 0) & (other_core(source) == 0)
        return jnp.where(ours, unit_of(source) * 8 + target_of(target), -1)

    back_cell = jnp.where(far_heads != far_tails, cell(far_tails, far_heads), -1)
    blocks = make_blocks(cell(far_heads, far_tails), back_cell, couplings, flip)
    blocks, low_later, high_later = lax.optimization_barrier((blocks, low, high))
    high_below = along_second(high_later, 1)
    low_above = along_second(low_later, -1)
    tables = (counts, targets, spread)

    carried = near("first", 0, (low, high), (), *tables, blocks)
    started = carried[0]
    low_below, high_above, carried = lax.optimization_barrier((low_below, high_above, carried))
    low_across = along_second(low_below, 1)
    high_across = along_second(high_above, -1)
    beside = (low_below, high_below, low_above, high_above)
    carried = near("middle", 4, beside, carried, *tables, blocks)
    across = (low_across, high_across)
    send, far = near("send", 12, across, carried, *tables, blocks)
    swapped = swap_core(send)
    (keep,) = near("keep", 12, across, (carried[0], far), *tables, blocks)
    both = [(keep[k] + swapped[k].astype(f32)).astype(bf16) for k in range(3)]
    both, far = lax.optimization_barrier((both, far))
    others = [along_z(both[0], 1), along_z(both[2], 3)]
    others.append(along_z(both[1], 2))
    own, pair = near("own", 4, beside + across, (started, far), *tables, blocks)
    chips = [[2 * k, 2 * k + 1] for k in range(SIDE)]
    swapped = lax.all_to_all(pair, "row", 0, 0, axis_index_groups=chips, tiled=True)
    return finish(core, own, swapped, others, bases)


def solution(mesh):
    return jax.shard_map(
        local,
        mesh=mesh,
        in_specs=(
            P(("row", "col"), None, None, None),
            P(),
            P(),
            P(("row", "col"), None, None, None),
            P(),
            P(),
            P(),
        ),
        out_specs=P(("row", "col"), None, None, None),
        check_vma=False,
    )
```
